32 devices in a mesh: dp: 8 (over y, x, core), mp: 4 (over z).
Axes of the slice: x: 2, y: 2, z: 4, core: 2. Of those that a mesh axis runs over, the one named last changes fastest.
Arguments:
- tokens: bfloat16 [3072, 2048], P(('dp', 'mp')), may hold values from -8 to 8
- teacher: bfloat16 [3072, 2048], P(('dp', 'mp')), may hold values from -6 to 6
- segments: int32 [8, 384], P('dp'), may hold values from 0 to 3, never falling along the last dimension, each value on 1 to 192 neighbouring positions
- block_counts: int32 [8], replicated, may hold values from 1 to 12, as said below
- loss_mask: int32 [3072], replicated, may hold values from 0 to 1, as said below
- mixer_in: float32 [4, 2048, 2048], P(None, 'dp', 'mp'), may hold values from -0.397747564 to 0.397747564
- mixer_in_moment: float32 [4, 2048, 2048], P(None, 'dp', 'mp'), may hold values from -1200 to 1200
- mixer_in_average: float32 [4, 2048, 2048], P(None, 'dp', 'mp'), may hold values from -0.125 to 0.125
- mixer_out: float32 [2048, 2048], P('mp', 'dp'), may hold values from -0.0625 to 0.0625
- mixer_out_moment: float32 [2048, 2048], P('mp', 'dp'), may hold values from -3600 to 3600
- mixer_out_average: float32 [2048, 2048], P('mp', 'dp'), may hold values from -0.0625 to 0.0625
- feed_in: float32 [2, 2048, 5632], P(None, 'dp', 'mp'), may hold values from -0.125 to 0.125
- feed_in_moment: float32 [2, 2048, 5632], P(None, 'dp', 'mp'), may hold values from -1800 to 1800
- feed_in_average: float32 [2, 2048, 5632], P(None, 'dp', 'mp'), may hold values from -0.125 to 0.125
- feed_out: float32 [5632, 2048], P('mp', 'dp'), may hold values from -0.109375 to 0.109375
- feed_out_moment: float32 [5632, 2048], P('mp', 'dp'), may hold values from -2400 to 2400
- feed_out_average: float32 [5632, 2048], P('mp', 'dp'), may hold values from -0.109375 to 0.109375
- norm_gains: float32 [3, 2048], P(None, 'dp'), may hold values from 0.5 to 1.5
- norm_gains_moment: float32 [3, 2048], P(None, 'dp'), may hold values from -1800 to 1800
- norm_gains_average: float32 [3, 2048], P(None, 'dp'), may hold values from 0.5 to 1.5
Outputs:
- output: bfloat16 [3072, 2048], P(('dp', 'mp'))
- tokens_grad: bfloat16 [3072, 2048], P(('dp', 'mp'))
- loss_value: float32 [], replicated
- mixer_in_grad: float32 [4, 2048, 2048], P(None, 'dp', 'mp')
- mixer_in_new: float32 [4, 2048, 2048], P(None, 'dp', 'mp')
- mixer_in_moment_new: float32 [4, 2048, 2048], P(None, 'dp', 'mp')
- mixer_in_average_new: float32 [4, 2048, 2048], P(None, 'dp', 'mp')
- mixer_out_grad: float32 [2048, 2048], P('mp', 'dp')
- mixer_out_new: float32 [2048, 2048], P('mp', 'dp')
- mixer_out_moment_new: float32 [2048, 2048], P('mp', 'dp')
- mixer_out_average_new: float32 [2048, 2048], P('mp', 'dp')
- feed_in_grad: float32 [2, 2048, 5632], P(None, 'dp', 'mp')
- feed_in_new: float32 [2, 2048, 5632], P(None, 'dp', 'mp')
- feed_in_moment_new: float32 [2, 2048, 5632], P(None, 'dp', 'mp')
- feed_in_average_new: float32 [2, 2048, 5632], P(None, 'dp', 'mp')
- feed_out_grad: float32 [5632, 2048], P('mp', 'dp')
- feed_out_new: float32 [5632, 2048], P('mp', 'dp')
- feed_out_moment_new: float32 [5632, 2048], P('mp', 'dp')
- feed_out_average_new: float32 [5632, 2048], P('mp', 'dp')
- norm_gains_grad: float32 [3, 2048], P(None, 'dp')
- norm_gains_new: float32 [3, 2048], P(None, 'dp')
- norm_gains_moment_new: float32 [3, 2048], P(None, 'dp')
- norm_gains_average_new: float32 [3, 2048], P(None, 'dp')
The draws below stay inside these ranges and needn't reach their ends.
Inputs may be any that keep to these rules, and one draw needn't show every extreme that they name: `segments`: never falling along a sequence. The first 32 * block_counts positions of a sequence are live; some sequence has all 12 blocks live. `loss_mask`: 1 at the first position of every sequence.
All inputs are finite; a program needn't handle non-finite values.
Results may differ from the reference program's by a relative error of at most 0.019.
Values may be sent and summed in bfloat16 or wider, within the bound.
No kernel may reach another device: no remote copies, remote signals or barrier semaphores. Data moves between devices by JAX's collectives and lax.ppermute only.
A program may use at most 256 MiB of HBM per device.

```python
import math
import jax
import jax.numpy as jnp
import numpy as np
from jax import lax

D = 2048
HEADS = 16
FF = 5632
SEQ_LEN = 384
BLOCK = 32
NBLK = 12
TOK_DEV = 384
SEQS = 8
TOKENS = 3072
N_DP = 8


def shared_pattern(key):
    sign_key, width_key, first_key, second_key = jax.random.split(jax.random.fold_in(key, 5), 4)
    signs = (2 * jax.random.randint(sign_key, (D,), 0, 2) - 1).astype(jnp.float32)
    widths = jax.random.uniform(width_key, (D,), jnp.float32, 0.5, 1.5)
    first = jnp.clip(jax.random.normal(first_key, (D,), jnp.float32), -3.0, 3.0)
    second = jnp.clip(jax.random.normal(second_key, (D,), jnp.float32), -3.0, 3.0)
    return (signs, widths, first, second)


def draw_tokens(key, part):
    signs, widths, first, second = shared_pattern(key)
    key = jax.random.fold_in(key, 41)
    position = (jnp.arange(TOKENS, dtype=jnp.int32) % SEQ_LEN).astype(jnp.float32)
    phase = 6.283185307179586 * 3.0 / SEQ_LEN * position
    noise = jnp.clip(jax.random.normal(key, (TOKENS, D), jnp.float32), -5.0, 5.0)
    common = signs * widths + jnp.cos(phase)[:, None] * first[None, :] + jnp.sin(phase)[:, None] * second[None, :]
    return (0.7 * noise + 0.5 * common).astype(jnp.bfloat16)


def draw_block_counts(key, part):
    first_key, second_key = jax.random.split(jax.random.fold_in(key, 11))
    level = jax.random.randint(first_key, (SEQS,), 0, 4)
    base = NBLK // jnp.power(2, level)
    jitter = jax.random.randint(second_key, (SEQS,), -1, 2)
    counts = jnp.clip(base + jitter, 1, NBLK)
    counts = counts.at[0].set(NBLK)
    return counts.astype(jnp.int32)


def draw_loss_mask(key, part):
    row = jnp.arange(TOKENS, dtype=jnp.int32)
    groups = TOKENS // TOK_DEV
    device = row // TOK_DEV
    limit = 100 + 800 * device // max(groups - 1, 1)
    picked = jax.random.randint(jax.random.fold_in(key, 23), (TOKENS,), 0, 1000)
    mask = (picked < limit) | (row % SEQ_LEN == 0)
    return mask.astype(jnp.int32)


def draw_mixer_in(key, part):
    signs, widths, first, second = shared_pattern(key)
    key = jax.random.fold_in(key, 37)
    base_key, rate_key = jax.random.split(key)
    base = jnp.clip(jax.random.normal(base_key, (4, D, D), jnp.float32), -6.0, 6.0)
    rough, lower_end, upper_end = (1.5, -1.0, 8.0)
    targets = jax.random.uniform(rate_key, (D,), jnp.float32, lower_end, upper_end)
    scales = jnp.array([1.0, rough, 1.0, 1.0], jnp.float32)[:, None, None] * D ** (-0.5)
    shift = signs[:, None] * targets[None, :] / (0.5 * D)
    weights = base * scales
    return weights.at[1].add(shift)


def level_of(key, extent, cuts, low, high):
    loudness, own = 1.0, jax.random.fold_in(key, 6)
    for axis_at, blocks in cuts:
        draws = jnp.exp(jax.random.uniform(jax.random.fold_in(own, axis_at), (blocks,), jnp.float32, low / len(cuts), high / len(cuts)))
        loudness = loudness * jnp.repeat(draws, extent[axis_at] // blocks).reshape([-1 if axis == axis_at else 1 for axis in range(len(extent))])
    return loudness


def split_up(number_of, total, most, skew):
    loads = [(1 << 20) // math.isqrt(standing ** skew) + 1 for standing in range(2, number_of + 1)]
    rest, holding = total - most - (number_of - 1), [1] * (number_of - 1)
    while rest > 0:
        candidates = [i for i in range(number_of - 1) if holding[i] < most]
        whole, budget = sum([loads[i] for i in candidates]), rest
        for i in candidates:
            extra = min(most - holding[i], max(1, budget * loads[i] // whole), rest)
            holding[i] = holding[i] + extra
            rest = rest - extra
    return np.array([most] + holding)


def ragged_sizes(rng, number_of, total, most, slope):
    if number_of == 2:
        one = jax.random.randint(rng, (), max(1, total - most), min(most, total - 1) + 1)
        return jnp.stack([one, total - one])
    sizes = jnp.asarray(split_up(number_of, total, most, slope), jnp.int32)
    twos = (number_of - 1) // 2
    source_of, receiver = sizes[1:1 + 2 * twos:2], sizes[2:2 + 2 * twos:2]
    room = jnp.minimum(source_of - 1, most - receiver)
    moved = jax.random.randint(jax.random.fold_in(rng, 1), (twos,), 0, 1 << 20) % (room + 1)
    sizes = sizes.at[1:1 + 2 * twos:2].set(source_of - moved).at[2:2 + 2 * twos:2].set(receiver + moved)
    return sizes[jax.random.permutation(jax.random.fold_in(rng, 2), number_of)]


def gaussian(rng, dims, scale, most, pieces=(), kind=jnp.bfloat16):
    values = scale * jax.random.normal(rng, dims, jnp.float32)
    if pieces:
        values = values * level_of(rng, dims, pieces, -0.22, 0.18)
    return jnp.clip(values, -most, most).astype(kind)


def setup_inputs(seed: int = 0) -> dict:
    key_list = jax.random.split(jax.random.key(seed), 21)
    return {
        "tokens": draw_tokens(jax.random.fold_in(key_list[20], 71), 0),
        "teacher": gaussian(key_list[1], (TOKENS, D), 1.0, 6.0, ((0, 32),)),
        "segments": jax.vmap(lambda own: jnp.searchsorted(jnp.cumsum(ragged_sizes(own, 4, SEQ_LEN, SEQ_LEN // 2, 2)), jnp.arange(SEQ_LEN), side="right"))(jax.random.split(key_list[2], SEQS)).reshape((SEQS, SEQ_LEN)).astype(jnp.int32),
        "block_counts": draw_block_counts(jax.random.fold_in(key_list[20], 71), 0),
        "loss_mask": draw_loss_mask(jax.random.fold_in(key_list[20], 71), 0),
        "mixer_in": draw_mixer_in(jax.random.fold_in(key_list[20], 71), 0),
        "mixer_in_moment": gaussian(key_list[6], (4, D, D), 200.0, 1200.0, ((1, 8), (2, 4)), jnp.float32),
        "mixer_in_average": gaussian(key_list[7], (4, D, D), D ** -0.5, 0.125, ((1, 8), (2, 4)), jnp.float32),
        "mixer_out": gaussian(key_list[8], (D, D), (4 * D) ** -0.5, 0.0625, ((0, 4), (1, 8)), jnp.float32),
        "mixer_out_moment": gaussian(key_list[9], (D, D), 600.0, 3600.0, ((0, 4), (1, 8)), jnp.float32),
        "mixer_out_average": gaussian(key_list[10], (D, D), (4 * D) ** -0.5, 0.0625, ((0, 4), (1, 8)), jnp.float32),
        "feed_in": gaussian(key_list[11], (2, D, FF), D ** -0.5, 0.125, ((1, 8), (2, 4)), jnp.float32),
        "feed_in_moment": gaussian(key_list[12], (2, D, FF), 300.0, 1800.0, ((1, 8), (2, 4)), jnp.float32),
        "feed_in_average": gaussian(key_list[13], (2, D, FF), D ** -0.5, 0.125, ((1, 8), (2, 4)), jnp.float32),
        "feed_out": gaussian(key_list[14], (FF, D), (FF // 2) ** -0.5, 0.109375, ((0, 4), (1, 8)), jnp.float32),
        "feed_out_moment": gaussian(key_list[15], (FF, D), 400.0, 2400.0, ((0, 4), (1, 8)), jnp.float32),
        "feed_out_average": gaussian(key_list[16], (FF, D), (FF // 2) ** -0.5, 0.109375, ((0, 4), (1, 8)), jnp.float32),
        "norm_gains": jnp.clip(1.0 + 0.1 * jax.random.normal(key_list[17], (3, D), jnp.float32), 0.5, 1.5),
        "norm_gains_moment": gaussian(key_list[18], (3, D), 300.0, 1800.0, ((1, 8),), jnp.float32),
        "norm_gains_average": jnp.clip(1.0 + 0.1 * jax.random.normal(key_list[19], (3, D), jnp.float32), 0.5, 1.5),
    }


EPS = 1e-06
MOMENT_RATE = 0.5
AVERAGE_RATE = 0.5
LEARN_RATE = 4e-05
HIGH_PRECISION = lax.Precision.HIGHEST

@jax.custom_vjp
def low(v):
    return lax.optimization_barrier(v.astype(jnp.bfloat16)).astype(jnp.float32)

@jax.custom_vjp
def low_back(v):
    return v

def low_keep(v):
    return (low(v), None)

def low_pass(kept, grad):
    return (grad,)

def back_keep(v):
    return (v, None)

def back_low(kept, grad):
    return (low(grad),)
low.defvjp(low_keep, low_pass)
low_back.defvjp(back_keep, back_low)

def rms_scale(value_rows, gain):
    return value_rows * lax.rsqrt(lax.optimization_barrier(jnp.mean(value_rows * value_rows, axis=-1, keepdims=True)) + EPS) * gain

def block_update(state_matrix, seg_prev, query_rows, logf, key_rows, value_rows, segs, live):
    width = segs.shape[0]
    cumulative_decay = jnp.cumsum(logf, axis=0)
    causal = jnp.arange(width)[:, None] >= jnp.arange(width)[None, :]
    keep = jnp.where(causal & (segs[:, None] == segs[None, :]), 1.0, 0.0).astype(jnp.float32)
    spread = jnp.where(causal[:, :, None, None], cumulative_decay[:, None] - cumulative_decay[None, :], 0.0)
    decay = jnp.exp(spread) * keep[:, :, None, None]
    scores = jnp.einsum('thk,tshk,shk->hts', query_rows, decay, key_rows, precision=HIGH_PRECISION)
    inner = jnp.einsum('hts,shv->thv', scores, value_rows, precision=HIGH_PRECISION)
    carried_state = jnp.where(segs == seg_prev, 1.0, 0.0).astype(jnp.float32)
    outer_product = jnp.einsum('qoi,oin->qon', query_rows * jnp.exp(cumulative_decay), state_matrix, precision=HIGH_PRECISION) * carried_state[:, None, None]
    last_decay = cumulative_decay[-1]
    tail_keep = jnp.where(segs == segs[-1], 1.0, 0.0).astype(jnp.float32)
    tail_decay = jnp.exp(last_decay[None] - cumulative_decay) * tail_keep[:, None, None]
    kept_rows = jnp.where(segs[-1] == seg_prev, 1.0, 0.0).astype(jnp.float32)
    next_state = jnp.exp(last_decay)[:, :, None] * state_matrix * kept_rows + jnp.einsum('ifm,ifg->fmg', key_rows * tail_decay, value_rows, precision=HIGH_PRECISION)
    return (next_state, (inner + outer_product) * live)

def sequence_mix(query_rows, logf, key_rows, value_rows, segs, count_here):
    blocks = segs.shape[0]
    seg_prev = jnp.concatenate([jnp.full((1,), -1, jnp.int32), segs[:-1, -1].astype(jnp.int32)])
    index = jnp.arange(blocks, dtype=jnp.int32)

    def step(state_matrix, items):
        q_block, f_block, k_block, v_block, s_block, p_block, idx = items
        live = jnp.where(idx < count_here, 1.0, 0.0).astype(jnp.float32)
        return block_update(state_matrix, p_block, q_block, f_block, k_block, v_block, s_block, live)
    start = jnp.zeros((query_rows.shape[2], query_rows.shape[3], value_rows.shape[3]), jnp.float32)
    _, outs = lax.scan(jax.checkpoint(step), start, (query_rows, logf, key_rows, value_rows, segs, seg_prev, index))
    return outs

def layer_forward(params, inputs, teacher, segs, counts, valid, scale):
    mixer_in, mixer_out, feed_in, feed_out, norm_gains = params
    mixer_in_w = low(mixer_in)
    mixer_out_w = low(mixer_out)
    feed_in_w = low(feed_in)
    feed_out_w = low(feed_out)
    gains_w = low(norm_gains)
    total_rows = inputs.shape[0]
    seq_total, seq_len = segs.shape
    blocks = seq_len // BLOCK
    norm_one = low(rms_scale(inputs, gains_w[0]))
    projected = low_back(jnp.einsum('td,jde->jte', norm_one, mixer_in_w, precision=HIGH_PRECISION))

    def split(v):
        return v.reshape(seq_total, blocks, BLOCK, HEADS, D // HEADS)
    query_rows = jax.nn.silu(projected[0])
    logf = jax.nn.log_sigmoid(projected[1])
    key_rows = jax.nn.sigmoid(-projected[1])
    value_rows = projected[2]
    mixed_heads = jax.vmap(sequence_mix)(split(query_rows), split(logf), split(key_rows), split(value_rows), segs.reshape(seq_total, blocks, BLOCK), counts)
    mixed_heads = mixed_heads.reshape(total_rows, D)
    out_normed = rms_scale(mixed_heads, gains_w[2])
    act = low(out_normed * jax.nn.silu(projected[3]))
    mixed = low_back(jnp.dot(act, mixer_out_w, precision=HIGH_PRECISION, preferred_element_type=jnp.float32))
    resid = inputs + mixed
    norm_two = low(rms_scale(resid, gains_w[1]))
    gate_up = low_back(jnp.einsum('td,jdf->jtf', norm_two, feed_in_w, precision=HIGH_PRECISION))
    hidden = low(jax.nn.silu(gate_up[0]) * gate_up[1])
    feed = low_back(jnp.dot(hidden, feed_out_w, precision=HIGH_PRECISION, preferred_element_type=jnp.float32))
    final = resid + feed
    error = (final - teacher) * valid[:, None]
    square = jnp.sum(error * error)
    return (scale * 0.5 * square, (final, square))

def apply_update(master, moment, average, gradient):
    moment_new = MOMENT_RATE * moment + gradient
    master_new = master - LEARN_RATE * (gradient + MOMENT_RATE * moment_new)
    average_new = AVERAGE_RATE * average + (1.0 - AVERAGE_RATE) * master_new
    return (gradient, master_new, moment_new, average_new)

def reference(tokens, teacher, segments, block_counts, loss_mask, mixer_in, mixer_in_moment, mixer_in_average, mixer_out, mixer_out_moment, mixer_out_average, feed_in, feed_in_moment, feed_in_average, feed_out, feed_out_moment, feed_out_average, norm_gains, norm_gains_moment, norm_gains_average):
    seq_total, seq_len = segments.shape
    position = jnp.arange(seq_len, dtype=jnp.int32)
    live = jnp.where(position[None, :] < BLOCK * block_counts[:, None], 1.0, 0.0).astype(jnp.float32)
    valid = loss_mask.reshape(seq_total, seq_len).astype(jnp.float32) * live
    total_count = jnp.sum(valid)
    scale = TOKENS / total_count
    params = (mixer_in, mixer_out, feed_in, feed_out, norm_gains)
    groups = N_DP
    per_group = seq_total // groups
    group_rows = per_group * seq_len
    items = (tokens.reshape(groups, group_rows, D), teacher.reshape(groups, group_rows, D), segments.reshape(groups, per_group, seq_len), block_counts.reshape(groups, per_group), valid.reshape(groups, group_rows))

    def group_step(total, group_items):
        inputs, target, seg_group, count_group, valid_group = group_items

        def objective(weights, value_rows):
            return layer_forward(weights, value_rows, target.astype(jnp.float32), seg_group, count_group, valid_group, scale)
        value, backward, aux = jax.vjp(objective, params, inputs.astype(jnp.float32), has_aux=True)
        grads, input_grad = backward(jnp.ones_like(value))
        final, square = aux
        total = jax.tree.map(lambda left, right: left + right, total, (grads, square))
        return (total, (final.astype(jnp.bfloat16), input_grad.astype(jnp.bfloat16)))
    start = (jax.tree.map(jnp.zeros_like, params), jnp.zeros((), jnp.float32))
    (grads, square_total), (finals, input_grads) = lax.scan(group_step, start, items)
    output = finals.reshape(TOKENS, D)
    tokens_grad = input_grads.reshape(TOKENS, D)
    loss_value = square_total / (total_count * D)
    first = apply_update(mixer_in, mixer_in_moment, mixer_in_average, grads[0])
    second = apply_update(mixer_out, mixer_out_moment, mixer_out_average, grads[1])
    third = apply_update(feed_in, feed_in_moment, feed_in_average, grads[2])
    fourth = apply_update(feed_out, feed_out_moment, feed_out_average, grads[3])
    fifth = apply_update(norm_gains, norm_gains_moment, norm_gains_average, grads[4])
    return (output, tokens_grad, loss_value, first[0], first[1], first[2], first[3], second[0], second[1], second[2], second[3], third[0], third[1], third[2], third[3], fourth[0], fourth[1], fourth[2], fourth[3], fifth[0], fifth[1], fifth[2], fifth[3])
```

```python
import functools

import jax
import jax.numpy as jnp
import numpy as np
from jax import lax
from jax.experimental import pallas as pl
from jax.experimental.pallas import tpu as pltpu
from jax.sharding import PartitionSpec as P

D = 2048
HEAD_DIM = 128
BLOCK = 32
CHUNK = 128
LEVELS = 7

EPS = 1e-06
MOMENT_RATE = 0.5
AVERAGE_RATE = 0.5
LEARN_RATE = 4e-05

BF = jnp.bfloat16
F32 = jnp.float32


def decay_sums():
    t = np.arange(CHUNK)[:, None]
    r = np.arange(CHUNK)[None, :]
    mats = []
    for level in range(LEVELS):
        half = 1 << level
        mid = (t // (2 * half)) * (2 * half) + half
        right = t >= mid
        mats.append(np.where(right, (r >= mid) & (r <= t), (r > t) & (r < mid)))
    mats.append(r <= t)
    mats.append(r > t)
    return np.stack(mats).astype(np.float32)


def dot(a, b):
    return lax.dot_general(a, b, (((1,), (0,)), ((), ())), preferred_element_type=F32)


def dot_nt(a, b):
    return lax.dot_general(a, b, (((1,), (1,)), ((), ())), preferred_element_type=F32)


def dot_tn(a, b):
    return lax.dot_general(a, b, (((0,), (0,)), ((), ())), preferred_element_type=F32)


def sigmoid(v):
    return 1.0 / (1.0 + jnp.exp(-v))


def forget_parts(z):
    small = jnp.exp(-jnp.abs(z))
    logf = jnp.minimum(z, 0.0) - jnp.log1p(small)
    key = jnp.where(z >= 0.0, small, 1.0) / (1.0 + small)
    return logf, key


def split_sum(mat, logf_pair):
    both = dot(mat, logf_pair)
    return both[:, :HEAD_DIM] + both[:, HEAD_DIM:]


def chunk_masks():
    row = lax.broadcasted_iota(jnp.int32, (CHUNK, CHUNK), 0)
    col = lax.broadcasted_iota(jnp.int32, (CHUNK, CHUNK), 1)
    return row, col, row ^ col


def mixer_forward_kernel(
    count_ref, z_ref, gain_ref, seg_row_ref, seg_col_ref, sums_ref, o_ref, act_ref, square_ref, state_ref, pair_ref
):
    head = pl.program_id(1)
    seq = pl.program_id(0)
    chunks = z_ref.shape[1] // CHUNK
    row, col, differ = chunk_masks()
    live_end = count_ref[seq] * BLOCK
    state = jnp.zeros((HEAD_DIM, HEAD_DIM), F32)
    gain = gain_ref[...]
    for c in range(chunks):
        rows = pl.ds(c * CHUNK, CHUNK)
        z0, z1, value, z3 = (z_ref[j, rows, :] for j in range(4))
        query = z0 * sigmoid(z0)
        logf, key = forget_parts(z1)
        high = logf.astype(BF)
        pair = jnp.concatenate([high, (logf - high.astype(F32)).astype(BF)], axis=1)
        seg_col = seg_col_ref[0, rows, :]
        seg_row = seg_row_ref[0, :, c * CHUNK : (c + 1) * CHUNK]
        seg_last = seg_row[:, CHUNK - 1 :]
        value_low = value.astype(BF)
        scores = None
        for level in reversed(range(LEVELS)):
            decay = jnp.exp(split_sum(sums_ref[level], pair))
            right = ((row >> level) & 1) == 1
            mixed = (decay * jnp.where(right, query, key)).astype(BF)
            product = dot_nt(mixed, mixed)
            scores = product if scores is None else jnp.where(differ < (2 << level), product, scores)
        diagonal = jnp.sum(query * key, axis=1, keepdims=True)
        scores = jnp.where(differ == 0, diagonal, scores)
        scores = jnp.where(seg_col == seg_row, scores, 0.0).astype(BF)
        pair_ref[0, 0, c] = scores
        out = dot(jnp.where(row >= col, scores, jnp.zeros_like(scores)), value_low)
        from_start = jnp.exp(split_sum(sums_ref[LEVELS], pair))
        if c > 0:
            carried = seg_col == seg_before
            reach = jnp.where(carried, query * from_start, 0.0).astype(BF)
            out = out + dot_nt(reach, state.astype(BF))
        state_ref[0, 0, c] = state
        position = c * CHUNK + lax.broadcasted_iota(jnp.int32, (CHUNK, 1), 0)
        out = jnp.where(position < live_end, out, 0.0)
        o_ref[rows, :] = out
        act_ref[rows, :] = (out * gain * (z3 * sigmoid(z3))).astype(BF)
        square = jnp.sum(out * out, axis=1, keepdims=True)
        square_ref[rows, :] = jnp.where(head == 0, square, square_ref[rows, :] + square)
        if c < chunks - 1:
            to_end = jnp.exp(split_sum(sums_ref[LEVELS + 1], pair))
            tail = jnp.where(seg_col == seg_last, key * to_end, 0.0).astype(BF)
            fresh = dot_tn(value_low, tail)
            if c > 0:
                kept = jnp.where(seg_last == seg_before, from_start[CHUNK - 1 :], 0.0)
                fresh = fresh + state * kept
            state = fresh
            seg_before = seg_last


def mixer_backward_kernel(
    count_ref, z_ref, o_ref, dact_ref, inv_ref, coef_ref, gain_ref, seg_row_ref, seg_col_ref,
    sums_ref, sums_t_ref, state_ref, pair_ref, dz_ref, gain_grad_ref,
):
    seq = pl.program_id(1)
    chunks = z_ref.shape[1] // CHUNK
    row, col, differ = chunk_masks()
    live_end = count_ref[seq] * BLOCK
    gain = gain_ref[...]
    dstate = jnp.zeros((HEAD_DIM, HEAD_DIM), F32)
    gain_total = jnp.zeros((1, HEAD_DIM), F32)
    for c in reversed(range(chunks)):
        rows = pl.ds(c * CHUNK, CHUNK)
        z0, z1, value, z3 = (z_ref[j, rows, :] for j in range(4))
        gate0 = sigmoid(z0)
        query = z0 * gate0
        logf, key = forget_parts(z1)
        high = logf.astype(BF)
        pair = jnp.concatenate([high, (logf - high.astype(F32)).astype(BF)], axis=1)
        seg_col = seg_col_ref[0, rows, :]
        seg_row = seg_row_ref[0, :, c * CHUNK : (c + 1) * CHUNK]
        seg_last = seg_row[:, CHUNK - 1 :]
        value_low = value.astype(BF)

        out = o_ref[rows, :]
        dact = dact_ref[rows, :]
        inv = inv_ref[rows, :]
        gate3 = sigmoid(z3)
        normed = out * inv
        dnorm = dact * (z3 * gate3)
        gain_total = gain_total + jnp.sum(dnorm * normed, axis=0, keepdims=True)
        dz_ref[3, rows, :] = (dact * (normed * gain) * gate3 * (1.0 + z3 * (1.0 - gate3))).astype(BF)
        dout = inv * (dnorm * gain) - out * coef_ref[rows, :]
        position = c * CHUNK + lax.broadcasted_iota(jnp.int32, (CHUNK, 1), 0)
        dout = jnp.where(position < live_end, dout, 0.0)
        dout_low = dout.astype(BF)

        dscore = jnp.where(row > col, dot_nt(dout_low, value_low), dot_nt(value_low, dout_low))
        dscore = jnp.where(seg_col == seg_row, dscore, 0.0).astype(BF)
        scores = pair_ref[0, 0, c]
        zero = jnp.zeros_like(scores)
        dvalue = dot(jnp.where(col >= row, scores, zero), dout_low)
        diagonal = jnp.sum(dout * value, axis=1, keepdims=True)
        dquery = diagonal * key
        dkey = diagonal * query
        dlogf = jnp.zeros((CHUNK, HEAD_DIM), F32)
        for level in range(LEVELS):
            decay = jnp.exp(split_sum(sums_ref[level], pair))
            right = ((row >> level) & 1) == 1
            mixed = decay * jnp.where(right, query, key)
            dmixed = dot(jnp.where((differ >> level) == 1, dscore, zero), mixed.astype(BF))
            through = dmixed * decay
            dquery = dquery + jnp.where(right, through, 0.0)
            dkey = dkey + jnp.where(right, 0.0, through)
            dlogf = dlogf + dot(sums_t_ref[level], (dmixed * mixed).astype(BF))
        from_start = jnp.exp(split_sum(sums_ref[LEVELS], pair))
        total = from_start[CHUNK - 1 :]
        if c > 0:
            seg_before = seg_row_ref[0, :, c * CHUNK - 1 : c * CHUNK]
            carried = seg_col == seg_before
            state = state_ref[0, 0, c]
            reach = jnp.where(carried, query * from_start, 0.0)
            dreach = jnp.where(carried, dot(dout_low, state.astype(BF)), 0.0)
            dquery = dquery + dreach * from_start
            dlogf = dlogf + dot(sums_t_ref[LEVELS], (dreach * reach).astype(BF))
            dstate_new = dot_tn(dout_low, reach.astype(BF))
        if c < chunks - 1:
            to_end = jnp.exp(split_sum(sums_ref[LEVELS + 1], pair))
            in_tail = seg_col == seg_last
            tail = jnp.where(in_tail, key * to_end, 0.0)
            dstate_low = dstate.astype(BF)
            dtail = jnp.where(in_tail, dot(value_low, dstate_low), 0.0)
            dkey = dkey + dtail * to_end
            dlogf = dlogf + dot(sums_t_ref[LEVELS + 1], (dtail * tail).astype(BF))
            dvalue = dvalue + dot_nt(tail.astype(BF), dstate_low)
            if c > 0:
                kept = jnp.where(seg_last == seg_before, total, 0.0)
                dlogf = dlogf + jnp.sum(state * dstate, axis=0, keepdims=True) * kept
                dstate_new = dstate_new + dstate * kept
        if c > 0:
            dstate = dstate_new
        dz_ref[0, rows, :] = (dquery * gate0 * (1.0 + z0 * (1.0 - gate0))).astype(BF)
        dz_ref[1, rows, :] = ((dlogf - dkey * (1.0 - key)) * key).astype(BF)
        dz_ref[2, rows, :] = dvalue.astype(BF)
    gain_grad_ref[...] = jnp.where(seq == 0, gain_total, gain_grad_ref[...] + gain_total)


def mixer_forward(z, gain, segments, counts):
    seqs, seq_len = segments.shape
    rows, width = z.shape[1:]
    heads = width // HEAD_DIM
    chunks = seq_len // CHUNK
    sums = jnp.asarray(decay_sums(), BF)
    grid = (seqs, heads)
    token_spec = pl.BlockSpec((seq_len, HEAD_DIM), lambda s, h: (s, h))
    square_spec = pl.BlockSpec((seq_len, 1), lambda s, h: (s, 0))
    state_spec = pl.BlockSpec((1, 1, chunks, HEAD_DIM, HEAD_DIM), lambda s, h: (s, h, 0, 0, 0))
    return pl.pallas_call(
        mixer_forward_kernel,
        grid=grid,
        in_specs=[
            pl.BlockSpec(memory_space=pltpu.SMEM),
            pl.BlockSpec((4, seq_len, HEAD_DIM), lambda s, h: (0, s, h)),
            pl.BlockSpec((1, HEAD_DIM), lambda s, h: (0, h)),
            pl.BlockSpec((1, 1, seq_len), lambda s, h: (s, 0, 0)),
            pl.BlockSpec((1, seq_len, 1), lambda s, h: (s, 0, 0)),
            pl.BlockSpec(sums.shape, lambda s, h: (0, 0, 0)),
        ],
        out_specs=[token_spec, token_spec, square_spec, state_spec, state_spec],
        out_shape=[
            jax.ShapeDtypeStruct((rows, width), F32),
            jax.ShapeDtypeStruct((rows, width), BF),
            jax.ShapeDtypeStruct((rows, 1), F32),
            jax.ShapeDtypeStruct((seqs, heads, chunks, HEAD_DIM, HEAD_DIM), F32),
            jax.ShapeDtypeStruct((seqs, heads, chunks, HEAD_DIM, HEAD_DIM), BF),
        ],
        compiler_params=pltpu.CompilerParams(vmem_limit_bytes=48 * 1024 * 1024),
        name="mixer_forward",
    )(counts, z, gain, segments[:, None, :], segments[:, :, None], sums)


def mixer_backward(z, o, dact, inv, coef, gain, segments, counts, states, pairs):
    seqs, seq_len = segments.shape
    rows, width = o.shape
    heads = width // HEAD_DIM
    chunks = seq_len // CHUNK
    sums = decay_sums()
    sums_t = jnp.asarray(sums.transpose(0, 2, 1), BF)
    sums = jnp.asarray(sums, BF)
    grid = (heads, seqs)
    token_spec = pl.BlockSpec((seq_len, HEAD_DIM), lambda h, s: (s, h))
    column_spec = pl.BlockSpec((seq_len, 1), lambda h, s: (s, 0))
    z_spec = pl.BlockSpec((4, seq_len, HEAD_DIM), lambda h, s: (0, s, h))
    state_spec = pl.BlockSpec((1, 1, chunks, HEAD_DIM, HEAD_DIM), lambda h, s: (s, h, 0, 0, 0))
    gain_spec = pl.BlockSpec((1, HEAD_DIM), lambda h, s: (0, h))
    sums_spec = pl.BlockSpec(sums.shape, lambda h, s: (0, 0, 0))
    return pl.pallas_call(
        mixer_backward_kernel,
        grid=grid,
        in_specs=[
            pl.BlockSpec(memory_space=pltpu.SMEM),
            z_spec,
            token_spec,
            token_spec,
            column_spec,
            column_spec,
            gain_spec,
            pl.BlockSpec((1, 1, seq_len), lambda h, s: (s, 0, 0)),
            pl.BlockSpec((1, seq_len, 1), lambda h, s: (s, 0, 0)),
            sums_spec,
            sums_spec,
            state_spec,
            state_spec,
        ],
        out_specs=[z_spec, gain_spec],
        out_shape=[
            jax.ShapeDtypeStruct((4, rows, width), BF),
            jax.ShapeDtypeStruct((1, width), F32),
        ],
        compiler_params=pltpu.CompilerParams(vmem_limit_bytes=48 * 1024 * 1024),
        name="mixer_backward",
    )(counts, z, o, dact, inv, coef, gain, segments[:, None, :], segments[:, :, None], sums, sums_t, states, pairs)


def turn(v, axis, step):
    n = lax.axis_size(axis)
    return lax.ppermute(v, axis, [(i, (i + step) % n) for i in range(n)])


def swap(v, axis, bit):
    n = lax.axis_size(axis)
    return lax.ppermute(v, axis, [(i, i ^ bit) for i in range(n)])


def gather_rows(v, axis):
    n = lax.axis_size(axis)
    me = lax.axis_index(axis)
    rows = v.shape[0]
    whole = jnp.zeros((n * rows,) + v.shape[1:], v.dtype)
    pieces = [v] + [turn(v, axis, k) for k in range(1, n)]
    for k, piece in enumerate(pieces):
        whole = lax.dynamic_update_slice_in_dim(whole, piece, (me - k) % n * rows, 0)
    return whole


def gather_near(v, axis):
    n = lax.axis_size(axis)
    return jnp.concatenate([v] + [turn(v, axis, k) for k in range(1, n)], axis=0)


def scatter_rows(v, axis):
    n = lax.axis_size(axis)
    me = lax.axis_index(axis)
    rows = v.shape[0] // n
    pieces = [lax.dynamic_slice_in_dim(v, (me + k) % n * rows, rows, 0) for k in range(n)]
    total = pieces[0].astype(F32)
    for k in range(1, n):
        total = total + turn(pieces[k], axis, k).astype(F32)
    return total


def scatter_near(v, axis):
    n = lax.axis_size(axis)
    rows = v.shape[0] // n
    total = v[:rows].astype(F32)
    for k in range(1, n):
        total = total + turn(v[k * rows : (k + 1) * rows], axis, -k).astype(F32)
    return total


def sum_everywhere(v, axis):
    n = lax.axis_size(axis)
    total = v
    for k in range(1, n):
        total = total + turn(v, axis, k)
    return total


def gather_gains(v):
    bit = 1
    me = lax.axis_index("dp")
    while bit < lax.axis_size("dp"):
        other = swap(v, "dp", bit)
        upper = (me & bit) > 0
        v = jnp.concatenate([jnp.where(upper, other, v), jnp.where(upper, v, other)], axis=1)
        bit *= 2
    return v


def sum_to_slices(v):
    me = lax.axis_index("dp")
    bit = lax.axis_size("dp") // 2
    while bit:
        upper = (me & bit) > 0
        half = v.shape[1] // 2
        keep = jnp.where(upper, v[:, half:], v[:, :half])
        give = jnp.where(upper, v[:, :half], v[:, half:])
        v = keep + swap(give, "dp", bit)
        bit //= 2
    bit = lax.axis_size("mp") // 2
    while bit:
        v = v + swap(v, "mp", bit)
        bit //= 2
    return v


def mean_square(v):
    return jnp.mean(v * v, axis=-1, keepdims=True)


def norm_back(v, scale, weighted):
    return scale * weighted - v * (scale * scale * scale * jnp.mean(weighted * v, axis=-1, keepdims=True))


def apply_update(master, moment, average, gradient):
    moment_new = MOMENT_RATE * moment + gradient
    master_new = master - LEARN_RATE * (gradient + MOMENT_RATE * moment_new)
    average_new = AVERAGE_RATE * average + (1.0 - AVERAGE_RATE) * master_new
    return (gradient, master_new, moment_new, average_new)


def gather_weight(w, dim):
    return lax.all_gather(w.astype(BF), "dp", axis=dim, tiled=True)


def scatter_gradient(g, dim):
    return lax.psum_scatter(g.astype(BF), "dp", scatter_dimension=dim, tiled=True).astype(F32)


def per_device(
    tokens,
    teacher,
    segments,
    block_counts,
    loss_mask,
    mixer_in,
    mixer_in_moment,
    mixer_in_average,
    mixer_out,
    mixer_out_moment,
    mixer_out_average,
    feed_in,
    feed_in_moment,
    feed_in_average,
    feed_out,
    feed_out_moment,
    feed_out_average,
    norm_gains,
    norm_gains_moment,
    norm_gains_average,
):
    mixer_in_work = gather_weight(mixer_in, 1)
    mixer_out_work = gather_weight(mixer_out, 1)
    feed_in_work = gather_weight(feed_in, 1)
    feed_out_work = gather_weight(feed_out, 1)
    gains = gather_gains(norm_gains.astype(BF)).astype(F32)

    row_total = tokens.shape[0]
    seq_here, seq_len = segments.shape
    seq_all = block_counts.shape[0]
    data_rank = lax.axis_index("dp")
    model_rank = lax.axis_index("mp")
    model_size = lax.axis_size("mp")
    local_counts = lax.dynamic_slice_in_dim(block_counts, data_rank * seq_here, seq_here, 0)
    column = jnp.arange(seq_len, dtype=jnp.int32)
    live_all = (column[None, :] < BLOCK * block_counts[:, None]).astype(F32)
    total_count = jnp.sum(loss_mask.reshape(seq_all, seq_len).astype(F32) * live_all)
    first_row = (data_rank * model_size + model_rank) * row_total
    valid = lax.dynamic_slice_in_dim(loss_mask.astype(F32) * live_all.reshape(-1), first_row, row_total, 0)

    inputs = tokens.astype(F32)
    inputs_scale = lax.rsqrt(mean_square(inputs) + EPS)
    tokens_full = gather_rows(tokens, "mp").astype(F32)
    first_full = (tokens_full * lax.rsqrt(mean_square(tokens_full) + EPS) * gains[0]).astype(BF)
    z = jnp.einsum("td,jde->jte", first_full, mixer_in_work, preferred_element_type=F32)
    local_width = z.shape[2]
    gain_out = lax.dynamic_slice_in_dim(gains[2], model_rank * local_width, local_width, 0)[None]
    recurrent, act_raw, square, states, pairs = mixer_forward(z, gain_out, segments, local_counts)
    square = sum_everywhere(square.reshape(-1), "mp")
    out_scale = lax.rsqrt(square / D + EPS)
    out_scale_here = lax.dynamic_slice_in_dim(out_scale, model_rank * row_total, row_total, 0)[:, None]
    mixed = out_scale_here * scatter_rows(dot(act_raw, mixer_out_work).astype(BF), "mp")

    resid = inputs + mixed
    resid_scale = lax.rsqrt(mean_square(resid) + EPS)
    second_full = gather_near((resid * resid_scale * gains[1]).astype(BF), "mp")
    gate_up = jnp.einsum("td,jdf->jtf", second_full, feed_in_work, preferred_element_type=F32)
    gate_sig = jax.nn.sigmoid(gate_up[0])
    gate_act = gate_up[0] * gate_sig
    hidden_low = (gate_act * gate_up[1]).astype(BF)
    final = resid + scatter_near(dot(hidden_low, feed_out_work).astype(BF), "mp")
    output = final.astype(BF)

    error = (final - teacher.astype(F32)) * valid[:, None]
    square_sum = jnp.sum(error * error)
    token_slots = row_total * lax.axis_size("dp") * model_size
    grad_final = token_slots / total_count * error

    grad_full = gather_near(grad_final.astype(BF), "mp")
    grad_hidden = dot_nt(grad_full, feed_out_work)
    grad_gate = (grad_hidden * gate_up[1] * gate_sig * (1.0 + gate_up[0] * (1.0 - gate_sig))).astype(BF)
    grad_up = (grad_hidden * gate_act).astype(BF)
    grad_second = scatter_near(
        (dot_nt(grad_gate, feed_in_work[0]) + dot_nt(grad_up, feed_in_work[1])).astype(BF), "mp"
    )
    feed_out_grad = dot_tn(hidden_low, grad_full)
    feed_in_grad = jnp.stack([dot_tn(second_full, grad_gate), dot_tn(second_full, grad_up)])
    grad_resid = grad_final + norm_back(resid, resid_scale, grad_second * gains[1])
    gain_two_grad = jnp.sum(grad_second * resid * resid_scale, axis=0)

    grad_resid_low = grad_resid.astype(BF)
    coef_here = out_scale_here * out_scale_here * jnp.mean(
        grad_resid_low.astype(F32) * mixed, axis=-1, keepdims=True
    )
    coef = gather_rows(coef_here[:, 0], "mp")
    resid_full = gather_rows(grad_resid_low, "mp")
    grad_act = dot_nt(resid_full, mixer_out_work)
    act_low = (act_raw.astype(F32) * out_scale[:, None]).astype(BF)
    mixer_out_grad = dot_tn(act_low, resid_full)
    dz, gain_out_grad = mixer_backward(
        z, recurrent, grad_act, out_scale[:, None], coef[:, None], gain_out, segments, local_counts, states, pairs
    )
    mixer_in_grad = jnp.einsum("td,jte->jde", first_full, dz, preferred_element_type=F32)
    grad_first = scatter_rows(
        jnp.einsum("jte,jde->td", dz, mixer_in_work, preferred_element_type=F32).astype(BF), "mp"
    )
    tokens_grad = (grad_resid + norm_back(inputs, inputs_scale, grad_first * gains[0])).astype(BF)
    gain_one_grad = jnp.sum(grad_first * inputs * inputs_scale, axis=0)

    feed_out_share = scatter_gradient(feed_out_grad, 1)
    feed_in_share = scatter_gradient(feed_in_grad, 1)
    mixer_out_share = scatter_gradient(mixer_out_grad, 1)
    mixer_in_share = scatter_gradient(mixer_in_grad, 1)

    gain_out_full = lax.dynamic_update_slice_in_dim(
        jnp.zeros((D,), F32), gain_out_grad[0], model_rank * local_width, 0
    )
    sums = sum_to_slices(
        jnp.stack([gain_one_grad, gain_two_grad, gain_out_full, jnp.full((D,), square_sum)])
    )
    gains_share = sums[:3]
    loss_value = sums[3, 0] / (total_count * D)
    first = apply_update(mixer_in, mixer_in_moment, mixer_in_average, mixer_in_share)
    second = apply_update(mixer_out, mixer_out_moment, mixer_out_average, mixer_out_share)
    third = apply_update(feed_in, feed_in_moment, feed_in_average, feed_in_share)
    fourth = apply_update(feed_out, feed_out_moment, feed_out_average, feed_out_share)
    fifth = apply_update(norm_gains, norm_gains_moment, norm_gains_average, gains_share)
    return (output, tokens_grad, loss_value) + first + second + third + fourth + fifth


def solution(mesh):
    tokens = P(("dp", "mp"), None)
    stacked = P(None, "dp", "mp")
    flat = P("mp", "dp")
    gains = P(None, "dp")
    return jax.shard_map(
        per_device,
        mesh=mesh,
        in_specs=(tokens, tokens, P("dp", None), P(), P())
        + (stacked,) * 3 + (flat,) * 3 + (stacked,) * 3 + (flat,) * 3 + (gains,) * 3,
        out_specs=(tokens, tokens, P()) + (stacked,) * 4 + (flat,) * 4 + (stacked,) * 4 + (flat,) * 4 + (gains,) * 4,
        check_vma=False,
    )
```

```python
import functools
import math

import jax
import jax.numpy as jnp
import numpy as np
from jax import lax
from jax.experimental import pallas as pl
from jax.experimental.pallas import tpu as pltpu
from jax.sharding import PartitionSpec as P

D = 2048
HEAD_DIM = 128
BLOCK = 32
CHUNK = 128
LEVELS = 7
VMEM_LIMIT = 16 * 1024 * 1024

EPS = 1e-06
MOMENT_RATE = 0.5
AVERAGE_RATE = 0.5
LEARN_RATE = 4e-05

BF = jnp.bfloat16
F32 = jnp.float32


def decay_sums():
    t = np.arange(CHUNK)[:, None]
    r = np.arange(CHUNK)[None, :]
    mats = []
    for level in range(LEVELS):
        half = 1 << level
        mid = (t // (2 * half)) * (2 * half) + half
        right = t >= mid
        mats.append(np.where(right, (r >= mid) & (r <= t), (r > t) & (r < mid)))
    mats.append(r <= t)
    mats.append(r > t)
    return np.stack(mats).astype(np.float32)


def dot(a, b):
    return lax.dot_general(a, b, (((1,), (0,)), ((), ())), preferred_element_type=F32)


def dot_nt(a, b):
    return lax.dot_general(a, b, (((1,), (1,)), ((), ())), preferred_element_type=F32)


def dot_tn(a, b):
    return lax.dot_general(a, b, (((0,), (0,)), ((), ())), preferred_element_type=F32)


def sigmoid(v):
    return 1.0 / (1.0 + jnp.exp(-v))


def mean_square(v):
    return jnp.mean(v * v, axis=-1, keepdims=True)


def norm_back(v, scale, weighted):
    return scale * weighted - v * (scale * scale * scale * jnp.mean(weighted * v, axis=-1, keepdims=True))


def forget_parts(z):
    small = jnp.exp(-jnp.abs(z))
    logf = jnp.minimum(z, 0.0) - jnp.log1p(small)
    key = jnp.where(z >= 0.0, small, 1.0) / (1.0 + small)
    return logf, key


def split_sum(mat, logf_pair):
    both = dot(mat, logf_pair)
    return both[:, :HEAD_DIM] + both[:, HEAD_DIM:]


def chunk_masks():
    row = lax.broadcasted_iota(jnp.int32, (CHUNK, CHUNK), 0)
    col = lax.broadcasted_iota(jnp.int32, (CHUNK, CHUNK), 1)
    return row, col, row ^ col


class RingRows:
    def __init__(self, rank, ranks, rows):
        self.rank = rank
        self.ranks = ranks
        self.size = rows // ranks
        self.step = math.gcd(CHUNK, self.size)

    def pieces(self, first):
        for at in range(first, first + CHUNK, self.step):
            place = lax.rem(self.rank - at // self.size + self.ranks, self.ranks)
            yield pl.ds(pl.multiple_of(place * self.size + at % self.size, self.step), self.step)

    def load(self, ref, first, *index):
        return jnp.concatenate([ref[(*index, piece)] for piece in self.pieces(first)], axis=0)

    def store(self, ref, first, value, *index):
        for i, piece in enumerate(self.pieces(first)):
            ref[(*index, piece)] = value[i * self.step : (i + 1) * self.step]


def mixer_forward_kernel(ranks, scalar_ref, z_ref, seg_row_ref, seg_col_ref, sums_ref, o_ref, square_ref, state_ref, pair_ref):
    head = pl.program_id(0)
    seqs, _, seq_len = seg_row_ref.shape
    chunks = seq_len // CHUNK
    ring = RingRows(scalar_ref[seqs], ranks, z_ref.shape[1])
    row, col, differ = chunk_masks()
    for seq, c in ((s, c) for s in range(seqs) for c in range(chunks)):
        first = seq * seq_len + c * CHUNK
        if c == 0:
            state = jnp.zeros((HEAD_DIM, HEAD_DIM), F32)
        z0, z1, value = (ring.load(z_ref, first, j) for j in range(3))
        query = z0 * sigmoid(z0)
        logf, key = forget_parts(z1)
        high = logf.astype(BF)
        pair = jnp.concatenate([high, (logf - high.astype(F32)).astype(BF)], axis=1)
        seg_col = seg_col_ref[seq, c * CHUNK : (c + 1) * CHUNK, :]
        seg_row = seg_row_ref[seq, :, c * CHUNK : (c + 1) * CHUNK]
        seg_last = seg_row[:, CHUNK - 1 :]
        value_low = value.astype(BF)
        scores = None
        for level in reversed(range(LEVELS)):
            decay = jnp.exp(split_sum(sums_ref[level], pair))
            right = ((row >> level) & 1) == 1
            mixed = (decay * jnp.where(right, query, key)).astype(BF)
            product = dot_nt(mixed, mixed)
            scores = product if scores is None else jnp.where(differ < (2 << level), product, scores)
        diagonal = jnp.sum(query * key, axis=1, keepdims=True)
        scores = jnp.where(differ == 0, diagonal, scores)
        scores = jnp.where(seg_col == seg_row, scores, 0.0).astype(BF)
        pair_ref[seq, 0, c] = scores
        out = dot(jnp.where(row >= col, scores, jnp.zeros_like(scores)), value_low)
        from_start = jnp.exp(split_sum(sums_ref[LEVELS], pair))
        if c > 0:
            carried = seg_col == seg_before
            reach = jnp.where(carried, query * from_start, 0.0).astype(BF)
            out = out + dot_nt(reach, state.astype(BF))
        state_ref[seq, 0, c] = state
        position = c * CHUNK + lax.broadcasted_iota(jnp.int32, (CHUNK, 1), 0)
        out = jnp.where(position < scalar_ref[seq] * BLOCK, out, 0.0)
        ring.store(o_ref, first, out)
        square = jnp.sum(out * out, axis=1, keepdims=True)
        square = jnp.where(head == 0, square, ring.load(square_ref, first) + square)
        ring.store(square_ref, first, square)
        if c < chunks - 1:
            to_end = jnp.exp(split_sum(sums_ref[LEVELS + 1], pair))
            tail = jnp.where(seg_col == seg_last, key * to_end, 0.0).astype(BF)
            fresh = dot_tn(value_low, tail)
            if c > 0:
                kept = jnp.where(seg_last == seg_before, from_start[CHUNK - 1 :], 0.0)
                fresh = fresh + state * kept
            state = fresh
            seg_before = seg_last


def mixer_backward_kernel(
    ranks, scalar_ref, z_ref, dout_ref, gate_ref, seg_row_ref, seg_col_ref, sums_ref, sums_t_ref, state_ref, pair_ref, dz_ref
):
    seqs, _, seq_len = seg_row_ref.shape
    chunks = seq_len // CHUNK
    ring = RingRows(scalar_ref[seqs], ranks, z_ref.shape[1])
    row, col, differ = chunk_masks()
    dz_ref[3] = gate_ref[...]
    for seq, c in ((s, c) for s in range(seqs) for c in reversed(range(chunks))):
        first = seq * seq_len + c * CHUNK
        z0, z1, value = (ring.load(z_ref, first, j) for j in range(3))
        gate0 = sigmoid(z0)
        query = z0 * gate0
        logf, key = forget_parts(z1)
        high = logf.astype(BF)
        pair = jnp.concatenate([high, (logf - high.astype(F32)).astype(BF)], axis=1)
        seg_col = seg_col_ref[seq, c * CHUNK : (c + 1) * CHUNK, :]
        seg_row = seg_row_ref[seq, :, c * CHUNK : (c + 1) * CHUNK]
        seg_last = seg_row[:, CHUNK - 1 :]
        value_low = value.astype(BF)
        position = c * CHUNK + lax.broadcasted_iota(jnp.int32, (CHUNK, 1), 0)
        dout = jnp.where(position < scalar_ref[seq] * BLOCK, ring.load(dout_ref, first), 0.0)
        dout_low = dout.astype(BF)

        dscore = jnp.where(row > col, dot_nt(dout_low, value_low), dot_nt(value_low, dout_low))
        dscore = jnp.where(seg_col == seg_row, dscore, 0.0).astype(BF)
        scores = pair_ref[seq, 0, c]
        zero = jnp.zeros_like(scores)
        dvalue = dot(jnp.where(col >= row, scores, zero), dout_low)
        diagonal = jnp.sum(dout * value, axis=1, keepdims=True)
        dquery = diagonal * key
        dkey = diagonal * query
        dlogf = jnp.zeros((CHUNK, HEAD_DIM), F32)
        for level in range(LEVELS):
            decay = jnp.exp(split_sum(sums_ref[level], pair))
            right = ((row >> level) & 1) == 1
            mixed = decay * jnp.where(right, query, key)
            dmixed = dot(jnp.where((differ >> level) == 1, dscore, zero), mixed.astype(BF))
            through = dmixed * decay
            dquery = dquery + jnp.where(right, through, 0.0)
            dkey = dkey + jnp.where(right, 0.0, through)
            dlogf = dlogf + dot(sums_t_ref[level], (dmixed * mixed).astype(BF))
        from_start = jnp.exp(split_sum(sums_ref[LEVELS], pair))
        total = from_start[CHUNK - 1 :]
        if c > 0:
            seg_before = seg_row_ref[seq, :, c * CHUNK - 1 : c * CHUNK]
            carried = seg_col == seg_before
            state = state_ref[seq, 0, c]
            reach = jnp.where(carried, query * from_start, 0.0)
            dreach = jnp.where(carried, dot(dout_low, state.astype(BF)), 0.0)
            dquery = dquery + dreach * from_start
            dlogf = dlogf + dot(sums_t_ref[LEVELS], (dreach * reach).astype(BF))
            dstate_new = dot_tn(dout_low, reach.astype(BF))
        if c < chunks - 1:
            to_end = jnp.exp(split_sum(sums_ref[LEVELS + 1], pair))
            in_tail = seg_col == seg_last
            tail = jnp.where(in_tail, key * to_end, 0.0)
            dstate_low = dstate.astype(BF)
            dtail = jnp.where(in_tail, dot(value_low, dstate_low), 0.0)
            dkey = dkey + dtail * to_end
            dlogf = dlogf + dot(sums_t_ref[LEVELS + 1], (dtail * tail).astype(BF))
            dvalue = dvalue + dot_nt(tail.astype(BF), dstate_low)
            if c > 0:
                kept = jnp.where(seg_last == seg_before, total, 0.0)
                dlogf = dlogf + jnp.sum(state * dstate, axis=0, keepdims=True) * kept
                dstate_new = dstate_new + dstate * kept
        if c > 0:
            dstate = dstate_new
        ring.store(dz_ref, first, (dquery * gate0 * (1.0 + z0 * (1.0 - gate0))).astype(BF), 0)
        ring.store(dz_ref, first, ((dlogf - dkey * (1.0 - key)) * key).astype(BF), 1)
        ring.store(dz_ref, first, dvalue.astype(BF), 2)


def mixer_call(kernel, name, operands, kinds, outputs, segments, z, ranks):
    seqs, seq_len = segments.shape
    rows, width = z.shape[1:]
    heads = width // HEAD_DIM
    chunks = seq_len // CHUNK
    matrices = (seqs, heads, chunks, HEAD_DIM, HEAD_DIM)
    shapes = {
        "z": (None, pl.BlockSpec((3, rows, HEAD_DIM), lambda h: (0, 0, h))),
        "dz": ((4, rows, width), pl.BlockSpec((4, rows, HEAD_DIM), lambda h: (0, 0, h))),
        "token": ((rows, width), pl.BlockSpec((rows, HEAD_DIM), lambda h: (0, h))),
        "column": ((rows, 1), pl.BlockSpec((rows, 1), lambda h: (0, 0))),
        "matrix": (matrices, pl.BlockSpec((seqs, 1) + matrices[2:], lambda h: (0, h, 0, 0, 0))),
        "segment_row": (None, pl.BlockSpec((seqs, 1, seq_len), lambda h: (0, 0, 0))),
        "segment_column": (None, pl.BlockSpec((seqs, seq_len, 1), lambda h: (0, 0, 0))),
        "sums": (None, pl.BlockSpec((LEVELS + 2, CHUNK, CHUNK), lambda h: (0, 0, 0))),
        "scalar": (None, pl.BlockSpec(memory_space=pltpu.SMEM)),
    }
    return pl.pallas_call(
        functools.partial(kernel, ranks),
        grid=(heads,),
        in_specs=[shapes[kind][1] for kind in kinds],
        out_specs=[shapes[kind][1] for kind, _ in outputs],
        out_shape=[jax.ShapeDtypeStruct(shapes[kind][0], dtype) for kind, dtype in outputs],
        compiler_params=pltpu.CompilerParams(vmem_limit_bytes=VMEM_LIMIT),
        name=name,
    )(*[pltpu.with_memory_space_constraint(v, pltpu.HBM) if v.ndim > 1 else v for v in operands])


def mixer_forward(z, segments, scalars, ranks):
    sums = jnp.asarray(decay_sums(), BF)
    return mixer_call(
        mixer_forward_kernel,
        "mixer_forward",
        (scalars, z, segments[:, None, :], segments[:, :, None], sums),
        ("scalar", "z", "segment_row", "segment_column", "sums"),
        (("token", F32), ("column", F32), ("matrix", F32), ("matrix", BF)),
        segments,
        z,
        ranks,
    )


def mixer_backward(z, dout, gate_dz, segments, scalars, states, pairs, ranks):
    sums = decay_sums()
    sums_t = jnp.asarray(sums.transpose(0, 2, 1), BF)
    return mixer_call(
        mixer_backward_kernel,
        "mixer_backward",
        (scalars, z, dout, gate_dz, segments[:, None, :], segments[:, :, None], jnp.asarray(sums, BF), sums_t, states, pairs),
        ("scalar", "z", "token", "token", "segment_row", "segment_column", "sums", "sums", "matrix", "matrix"),
        (("dz", BF),),
        segments,
        z,
        ranks,
    )[0]


FREE = pl.CostEstimate(flops=0, bytes_accessed=0, transcendentals=0)


EXTRA = 128
SMALL = 8


def to_columns(small):
    high = small.astype(BF).astype(F32)
    zeros = jnp.zeros((EXTRA - 2 * SMALL, small.shape[1]), F32)
    return jnp.concatenate([high, small - high, zeros], axis=0).T.astype(BF)


def from_columns(columns):
    rows = columns.astype(F32).T
    return rows[:SMALL] + rows[SMALL : 2 * SMALL]


def mixer_gradient_kernel(rows_ref, grads_ref, small_ref, *refs):
    *arrived, out_ref = refs
    rows = rows_ref[...]
    width = grads_ref.shape[2]
    for j in range(grads_ref.shape[0]):
        columns = slice(j * width, (j + 1) * width)
        total = dot_tn(rows, grads_ref[j])
        for ref in arrived:
            total = total + ref[:, columns].astype(F32)
        out_ref[:, columns] = total.astype(BF)
    last = slice(grads_ref.shape[0] * width, out_ref.shape[1])
    small = small_ref[...]
    for ref in arrived:
        small = small + from_columns(ref[:, last])
    out_ref[:, last] = to_columns(small)


def mixer_gradient(rows, span, grads, small, arrived, tile):
    tokens = rows.shape[0]
    count, _, width = grads.shape
    first, last = span
    tile = min(tile, last - first)
    whole = count * width + EXTRA
    return pl.pallas_call(
        mixer_gradient_kernel,
        grid=((last - first) // tile,),
        in_specs=[
            pl.BlockSpec((tokens, tile), lambda i: (0, first // tile + i)),
            pl.BlockSpec((count, tokens, width), lambda i: (0, 0, 0)),
            pl.BlockSpec((SMALL, tile), lambda i: (0, first // tile + i)),
        ]
        + [pl.BlockSpec((tile, whole), lambda i, at=at: (at // tile + i, 0)) for _, at in arrived],
        out_specs=pl.BlockSpec((tile, whole), lambda i: (i, 0)),
        out_shape=jax.ShapeDtypeStruct((last - first, whole), BF),
        compiler_params=pltpu.CompilerParams(vmem_limit_bytes=2 * VMEM_LIMIT),
        cost_estimate=FREE,
        name="mixer_gradient",
    )(rows, grads, small, *[a for a, _ in arrived])


def mixer_in_update_kernel(count, rows_ref, grads_ref, small_ref, *refs):
    arrived, columns = refs[:count], refs[count : 2 * count]
    (master_ref, moment_ref, average_ref, grad_out, master_out, moment_out, average_out, gain_out, small_out) = refs[
        2 * count :
    ]
    total = dot_tn(rows_ref[...], grads_ref[0])
    for ref in arrived:
        total = total + ref[...].astype(F32)
    moment = MOMENT_RATE * moment_ref[0] + total
    master = master_ref[0] - LEARN_RATE * (total + MOMENT_RATE * moment)
    grad_out[0] = total
    moment_out[0] = moment
    master_out[0] = master
    average_out[0] = AVERAGE_RATE * average_ref[0] + (1.0 - AVERAGE_RATE) * master
    product = (master_ref[0].astype(BF).astype(F32) * total).astype(BF)
    gain = dot_nt(jnp.ones((SMALL, product.shape[1]), BF), product)
    gain_out[...] = jnp.where(pl.program_id(0) == 0, gain, gain_out[...] + gain)
    small = small_ref[...]
    for ref in columns:
        small = small + from_columns(ref[...])
    small_out[...] = small


def mixer_in_update(rows, grads, small, arrived, master, moment, average):
    n = master.shape[1]
    count, tokens, width = grads.shape
    last = rows.shape[1] // n - 1
    weight = pl.BlockSpec((1, n, width), lambda k: (k, 0, 0))
    thin = pl.BlockSpec((SMALL, n), lambda k: (0, 0))
    behind = count * width // EXTRA
    return pl.pallas_call(
        functools.partial(mixer_in_update_kernel, len(arrived)),
        grid=(count,),
        in_specs=[
            pl.BlockSpec((tokens, n), lambda k: (0, last)),
            pl.BlockSpec((1, tokens, width), lambda k: (k, 0, 0)),
            pl.BlockSpec((SMALL, n), lambda k: (0, last)),
        ]
        + [pl.BlockSpec((n, width), lambda k, at=at: (at // n, k)) for _, at in arrived]
        + [pl.BlockSpec((n, EXTRA), lambda k, at=at: (at // n, behind)) for _, at in arrived]
        + [weight] * 3,
        out_specs=[weight] * 4 + [thin] * 2,
        out_shape=[jax.ShapeDtypeStruct(master.shape, F32)] * 4 + [jax.ShapeDtypeStruct((SMALL, n), F32)] * 2,
        compiler_params=pltpu.CompilerParams(vmem_limit_bytes=2 * VMEM_LIMIT),
        name="mixer_in_update",
    )(rows, grads, small, *[a for a, _ in arrived], *[a for a, _ in arrived], master, moment, average)


def pair_gradient_kernel(rows_ref, first_ref, second_ref, *refs):
    *arrived, out_ref = refs
    rows = rows_ref[...]
    for j, side in enumerate((first_ref, second_ref)):
        total = dot_tn(rows, side[...])
        for ref in arrived:
            total = total + ref[j].astype(F32)
        out_ref[j] = total.astype(BF)


def pair_gradient(rows, span, first_side, second_side, arrived, tile):
    tokens = rows.shape[0]
    width = first_side.shape[1]
    first, last = span
    tile = min(tile, last - first)
    side = pl.BlockSpec((tokens, width), lambda i: (0, 0))
    return pl.pallas_call(
        pair_gradient_kernel,
        grid=((last - first) // tile,),
        in_specs=[pl.BlockSpec((tokens, tile), lambda i: (0, first // tile + i)), side, side]
        + [pl.BlockSpec((2, tile, width), lambda i, at=at: (0, at // tile + i, 0)) for _, at in arrived],
        out_specs=pl.BlockSpec((2, tile, width), lambda i: (0, i, 0)),
        out_shape=jax.ShapeDtypeStruct((2, last - first, width), BF),
        compiler_params=pltpu.CompilerParams(vmem_limit_bytes=2 * VMEM_LIMIT),
        cost_estimate=FREE,
        name="pair_gradient",
    )(rows, first_side, second_side, *[a for a, _ in arrived])


def wide_gradient_kernel(left_ref, right_ref, *refs):
    *arrived, out_ref = refs
    total = dot_tn(left_ref[...], right_ref[...])
    for ref in arrived:
        total = total + ref[...].astype(F32)
    out_ref[...] = total.astype(BF)


def wide_gradient(left, right, span, arrived, tile):
    tokens, n = left.shape
    first, last = span
    tile = min(tile, last - first)
    return pl.pallas_call(
        wide_gradient_kernel,
        grid=((last - first) // tile,),
        in_specs=[
            pl.BlockSpec((tokens, n), lambda i: (0, 0)),
            pl.BlockSpec((tokens, tile), lambda i: (0, first // tile + i)),
        ]
        + [pl.BlockSpec((n, tile), lambda i, at=at: (0, at // tile + i)) for _, at in arrived],
        out_specs=pl.BlockSpec((n, tile), lambda i: (0, i)),
        out_shape=jax.ShapeDtypeStruct((n, last - first), BF),
        compiler_params=pltpu.CompilerParams(vmem_limit_bytes=VMEM_LIMIT),
        cost_estimate=FREE,
        name="wide_gradient",
    )(left, right, *[a for a, _ in arrived])


def split_column(v):
    high = v.astype(BF)
    return high, (v - high.astype(F32)).astype(BF)


def after_mixer_kernel(count, own_ref, square_ref, tokens_ref, gain_ref, *refs):
    arrived = refs[:count]
    resid_ref, scale_ref, norm_ref = refs[count:]
    mixed = own_ref[...].astype(F32)
    square = square_ref[...]
    for ref in arrived:
        mixed = mixed + ref[:, :D].astype(F32)
        square = square + ref[:, D : D + 1].astype(F32) + ref[:, D + 1 : D + 2].astype(F32)
    scale = lax.rsqrt(square / D + EPS)
    resid = tokens_ref[...].astype(F32) + mixed * scale
    resid_ref[...] = resid
    scale_ref[...] = scale
    norm_ref[...] = (resid * lax.rsqrt(mean_square(resid) + EPS) * gain_ref[...]).astype(BF)


def after_mixer(parts, square, tokens, gain, arrived):
    rows = tokens.shape[0]
    whole = pl.BlockSpec((rows, D), lambda i: (0, 0))
    column = pl.BlockSpec((rows, 1), lambda i: (0, 0))
    return pl.pallas_call(
        functools.partial(after_mixer_kernel, len(arrived)),
        grid=(1,),
        in_specs=[whole, column, whole, pl.BlockSpec((1, D), lambda i: (0, 0))]
        + [pl.BlockSpec((rows, D + EXTRA), lambda i: (0, 0))] * len(arrived),
        out_specs=[whole, column, whole],
        out_shape=[
            jax.ShapeDtypeStruct((rows, D), F32),
            jax.ShapeDtypeStruct((rows, 1), F32),
            jax.ShapeDtypeStruct((rows, D), BF),
        ],
        compiler_params=pltpu.CompilerParams(vmem_limit_bytes=VMEM_LIMIT),
        name="after_mixer",
    )(parts, square, tokens, gain, *arrived)


def after_feed_kernel(count, own_ref, resid_ref, tokens_ref, final_ref, gain_ref, scale_ref, *refs):
    arrived = refs[:count]
    grad_ref, payload_ref = refs[count:]
    grad = own_ref[...].astype(F32)
    for ref in arrived:
        grad = grad + ref[...].astype(F32)
    resid = resid_ref[...]
    grad = final_ref[...] + norm_back(resid, lax.rsqrt(mean_square(resid) + EPS), grad * gain_ref[...])
    grad_ref[...] = grad
    low = grad.astype(BF)
    payload_ref[:, :D] = low
    scale = scale_ref[...]
    mixed = resid - tokens_ref[...].astype(F32)
    coef = scale * scale * jnp.mean(low.astype(F32) * mixed, axis=-1, keepdims=True)
    columns = [part for v in (scale, coef) for part in split_column(v)]
    lane = lax.broadcasted_iota(jnp.int32, (low.shape[0], EXTRA), 1)
    extra = jnp.zeros((low.shape[0], EXTRA), F32)
    for i, part in enumerate(columns):
        extra = jnp.where(lane == i, part.astype(F32), extra)
    payload_ref[:, D:] = extra.astype(BF)


def after_feed(parts, resid, tokens, final, gain, scale, arrived):
    rows = tokens.shape[0]
    whole = pl.BlockSpec((rows, D), lambda i: (0, 0))
    column = pl.BlockSpec((rows, 1), lambda i: (0, 0))
    return pl.pallas_call(
        functools.partial(after_feed_kernel, len(arrived)),
        grid=(1,),
        in_specs=[whole] * 4 + [pl.BlockSpec((1, D), lambda i: (0, 0)), column] + [whole] * len(arrived),
        out_specs=[whole, pl.BlockSpec((rows, D + EXTRA), lambda i: (0, 0))],
        out_shape=[jax.ShapeDtypeStruct((rows, D), F32), jax.ShapeDtypeStruct((rows, D + EXTRA), BF)],
        compiler_params=pltpu.CompilerParams(vmem_limit_bytes=VMEM_LIMIT),
        name="after_feed",
    )(parts, resid, tokens, final, gain, scale, *arrived)


def column_sums_kernel(left_ref, right_ref, out_ref):
    product = left_ref[...].astype(F32) * right_ref[...].astype(F32)
    out_ref[...] = jnp.sum(product, axis=0, keepdims=True)


def column_sums(left, right):
    rows, width = left.shape
    tile = width // 4
    block = pl.BlockSpec((rows, tile), lambda i: (0, i))
    return pl.pallas_call(
        column_sums_kernel,
        grid=(4,),
        in_specs=[block, block],
        out_specs=pl.BlockSpec((1, tile), lambda i: (0, i)),
        out_shape=jax.ShapeDtypeStruct((1, width), F32),
        compiler_params=pltpu.CompilerParams(vmem_limit_bytes=VMEM_LIMIT),
        cost_estimate=FREE,
        name="column_sums",
    )(left, right)[0]


def project_back_kernel(grads_ref, weight_ref, out_ref):
    total = dot_nt(grads_ref[0], weight_ref[0])
    for j in range(1, grads_ref.shape[0]):
        total = total + dot_nt(grads_ref[j], weight_ref[j])
    out_ref[...] = total.astype(BF)


def project_back(grads, weight, tile):
    count, rows, width = grads.shape
    n = weight.shape[1]
    return pl.pallas_call(
        project_back_kernel,
        grid=(n // tile,),
        in_specs=[
            pl.BlockSpec((count, rows, width), lambda i: (0, 0, 0)),
            pl.BlockSpec((count, tile, width), lambda i: (0, i, 0)),
        ],
        out_specs=pl.BlockSpec((rows, tile), lambda i: (0, i)),
        out_shape=jax.ShapeDtypeStruct((rows, n), BF),
        compiler_params=pltpu.CompilerParams(vmem_limit_bytes=VMEM_LIMIT),
        cost_estimate=pl.CostEstimate(flops=0, bytes_accessed=100_000_000, transcendentals=0),
        name="project_back",
    )(grads, weight)


def take_blocks_kernel(order_ref, in_ref, out_ref):
    out_ref[...] = in_ref[...]


def take_blocks(v, order):
    rows, width = v.shape
    count = order.shape[0]
    block = (rows, width // count)
    return pl.pallas_call(
        take_blocks_kernel,
        grid_spec=pltpu.PrefetchScalarGridSpec(
            num_scalar_prefetch=1,
            grid=(count,),
            in_specs=[pl.BlockSpec(block, lambda i, order: (0, order[i]))],
            out_specs=pl.BlockSpec(block, lambda i, order: (0, i)),
        ),
        out_shape=jax.ShapeDtypeStruct(v.shape, v.dtype),
        compiler_params=pltpu.CompilerParams(vmem_limit_bytes=VMEM_LIMIT),
        cost_estimate=FREE,
        name="take_blocks",
    )(order, v)


def mixer_out_update_kernel(count, act_ref, rows_ref, *refs):
    arrived = refs[:count]
    master_ref, moment_ref, average_ref, grad_out, master_out, moment_out, average_out = refs[count:]
    total = arrived[0][...].astype(F32)
    for ref in arrived[1:]:
        total = total + ref[...].astype(F32)
    total = dot_tn(act_ref[...], rows_ref[...]) + total.T
    moment = MOMENT_RATE * moment_ref[...] + total
    master = master_ref[...] - LEARN_RATE * (total + MOMENT_RATE * moment)
    grad_out[...] = total
    moment_out[...] = moment
    master_out[...] = master
    average_out[...] = AVERAGE_RATE * average_ref[...] + (1.0 - AVERAGE_RATE) * master


def mixer_out_update(act, rows, arrived, master, moment, average):
    n = master.shape[1]
    tokens, width = act.shape
    last = rows.shape[1] // n - 1
    whole = pl.BlockSpec((width, n), lambda i: (0, 0))
    return pl.pallas_call(
        functools.partial(mixer_out_update_kernel, len(arrived)),
        grid=(1,),
        in_specs=[pl.BlockSpec((tokens, width), lambda i: (0, 0)), pl.BlockSpec((tokens, n), lambda i: (0, last))]
        + [pl.BlockSpec((n, width), lambda i, at=at: (at // n, 0)) for _, at in arrived]
        + [whole] * 3,
        out_specs=[whole] * 4,
        out_shape=[jax.ShapeDtypeStruct(master.shape, F32)] * 4,
        compiler_params=pltpu.CompilerParams(vmem_limit_bytes=VMEM_LIMIT),
        name="mixer_out_update",
    )(act, rows, *[a for a, _ in arrived], master, moment, average)


def turn(v, axis, step):
    n = lax.axis_size(axis)
    return lax.ppermute(v, axis, [(i, (i + step) % n) for i in range(n)])


def swap(v, axis, bit):
    n = lax.axis_size(axis)
    return lax.ppermute(v, axis, [(i, i ^ bit) for i in range(n)])


def gather_near(v, axis):
    n = lax.axis_size(axis)
    return jnp.concatenate([v] + [turn(v, axis, k) for k in range(1, n)], axis=0)


def scatter_near(v, axis):
    n = lax.axis_size(axis)
    rows = v.shape[0] // n
    total = v[:rows].astype(F32)
    for k in range(1, n):
        total = total + turn(v[k * rows : (k + 1) * rows], axis, -k).astype(F32)
    return total


def gather_gains(v):
    bit = 1
    me = lax.axis_index("dp")
    while bit < lax.axis_size("dp"):
        other = swap(v, "dp", bit)
        upper = (me & bit) > 0
        v = jnp.concatenate([jnp.where(upper, other, v), jnp.where(upper, v, other)], axis=1)
        bit *= 2
    return v


def apply_update(master, moment, average, gradient):
    moment_new = MOMENT_RATE * moment + gradient
    master_new = master - LEARN_RATE * (gradient + MOMENT_RATE * moment_new)
    average_new = AVERAGE_RATE * average + (1.0 - AVERAGE_RATE) * master_new
    return (gradient, master_new, moment_new, average_new)


def gather_weight(w, dim):
    return lax.all_gather(w.astype(BF), "dp", axis=dim, tiled=True)


def link_bits():
    bits = []
    bit = 2
    while bit < lax.axis_size("dp"):
        bits.append(bit)
        bit *= 2
    return bits, bits[::-1]


def block_order(bits):
    if not bits:
        return [0]
    rest = block_order(bits[1:])
    return [bits[0] ^ r for r in rest] + rest


def exchange_order(me):
    even, odd = (block_order(bits) for bits in link_bits())
    order_even = [1 ^ r for r in odd] + even
    order_odd = [1 ^ r for r in even] + odd
    return me ^ jnp.where((me & 1) == 0, jnp.array(order_even, jnp.int32), jnp.array(order_odd, jnp.int32))


def cross_swap(v, stage):
    even, odd = link_bits()
    n = lax.axis_size("dp")
    return lax.ppermute(v, "dp", [(i, i ^ (odd if i & 1 else even)[stage]) for i in range(n)])


def after(v, *others):
    return lax.optimization_barrier((v,) + others)[0]


class GradientSum:
    def __init__(self, piece):
        self.piece = piece
        self.at = 0
        self.left = D
        self.received = []

    def arrived(self):
        return [(r, self.at - first) for r, first in self.received]

    def send(self):
        self.left //= 2
        give = self.piece(self.at, self.at + self.left, self.arrived())
        stage = len(self.received) - 1
        self.at += self.left
        self.received.append((swap(give, "dp", 1) if stage < 0 else cross_swap(give, stage), self.at))
        return give

    def send_rest(self):
        while self.left > D // lax.axis_size("dp"):
            give = self.send()
        return give

    def last(self):
        return self.at, D, self.arrived()


def two_parts(v):
    high = lax.reduce_precision(v, 8, 7)
    return [high.astype(BF), (v - high).astype(BF)]


def pack_columns(values):
    parts = jnp.stack([part for v in values for part in two_parts(v)], axis=1)
    return jnp.pad(parts, ((0, 0), (0, EXTRA - parts.shape[1])))


def unpack_columns(v, count):
    return [v[:, 2 * i].astype(F32) + v[:, 2 * i + 1].astype(F32) for i in range(count)]


def gather_block_weight(w, dim):
    me = lax.axis_index("dp")
    core = me & 1
    even, odd = (block_order(bits) for bits in link_bits())
    order_even = [1 ^ r for r in odd] + even
    order_odd = [1 ^ r for r in even] + odd
    v = w.astype(BF)
    width = v.shape[dim]
    for stage in reversed(range(len(link_bits()[0]))):
        v = jnp.concatenate([cross_swap(v, stage), v], axis=dim)
    parts = [swap(v, "dp", 1), v]
    shape = list(v.shape)
    shape[dim] *= 2
    whole = jnp.zeros(shape, BF)
    for i, (a, b) in enumerate(zip(order_even, order_odd)):
        part = parts[i * 2 // len(order_even)]
        at = i % (len(order_even) // 2) * width
        block = lax.slice_in_dim(part, at, at + width, axis=dim)
        whole = lax.dynamic_update_slice_in_dim(whole, block, (me ^ jnp.where(core == 0, a, b)) * width, dim)
    return whole


def per_device(
    tokens,
    teacher,
    segments,
    block_counts,
    loss_mask,
    mixer_in,
    mixer_in_moment,
    mixer_in_average,
    mixer_out,
    mixer_out_moment,
    mixer_out_average,
    feed_in,
    feed_in_moment,
    feed_in_average,
    feed_out,
    feed_out_moment,
    feed_out_average,
    norm_gains,
    norm_gains_moment,
    norm_gains_average,
):
    mixer_in_work = gather_weight(mixer_in, 1)
    mixer_out_work = gather_block_weight(mixer_out, 1)
    feed_in_work = gather_weight(feed_in, 1)
    feed_out_work = gather_weight(feed_out, 1)
    gains = gather_gains(norm_gains.astype(BF)).astype(F32)

    row_total = tokens.shape[0]
    seq_here, seq_len = segments.shape
    seq_all = block_counts.shape[0]
    data_rank = lax.axis_index("dp")
    model_rank = lax.axis_index("mp")
    model_size = lax.axis_size("mp")
    local_counts = lax.dynamic_slice_in_dim(block_counts, data_rank * seq_here, seq_here, 0)
    order = exchange_order(data_rank.astype(jnp.int32))
    scalars = jnp.concatenate([local_counts, model_rank[None].astype(jnp.int32)])
    column = jnp.arange(seq_len, dtype=jnp.int32)
    live_all = (column[None, :] < BLOCK * block_counts[:, None]).astype(F32)
    total_count = jnp.sum(loss_mask.reshape(seq_all, seq_len).astype(F32) * live_all)
    first_row = (data_rank * model_size + model_rank) * row_total
    valid = lax.dynamic_slice_in_dim(loss_mask.astype(F32) * live_all.reshape(-1), first_row, row_total, 0)

    inputs = tokens.astype(F32)
    inputs_scale = lax.rsqrt(mean_square(inputs) + EPS)
    tokens_full = gather_near(tokens, "mp").astype(F32)
    first_full = (tokens_full * lax.rsqrt(mean_square(tokens_full) + EPS) * gains[0]).astype(BF)
    z = jnp.einsum("td,jde->jte", first_full, mixer_in_work, preferred_element_type=F32)
    gate_z = z[3]
    local_width = z.shape[2]
    gain_out = lax.dynamic_slice_in_dim(gains[2], model_rank * local_width, local_width, 0)[None]
    recurrent, square, states, pairs = mixer_forward(z, segments, scalars, model_size)
    gate_z_sig = jax.nn.sigmoid(gate_z)
    gate_z_act = gate_z * gate_z_sig
    act_raw = (recurrent * gain_out * gate_z_act).astype(BF)
    mixed_parts = dot(act_raw, mixer_out_work).astype(BF)
    arrived = []
    for k in range(1, model_size):
        rows = slice(k * row_total, (k + 1) * row_total)
        payload = jnp.concatenate([mixed_parts[rows], pack_columns([square[rows, 0]])], axis=1)
        arrived.append(turn(payload, "mp", -k))
    first_blocks = take_blocks(first_full, order)
    *arrived, first_blocks = lax.optimization_barrier((*arrived, first_blocks))
    resid, out_scale_here, norm_second = after_mixer(mixed_parts, square, tokens, gains[1:2], arrived)

    second_full = gather_near(norm_second, "mp")
    gate_up = jnp.einsum("td,jdf->jtf", second_full, feed_in_work, preferred_element_type=F32)
    gate_sig = jax.nn.sigmoid(gate_up[0])
    gate_act = gate_up[0] * gate_sig
    hidden_low = (gate_act * gate_up[1]).astype(BF)
    final = resid + scatter_near(dot(hidden_low, feed_out_work).astype(BF), "mp")
    output = final.astype(BF)

    error = (final - teacher.astype(F32)) * valid[:, None]
    square_sum = jnp.sum(error * error)
    token_slots = row_total * lax.axis_size("dp") * model_size
    grad_final = token_slots / total_count * error

    grad_full = gather_near(grad_final.astype(BF), "mp")
    grad_hidden = dot_nt(grad_full, feed_out_work)
    grad_gate = (grad_hidden * gate_up[1] * gate_sig * (1.0 + gate_up[0] * (1.0 - gate_sig))).astype(BF)
    grad_up = (grad_hidden * gate_act).astype(BF)
    grad_second_parts = (dot_nt(grad_gate, feed_in_work[0]) + dot_nt(grad_up, feed_in_work[1])).astype(BF)
    parts = [grad_second_parts[k * row_total : (k + 1) * row_total] for k in range(1, model_size)]
    *parts, grad_late = lax.optimization_barrier((*parts, grad_full))
    arrived = [turn(part, "mp", -k) for k, part in enumerate(parts, 1)]
    grad_blocks = take_blocks(grad_late, order)
    feed_out_sum = GradientSum(
        lambda a, b, arrived: wide_gradient(hidden_low, grad_blocks, (a, b), arrived, 512)
    )
    sent = feed_out_sum.send()
    feed_in_grad = pair_gradient(second_full, (0, D), grad_gate, after(grad_up, sent), [], 256)
    gain_two_grad = column_sums(grad_second_parts, after(second_full, feed_in_grad)) / gains[1]
    sent = feed_out_sum.send()
    *arrived, feed_in_grad, gain_two_grad, _ = lax.optimization_barrier((*arrived, feed_in_grad, gain_two_grad, sent))
    grad_resid, payload = after_feed(
        grad_second_parts, resid, tokens, grad_final, gains[1:2], out_scale_here, arrived
    )

    pieces = [payload] + [turn(payload, "mp", k) for k in range(1, model_size)]
    *pieces, _ = lax.optimization_barrier((*pieces, feed_out_sum.send_rest()))
    payload = jnp.concatenate(pieces, axis=0)
    resid_full = payload[:, :D]
    out_scale, coef = (v[:, None] for v in unpack_columns(payload[:, D:], 2))
    grad_act = dot_nt(resid_full, mixer_out_work)
    act_low = (act_raw.astype(F32) * out_scale).astype(BF)
    normed = recurrent * out_scale
    gate_dz = (grad_act * normed * gain_out * gate_z_sig * (1.0 + gate_z * (1.0 - gate_z_sig))).astype(BF)
    grad_normed = grad_act * gate_z_act
    gain_out_grad = jnp.sum(grad_normed * normed, axis=0)
    grad_recurrent = out_scale * (grad_normed * gain_out) - recurrent * coef

    gain_out_full = lax.dynamic_update_slice_in_dim(
        jnp.zeros((D,), F32), gain_out_grad, model_rank * local_width, 0
    )
    zero = jnp.zeros((D,), F32)
    small = jnp.stack([gain_two_grad, gain_out_full, jnp.full((D,), square_sum)] + [zero] * (SMALL - 3))
    small = take_blocks(small, order)
    dz = mixer_backward(z, grad_recurrent, gate_dz, segments, scalars, states, pairs, model_size)

    in_sum = GradientSum(None)

    def in_piece(dz_then):
        return lambda a, b, arrived: mixer_gradient(first_blocks, (a, b), dz_then, small, arrived, 256)

    in_sum.piece = in_piece(dz)
    sent = in_sum.send()
    grad_first_parts = project_back(after(dz, sent), mixer_in_work, 512)
    in_sum.piece = in_piece(after(dz, grad_first_parts))
    sent = in_sum.send()
    parts = [grad_first_parts[k * row_total : (k + 1) * row_total] for k in range(1, model_size)]
    *parts, act_low, resid_full, dz_then, grad_blocks = lax.optimization_barrier(
        (*parts, act_low, resid_full, dz, grad_blocks, sent)
    )[:-1]
    arrived = [turn(part, "mp", -k) for k, part in enumerate(parts, 1)]

    resid_blocks = take_blocks(resid_full, order)

    def out_piece(a, b, arrived, dtype=BF):
        out = dot_tn(resid_blocks[:, a:b], act_low)
        for r, at in arrived:
            out = out + r[at : at + b - a].astype(F32)
        return out.astype(dtype)

    out_sum = GradientSum(out_piece)
    out_sum.send()
    at, _, feed_arrived = feed_out_sum.last()
    feed_out_share = wide_gradient(hidden_low, grad_blocks, (at, D), feed_arrived, 512)
    fourth = apply_update(feed_out, feed_out_moment, feed_out_average, feed_out_share.astype(F32))

    in_sum.piece = in_piece(dz_then)
    sent = in_sum.send_rest()
    out_sum.send()
    resid_blocks = after(resid_blocks, sent)
    out_sum.send_rest()
    feed_in_share = lax.psum_scatter(feed_in_grad, "dp", scatter_dimension=1, tiled=True)
    feed_in_share = after(feed_in_share, sent)
    third = apply_update(feed_in, feed_in_moment, feed_in_average, feed_in_share.astype(F32))
    *arrived, _ = lax.optimization_barrier((*arrived, sent))
    grad_first = grad_first_parts[:row_total].astype(F32)
    for piece in arrived:
        grad_first = grad_first + piece.astype(F32)
    tokens_grad = (grad_resid + norm_back(inputs, inputs_scale, grad_first * gains[0])).astype(BF)
    *first, gain_one, small = mixer_in_update(
        first_blocks, after(dz, third[3], tokens_grad), small, in_sum.last()[2], mixer_in, mixer_in_moment, mixer_in_average
    )
    sums = jnp.concatenate([gain_one[:1], small[:3]])
    resid_blocks = after(resid_blocks, sums)
    second = tuple(
        mixer_out_update(act_low, resid_blocks, out_sum.last()[2], mixer_out, mixer_out_moment, mixer_out_average)
    )
    sums = sums + sum(turn(sums, "mp", k) for k in range(1, model_size))
    sums = after(sums, second[3])
    gains_share = jnp.concatenate([sums[:1] / norm_gains[:1].astype(BF).astype(F32), sums[1:3]])
    loss_value = sums[3, 0] / (total_count * D)
    fifth = apply_update(norm_gains, norm_gains_moment, norm_gains_average, gains_share)
    return (output, tokens_grad, loss_value) + tuple(first) + second + third + fourth + fifth


def solution(mesh):
    tokens = P(("dp", "mp"), None)
    stacked = P(None, "dp", "mp")
    flat = P("mp", "dp")
    gains = P(None, "dp")
    return jax.shard_map(
        per_device,
        mesh=mesh,
        in_specs=(tokens, tokens, P("dp", None), P(), P())
        + (stacked,) * 3 + (flat,) * 3 + (stacked,) * 3 + (flat,) * 3 + (gains,) * 3,
        out_specs=(tokens, tokens, P()) + (stacked,) * 4 + (flat,) * 4 + (stacked,) * 4 + (flat,) * 4 + (gains,) * 4,
        check_vma=False,
    )
```

```python
import functools
import math

import jax
import jax.numpy as jnp
import numpy as np
from jax import lax
from jax.experimental import pallas as pl
from jax.experimental.pallas import tpu as pltpu
from jax.sharding import PartitionSpec as P

D = 2048
HEAD_DIM = 128
BLOCK = 32
CHUNK = 128
LEVELS = 7
TOGETHER = 1
VMEM_LIMIT = 16 * 1024 * 1024

EPS = 1e-06
MOMENT_RATE = 0.5
AVERAGE_RATE = 0.5
LEARN_RATE = 4e-05

BF = jnp.bfloat16
F32 = jnp.float32


def decay_sums():
    t = np.arange(CHUNK)[:, None]
    r = np.arange(CHUNK)[None, :]
    mats = []
    for level in range(LEVELS):
        half = 1 << level
        mid = (t // (2 * half)) * (2 * half) + half
        right = t >= mid
        mats.append(np.where(right, (r >= mid) & (r <= t), (r > t) & (r < mid)))
    mats.append(r <= t)
    mats.append(r > t)
    return np.stack(mats).astype(np.float32)


def dot(a, b):
    return lax.dot_general(a, b, (((1,), (0,)), ((), ())), preferred_element_type=F32)


def dot_nt(a, b):
    return lax.dot_general(a, b, (((1,), (1,)), ((), ())), preferred_element_type=F32)


def dot_tn(a, b):
    return lax.dot_general(a, b, (((0,), (0,)), ((), ())), preferred_element_type=F32)


def sigmoid(v):
    return 1.0 / (1.0 + jnp.exp(-v))


def mean_square(v):
    return jnp.mean(v * v, axis=-1, keepdims=True)


def norm_back(v, scale, weighted):
    return scale * weighted - v * (scale * scale * scale * jnp.mean(weighted * v, axis=-1, keepdims=True))


def forget_parts(z):
    small = jnp.exp(-jnp.abs(z))
    logf = jnp.minimum(z, 0.0) - jnp.log1p(small)
    key = jnp.where(z >= 0.0, small, 1.0) / (1.0 + small)
    return logf, key


def all_decays(sums_ref, pair):
    count = sums_ref.shape[0]
    both = dot(sums_ref[...].reshape(count * CHUNK, CHUNK), pair)
    decays = jnp.exp(both[:, :HEAD_DIM] + both[:, HEAD_DIM:])
    return [decays[i * CHUNK : (i + 1) * CHUNK] for i in range(count)]


def chunk_masks():
    row = lax.broadcasted_iota(jnp.int32, (CHUNK, CHUNK), 0)
    col = lax.broadcasted_iota(jnp.int32, (CHUNK, CHUNK), 1)
    return row, col, row ^ col


class RingRows:
    def __init__(self, rank, ranks, rows):
        self.rank = rank
        self.ranks = ranks
        self.size = rows // ranks
        self.step = math.gcd(CHUNK, self.size)

    def pieces(self, first):
        for at in range(first, first + CHUNK, self.step):
            place = lax.rem(self.rank - at // self.size + self.ranks, self.ranks)
            yield pl.ds(pl.multiple_of(place * self.size + at % self.size, self.step), self.step)

    def load(self, ref, first, lanes, *index):
        return jnp.concatenate([ref[(*index, piece, lanes)] for piece in self.pieces(first)], axis=0)

    def store(self, ref, first, value, lanes, *index):
        for i, piece in enumerate(self.pieces(first)):
            ref[(*index, piece, lanes)] = value[i * self.step : (i + 1) * self.step]


def mixer_forward_kernel(ranks, scalar_ref, z_ref, seg_row_ref, seg_col_ref, sums_ref, o_ref, square_ref, state_ref, pair_ref):
    step = pl.program_id(0)
    seqs, _, seq_len = seg_row_ref.shape
    chunks = seq_len // CHUNK
    ring = RingRows(scalar_ref[seqs], ranks, z_ref.shape[1])
    row, col, differ = chunk_masks()
    together = z_ref.shape[2] // HEAD_DIM
    carry = [None] * together
    for seq, c, h in ((s, c, h) for s in range(seqs) for c in range(chunks) for h in range(together)):
        first = seq * seq_len + c * CHUNK
        lanes = pl.ds(h * HEAD_DIM, HEAD_DIM)
        state = carry[h]
        if c == 0:
            state = jnp.zeros((HEAD_DIM, HEAD_DIM), F32)
        z0, z1, value = (ring.load(z_ref, first, lanes, j) for j in range(3))
        query = z0 * sigmoid(z0)
        logf, key = forget_parts(z1)
        high = logf.astype(BF)
        pair = jnp.concatenate([high, (logf - high.astype(F32)).astype(BF)], axis=1)
        decays = all_decays(sums_ref, pair)
        seg_col = seg_col_ref[seq, c * CHUNK : (c + 1) * CHUNK, :]
        seg_row = seg_row_ref[seq, :, c * CHUNK : (c + 1) * CHUNK]
        seg_last = seg_row[:, CHUNK - 1 :]
        value_low = value.astype(BF)
        scores = None
        for level in reversed(range(LEVELS)):
            decay = decays[level]
            right = ((row >> level) & 1) == 1
            mixed = (decay * jnp.where(right, query, key)).astype(BF)
            product = dot_nt(mixed, mixed)
            scores = product if scores is None else jnp.where(differ < (2 << level), product, scores)
        diagonal = jnp.sum(query * key, axis=1, keepdims=True)
        scores = jnp.where(differ == 0, diagonal, scores)
        scores = jnp.where(seg_col == seg_row, scores, 0.0).astype(BF)
        pair_ref[seq, h, c] = scores
        out = dot(jnp.where(row >= col, scores, jnp.zeros_like(scores)), value_low)
        from_start = decays[LEVELS]
        if c > 0:
            carried = seg_col == seg_before
            reach = jnp.where(carried, query * from_start, 0.0).astype(BF)
            out = out + dot_nt(reach, state.astype(BF))
        state_ref[seq, h, c] = state
        position = c * CHUNK + lax.broadcasted_iota(jnp.int32, (CHUNK, 1), 0)
        out = jnp.where(position < scalar_ref[seq] * BLOCK, out, 0.0)
        ring.store(o_ref, first, out, lanes)
        square = jnp.sum(out * out, axis=1, keepdims=True)
        if h == 0:
            square = jnp.where(step == 0, square, ring.load(square_ref, first, slice(None)) + square)
        else:
            square = ring.load(square_ref, first, slice(None)) + square
        ring.store(square_ref, first, square, slice(None))
        if c < chunks - 1:
            to_end = decays[LEVELS + 1]
            tail = jnp.where(seg_col == seg_last, key * to_end, 0.0).astype(BF)
            fresh = dot_tn(value_low, tail)
            if c > 0:
                kept = jnp.where(seg_last == seg_before, from_start[CHUNK - 1 :], 0.0)
                fresh = fresh + state * kept
            carry[h] = fresh
            if h == together - 1:
                seg_before = seg_last


def mixer_backward_kernel(
    ranks, scalar_ref, z_ref, dout_ref, gate_ref, seg_row_ref, seg_col_ref, sums_ref, sums_t_ref, state_ref, pair_ref, dz_ref
):
    seqs, _, seq_len = seg_row_ref.shape
    chunks = seq_len // CHUNK
    ring = RingRows(scalar_ref[seqs], ranks, z_ref.shape[1])
    row, col, differ = chunk_masks()
    dz_ref[3] = gate_ref[...]
    together = z_ref.shape[2] // HEAD_DIM
    carry = [None] * together
    for seq, c, h in ((s, c, h) for s in range(seqs) for c in reversed(range(chunks)) for h in range(together)):
        first = seq * seq_len + c * CHUNK
        lanes = pl.ds(h * HEAD_DIM, HEAD_DIM)
        dstate = carry[h]
        z0, z1, value = (ring.load(z_ref, first, lanes, j) for j in range(3))
        gate0 = sigmoid(z0)
        query = z0 * gate0
        logf, key = forget_parts(z1)
        high = logf.astype(BF)
        pair = jnp.concatenate([high, (logf - high.astype(F32)).astype(BF)], axis=1)
        decays = all_decays(sums_ref, pair)
        seg_col = seg_col_ref[seq, c * CHUNK : (c + 1) * CHUNK, :]
        seg_row = seg_row_ref[seq, :, c * CHUNK : (c + 1) * CHUNK]
        seg_last = seg_row[:, CHUNK - 1 :]
        value_low = value.astype(BF)
        position = c * CHUNK + lax.broadcasted_iota(jnp.int32, (CHUNK, 1), 0)
        dout = jnp.where(position < scalar_ref[seq] * BLOCK, ring.load(dout_ref, first, lanes), 0.0)
        dout_low = dout.astype(BF)

        dscore = jnp.where(row > col, dot_nt(dout_low, value_low), dot_nt(value_low, dout_low))
        dscore = jnp.where(seg_col == seg_row, dscore, 0.0).astype(BF)
        scores = pair_ref[seq, h, c]
        zero = jnp.zeros_like(scores)
        dvalue = dot(jnp.where(col >= row, scores, zero), dout_low)
        diagonal = jnp.sum(dout * value, axis=1, keepdims=True)
        dquery = diagonal * key
        dkey = diagonal * query
        dsums = []
        for level in range(LEVELS):
            decay = decays[level]
            right = ((row >> level) & 1) == 1
            mixed = decay * jnp.where(right, query, key)
            dmixed = dot(jnp.where((differ >> level) == 1, dscore, zero), mixed.astype(BF))
            through = dmixed * decay
            dquery = dquery + jnp.where(right, through, 0.0)
            dkey = dkey + jnp.where(right, 0.0, through)
            dsums.append((dmixed * mixed).astype(BF))
        from_start = decays[LEVELS]
        total = from_start[CHUNK - 1 :]
        if c > 0:
            seg_before = seg_row_ref[seq, :, c * CHUNK - 1 : c * CHUNK]
            carried = seg_col == seg_before
            state = state_ref[seq, h, c]
            reach = jnp.where(carried, query * from_start, 0.0)
            dreach = jnp.where(carried, dot(dout_low, state.astype(BF)), 0.0)
            dquery = dquery + dreach * from_start
            dsums.append((dreach * reach).astype(BF))
            dstate_new = dot_tn(dout_low, reach.astype(BF))
        if c < chunks - 1:
            to_end = decays[LEVELS + 1]
            in_tail = seg_col == seg_last
            tail = jnp.where(in_tail, key * to_end, 0.0)
            dstate_low = dstate.astype(BF)
            dtail = jnp.where(in_tail, dot(value_low, dstate_low), 0.0)
            dkey = dkey + dtail * to_end
            dsums.append((dtail * tail).astype(BF))
            dvalue = dvalue + dot_nt(tail.astype(BF), dstate_low)
            if c > 0:
                kept = jnp.where(seg_last == seg_before, total, 0.0)
                dkept = jnp.sum(state * dstate, axis=0, keepdims=True) * kept
                dstate_new = dstate_new + dstate * kept
        if c > 0:
            carry[h] = dstate_new
        used = LEVELS + int(c > 0)
        sums_t = sums_t_ref[:, : used * CHUNK]
        if c < chunks - 1:
            sums_t = jnp.concatenate([sums_t, sums_t_ref[:, (LEVELS + 1) * CHUNK :]], axis=1)
        dlogf = dot(sums_t, jnp.concatenate(dsums, axis=0))
        if 0 < c < chunks - 1:
            dlogf = dlogf + dkept
        ring.store(dz_ref, first, (dquery * gate0 * (1.0 + z0 * (1.0 - gate0))).astype(BF), lanes, 0)
        ring.store(dz_ref, first, ((dlogf - dkey * (1.0 - key)) * key).astype(BF), lanes, 1)
        ring.store(dz_ref, first, dvalue.astype(BF), lanes, 2)


def mixer_call(kernel, name, operands, kinds, outputs, segments, z, ranks):
    seqs, seq_len = segments.shape
    rows, width = z.shape[1:]
    heads = width // HEAD_DIM
    together = math.gcd(heads, TOGETHER)
    lanes = together * HEAD_DIM
    chunks = seq_len // CHUNK
    matrices = (seqs, heads, chunks, HEAD_DIM, HEAD_DIM)
    shapes = {
        "z": (None, pl.BlockSpec((3, rows, lanes), lambda h: (0, 0, h))),
        "dz": ((4, rows, width), pl.BlockSpec((4, rows, lanes), lambda h: (0, 0, h))),
        "token": ((rows, width), pl.BlockSpec((rows, lanes), lambda h: (0, h))),
        "column": ((rows, 1), pl.BlockSpec((rows, 1), lambda h: (0, 0))),
        "matrix": (matrices, pl.BlockSpec((seqs, together) + matrices[2:], lambda h: (0, h, 0, 0, 0))),
        "segment_row": (None, pl.BlockSpec((seqs, 1, seq_len), lambda h: (0, 0, 0))),
        "segment_column": (None, pl.BlockSpec((seqs, seq_len, 1), lambda h: (0, 0, 0))),
        "sums": (None, pl.BlockSpec((LEVELS + 2, CHUNK, CHUNK), lambda h: (0, 0, 0))),
        "sums_t": (None, pl.BlockSpec((CHUNK, (LEVELS + 2) * CHUNK), lambda h: (0, 0))),
        "scalar": (None, pl.BlockSpec(memory_space=pltpu.SMEM)),
    }
    return pl.pallas_call(
        functools.partial(kernel, ranks),
        grid=(heads // together,),
        in_specs=[shapes[kind][1] for kind in kinds],
        out_specs=[shapes[kind][1] for kind, _ in outputs],
        out_shape=[jax.ShapeDtypeStruct(shapes[kind][0], dtype) for kind, dtype in outputs],
        compiler_params=pltpu.CompilerParams(vmem_limit_bytes=VMEM_LIMIT),
        name=name,
    )(*[pltpu.with_memory_space_constraint(v, pltpu.HBM) if v.ndim > 1 else v for v in operands])


def mixer_forward(z, segments, scalars, ranks):
    sums = jnp.asarray(decay_sums(), BF)
    return mixer_call(
        mixer_forward_kernel,
        "mixer_forward",
        (scalars, z, segments[:, None, :], segments[:, :, None], sums),
        ("scalar", "z", "segment_row", "segment_column", "sums"),
        (("token", F32), ("column", F32), ("matrix", F32), ("matrix", BF)),
        segments,
        z,
        ranks,
    )


def mixer_backward(z, dout, gate_dz, segments, scalars, states, pairs, ranks):
    sums = decay_sums()
    sums_t = jnp.asarray(sums.reshape(-1, CHUNK).T, BF)
    return mixer_call(
        mixer_backward_kernel,
        "mixer_backward",
        (scalars, z, dout, gate_dz, segments[:, None, :], segments[:, :, None], jnp.asarray(sums, BF), sums_t, states, pairs),
        ("scalar", "z", "token", "token", "segment_row", "segment_column", "sums", "sums_t", "matrix", "matrix"),
        (("dz", BF),),
        segments,
        z,
        ranks,
    )[0]


def in_hbm(*arrays):
    return [pltpu.with_memory_space_constraint(a, pltpu.HBM) for a in arrays]


FREE = pl.CostEstimate(flops=0, bytes_accessed=0, transcendentals=0)


EXTRA = 128
SMALL = 8


def to_columns(small):
    high = small.astype(BF).astype(F32)
    zeros = jnp.zeros((EXTRA - 2 * SMALL, small.shape[1]), F32)
    return jnp.concatenate([high, small - high, zeros], axis=0).T.astype(BF)


def from_columns(columns):
    rows = columns.astype(F32).T
    return rows[:SMALL] + rows[SMALL : 2 * SMALL]


def mixer_gradient_kernel(rows_ref, grads_ref, small_ref, *refs):
    *arrived, out_ref = refs
    rows = rows_ref[...]
    width = grads_ref.shape[2]
    for j in range(grads_ref.shape[0]):
        columns = slice(j * width, (j + 1) * width)
        total = dot_tn(rows, grads_ref[j])
        for ref in arrived:
            total = total + ref[:, columns].astype(F32)
        out_ref[:, columns] = total.astype(BF)
    last = slice(grads_ref.shape[0] * width, out_ref.shape[1])
    small = small_ref[...]
    for ref in arrived:
        small = small + from_columns(ref[:, last])
    out_ref[:, last] = to_columns(small)


def mixer_gradient(rows, span, grads, small, arrived, tile):
    tokens = rows.shape[0]
    count, _, width = grads.shape
    first, last = span
    tile = min(tile, last - first)
    whole = count * width + EXTRA
    return pl.pallas_call(
        mixer_gradient_kernel,
        grid=((last - first) // tile,),
        in_specs=[
            pl.BlockSpec((tokens, tile), lambda i: (0, first // tile + i)),
            pl.BlockSpec((count, tokens, width), lambda i: (0, 0, 0)),
            pl.BlockSpec((SMALL, tile), lambda i: (0, first // tile + i)),
        ]
        + [pl.BlockSpec((tile, whole), lambda i, at=at: (at // tile + i, 0)) for _, at in arrived],
        out_specs=pl.BlockSpec((tile, whole), lambda i: (i, 0)),
        out_shape=jax.ShapeDtypeStruct((last - first, whole), BF),
        compiler_params=pltpu.CompilerParams(vmem_limit_bytes=2 * VMEM_LIMIT),
        cost_estimate=FREE,
        name="mixer_gradient",
    )(rows, grads, small, *[a for a, _ in arrived])


def mixer_in_update_kernel(count, rows_ref, grads_ref, small_ref, *refs):
    arrived, columns = refs[:count], refs[count : 2 * count]
    (master_ref, moment_ref, average_ref, grad_out, master_out, moment_out, average_out, gain_out, small_out) = refs[
        2 * count :
    ]
    total = dot_tn(rows_ref[...], grads_ref[0])
    for ref in arrived:
        total = total + ref[...].astype(F32)
    moment = MOMENT_RATE * moment_ref[0] + total
    master = master_ref[0] - LEARN_RATE * (total + MOMENT_RATE * moment)
    grad_out[0] = total
    moment_out[0] = moment
    master_out[0] = master
    average_out[0] = AVERAGE_RATE * average_ref[0] + (1.0 - AVERAGE_RATE) * master
    product = (master_ref[0].astype(BF).astype(F32) * total).astype(BF)
    gain = dot_nt(jnp.ones((SMALL, product.shape[1]), BF), product)
    gain_out[...] = jnp.where(pl.program_id(0) == 0, gain, gain_out[...] + gain)
    small = small_ref[...]
    for ref in columns:
        small = small + from_columns(ref[...])
    small_out[...] = small


def mixer_in_update(rows, grads, small, arrived, master, moment, average):
    n = master.shape[1]
    count, tokens, width = grads.shape
    last = rows.shape[1] // n - 1
    weight = pl.BlockSpec((1, n, width), lambda k: (k, 0, 0))
    thin = pl.BlockSpec((SMALL, n), lambda k: (0, 0))
    behind = count * width // EXTRA
    return pl.pallas_call(
        functools.partial(mixer_in_update_kernel, len(arrived)),
        grid=(count,),
        in_specs=[
            pl.BlockSpec((tokens, n), lambda k: (0, last)),
            pl.BlockSpec((1, tokens, width), lambda k: (k, 0, 0)),
            pl.BlockSpec((SMALL, n), lambda k: (0, last)),
        ]
        + [pl.BlockSpec((n, width), lambda k, at=at: (at // n, k)) for _, at in arrived]
        + [pl.BlockSpec((n, EXTRA), lambda k, at=at: (at // n, behind)) for _, at in arrived]
        + [weight] * 3,
        out_specs=[weight] * 4 + [thin] * 2,
        out_shape=[jax.ShapeDtypeStruct(master.shape, F32)] * 4 + [jax.ShapeDtypeStruct((SMALL, n), F32)] * 2,
        compiler_params=pltpu.CompilerParams(vmem_limit_bytes=2 * VMEM_LIMIT),
        name="mixer_in_update",
    )(
        rows,
        grads,
        small,
        *[a for a, _ in arrived],
        *[a for a, _ in arrived],
        *in_hbm(master, moment, average),
    )


def pair_gradient_kernel(rows_ref, first_ref, second_ref, *refs):
    *arrived, out_ref = refs
    rows = rows_ref[...]
    for j, side in enumerate((first_ref, second_ref)):
        total = dot_tn(rows, side[...])
        for ref in arrived:
            total = total + ref[j].astype(F32)
        out_ref[j] = total.astype(BF)


def pair_gradient(rows, span, first_side, second_side, arrived, tile):
    tokens = rows.shape[0]
    width = first_side.shape[1]
    first, last = span
    tile = min(tile, last - first)
    side = pl.BlockSpec((tokens, width), lambda i: (0, 0))
    return pl.pallas_call(
        pair_gradient_kernel,
        grid=((last - first) // tile,),
        in_specs=[pl.BlockSpec((tokens, tile), lambda i: (0, first // tile + i)), side, side]
        + [pl.BlockSpec((2, tile, width), lambda i, at=at: (0, at // tile + i, 0)) for _, at in arrived],
        out_specs=pl.BlockSpec((2, tile, width), lambda i: (0, i, 0)),
        out_shape=jax.ShapeDtypeStruct((2, last - first, width), BF),
        compiler_params=pltpu.CompilerParams(vmem_limit_bytes=2 * VMEM_LIMIT),
        cost_estimate=FREE,
        name="pair_gradient",
    )(rows, first_side, second_side, *[a for a, _ in arrived])


def wide_gradient_kernel(left_ref, right_ref, *refs):
    *arrived, out_ref = refs
    total = dot_tn(left_ref[...], right_ref[...])
    for ref in arrived:
        total = total + ref[...].astype(F32)
    out_ref[...] = total.astype(BF)


def wide_gradient(left, right, span, arrived, tile):
    tokens, n = left.shape
    first, last = span
    tile = min(tile, last - first)
    return pl.pallas_call(
        wide_gradient_kernel,
        grid=((last - first) // tile,),
        in_specs=[
            pl.BlockSpec((tokens, n), lambda i: (0, 0)),
            pl.BlockSpec((tokens, tile), lambda i: (0, first // tile + i)),
        ]
        + [pl.BlockSpec((n, tile), lambda i, at=at: (0, at // tile + i)) for _, at in arrived],
        out_specs=pl.BlockSpec((n, tile), lambda i: (0, i)),
        out_shape=jax.ShapeDtypeStruct((n, last - first), BF),
        compiler_params=pltpu.CompilerParams(vmem_limit_bytes=VMEM_LIMIT),
        cost_estimate=FREE,
        name="wide_gradient",
    )(*in_hbm(left, right, *[a for a, _ in arrived]))


def split_column(v):
    high = v.astype(BF)
    return high, (v - high.astype(F32)).astype(BF)


def after_mixer_kernel(count, own_ref, square_ref, tokens_ref, gain_ref, *refs):
    arrived = refs[:count]
    resid_ref, scale_ref, norm_ref = refs[count:]
    mixed = own_ref[...].astype(F32)
    square = square_ref[...]
    for ref in arrived:
        mixed = mixed + ref[:, :D].astype(F32)
        square = square + ref[:, D : D + 1].astype(F32) + ref[:, D + 1 : D + 2].astype(F32)
    scale = lax.rsqrt(square / D + EPS)
    resid = tokens_ref[...].astype(F32) + mixed * scale
    resid_ref[...] = resid
    scale_ref[...] = scale
    norm_ref[...] = (resid * lax.rsqrt(mean_square(resid) + EPS) * gain_ref[...]).astype(BF)


def after_mixer(parts, square, tokens, gain, arrived):
    rows = tokens.shape[0]
    whole = pl.BlockSpec((rows, D), lambda i: (0, 0))
    column = pl.BlockSpec((rows, 1), lambda i: (0, 0))
    return pl.pallas_call(
        functools.partial(after_mixer_kernel, len(arrived)),
        grid=(1,),
        in_specs=[whole, column, whole, pl.BlockSpec((1, D), lambda i: (0, 0))]
        + [pl.BlockSpec((rows, D + EXTRA), lambda i: (0, 0))] * len(arrived),
        out_specs=[whole, column, whole],
        out_shape=[
            jax.ShapeDtypeStruct((rows, D), F32),
            jax.ShapeDtypeStruct((rows, 1), F32),
            jax.ShapeDtypeStruct((rows, D), BF),
        ],
        compiler_params=pltpu.CompilerParams(vmem_limit_bytes=VMEM_LIMIT),
        name="after_mixer",
    )(parts, square, tokens, gain, *arrived)


def after_feed_kernel(count, own_ref, resid_ref, tokens_ref, final_ref, gain_ref, scale_ref, *refs):
    arrived = refs[:count]
    grad_ref, payload_ref = refs[count:]
    grad = own_ref[...].astype(F32)
    for ref in arrived:
        grad = grad + ref[...].astype(F32)
    resid = resid_ref[...]
    grad = final_ref[...] + norm_back(resid, lax.rsqrt(mean_square(resid) + EPS), grad * gain_ref[...])
    grad_ref[...] = grad
    low = grad.astype(BF)
    payload_ref[:, :D] = low
    scale = scale_ref[...]
    mixed = resid - tokens_ref[...].astype(F32)
    coef = scale * scale * jnp.mean(low.astype(F32) * mixed, axis=-1, keepdims=True)
    columns = [part for v in (scale, coef) for part in split_column(v)]
    lane = lax.broadcasted_iota(jnp.int32, (low.shape[0], EXTRA), 1)
    extra = jnp.zeros((low.shape[0], EXTRA), F32)
    for i, part in enumerate(columns):
        extra = jnp.where(lane == i, part.astype(F32), extra)
    payload_ref[:, D:] = extra.astype(BF)


def after_feed(parts, resid, tokens, final, gain, scale, arrived):
    rows = tokens.shape[0]
    whole = pl.BlockSpec((rows, D), lambda i: (0, 0))
    column = pl.BlockSpec((rows, 1), lambda i: (0, 0))
    return pl.pallas_call(
        functools.partial(after_feed_kernel, len(arrived)),
        grid=(1,),
        in_specs=[whole] * 4 + [pl.BlockSpec((1, D), lambda i: (0, 0)), column] + [whole] * len(arrived),
        out_specs=[whole, pl.BlockSpec((rows, D + EXTRA), lambda i: (0, 0))],
        out_shape=[jax.ShapeDtypeStruct((rows, D), F32), jax.ShapeDtypeStruct((rows, D + EXTRA), BF)],
        compiler_params=pltpu.CompilerParams(vmem_limit_bytes=VMEM_LIMIT),
        name="after_feed",
    )(parts, resid, tokens, final, gain, scale, *arrived)


def column_sums_kernel(left_ref, right_ref, out_ref):
    product = left_ref[...].astype(F32) * right_ref[...].astype(F32)
    out_ref[...] = jnp.sum(product, axis=0, keepdims=True)


def column_sums(left, right):
    rows, width = left.shape
    tile = width // 4
    block = pl.BlockSpec((rows, tile), lambda i: (0, i))
    return pl.pallas_call(
        column_sums_kernel,
        grid=(4,),
        in_specs=[block, block],
        out_specs=pl.BlockSpec((1, tile), lambda i: (0, i)),
        out_shape=jax.ShapeDtypeStruct((1, width), F32),
        compiler_params=pltpu.CompilerParams(vmem_limit_bytes=VMEM_LIMIT),
        cost_estimate=FREE,
        name="column_sums",
    )(left, right)[0]


def project_back_kernel(grads_ref, weight_ref, out_ref):
    total = dot_nt(grads_ref[0], weight_ref[0])
    for j in range(1, grads_ref.shape[0]):
        total = total + dot_nt(grads_ref[j], weight_ref[j])
    out_ref[...] = total.astype(BF)


def project_back(grads, weight, tile):
    count, rows, width = grads.shape
    n = weight.shape[1]
    return pl.pallas_call(
        project_back_kernel,
        grid=(n // tile,),
        in_specs=[
            pl.BlockSpec((count, rows, width), lambda i: (0, 0, 0)),
            pl.BlockSpec((count, tile, width), lambda i: (0, i, 0)),
        ],
        out_specs=pl.BlockSpec((rows, tile), lambda i: (0, i)),
        out_shape=jax.ShapeDtypeStruct((rows, n), BF),
        compiler_params=pltpu.CompilerParams(vmem_limit_bytes=VMEM_LIMIT),
        cost_estimate=pl.CostEstimate(flops=0, bytes_accessed=100_000_000, transcendentals=0),
        name="project_back",
    )(grads, *in_hbm(weight))


def take_blocks_kernel(order_ref, in_ref, out_ref):
    out_ref[...] = in_ref[...]


def take_blocks(v, order):
    rows, width = v.shape[0], D
    count = order.shape[0]
    block = (rows, width // count)
    return pl.pallas_call(
        take_blocks_kernel,
        grid_spec=pltpu.PrefetchScalarGridSpec(
            num_scalar_prefetch=1,
            grid=(count,),
            in_specs=[pl.BlockSpec(block, lambda i, order: (0, order[i]))],
            out_specs=pl.BlockSpec(block, lambda i, order: (0, i)),
        ),
        out_shape=jax.ShapeDtypeStruct((rows, width), v.dtype),
        compiler_params=pltpu.CompilerParams(vmem_limit_bytes=VMEM_LIMIT),
        cost_estimate=FREE,
        name="take_blocks",
    )(order, v)


def mixer_out_update_kernel(count, act_ref, rows_ref, *refs):
    arrived = refs[:count]
    master_ref, moment_ref, average_ref, grad_out, master_out, moment_out, average_out = refs[count:]
    total = arrived[0][...].astype(F32)
    for ref in arrived[1:]:
        total = total + ref[...].astype(F32)
    total = dot_tn(act_ref[...], rows_ref[...]) + total.T
    moment = MOMENT_RATE * moment_ref[...] + total
    master = master_ref[...] - LEARN_RATE * (total + MOMENT_RATE * moment)
    grad_out[...] = total
    moment_out[...] = moment
    master_out[...] = master
    average_out[...] = AVERAGE_RATE * average_ref[...] + (1.0 - AVERAGE_RATE) * master


def mixer_out_update(act, rows, arrived, master, moment, average):
    n = master.shape[1]
    tokens, width = act.shape
    last = rows.shape[1] // n - 1
    whole = pl.BlockSpec((width, n), lambda i: (0, 0))
    return pl.pallas_call(
        functools.partial(mixer_out_update_kernel, len(arrived)),
        grid=(1,),
        in_specs=[pl.BlockSpec((tokens, width), lambda i: (0, 0)), pl.BlockSpec((tokens, n), lambda i: (0, last))]
        + [pl.BlockSpec((n, width), lambda i, at=at: (at // n, 0)) for _, at in arrived]
        + [whole] * 3,
        out_specs=[whole] * 4,
        out_shape=[jax.ShapeDtypeStruct(master.shape, F32)] * 4,
        compiler_params=pltpu.CompilerParams(vmem_limit_bytes=VMEM_LIMIT),
        name="mixer_out_update",
    )(act, rows, *[a for a, _ in arrived], *in_hbm(master, moment, average))


def turn(v, axis, step):
    n = lax.axis_size(axis)
    return lax.ppermute(v, axis, [(i, (i + step) % n) for i in range(n)])


def swap(v, axis, bit):
    n = lax.axis_size(axis)
    return lax.ppermute(v, axis, [(i, i ^ bit) for i in range(n)])


def gather_near(v, axis):
    n = lax.axis_size(axis)
    return jnp.concatenate([v] + [turn(v, axis, k) for k in range(1, n)], axis=0)


def scatter_near(v, axis):
    n = lax.axis_size(axis)
    rows = v.shape[0] // n
    total = v[:rows].astype(F32)
    for k in range(1, n):
        total = total + turn(v[k * rows : (k + 1) * rows], axis, -k).astype(F32)
    return total


def gather_gains(v):
    bit = 1
    me = lax.axis_index("dp")
    while bit < lax.axis_size("dp"):
        other = swap(v, "dp", bit)
        upper = (me & bit) > 0
        v = jnp.concatenate([jnp.where(upper, other, v), jnp.where(upper, v, other)], axis=1)
        bit *= 2
    return v


def apply_update(master, moment, average, gradient):
    moment_new = MOMENT_RATE * moment + gradient
    master_new = master - LEARN_RATE * (gradient + MOMENT_RATE * moment_new)
    average_new = AVERAGE_RATE * average + (1.0 - AVERAGE_RATE) * master_new
    return (gradient, master_new, moment_new, average_new)


def gather_weight(w, dim):
    return lax.all_gather(w.astype(BF), "dp", axis=dim, tiled=True)


def link_bits():
    bits = []
    bit = 2
    while bit < lax.axis_size("dp"):
        bits.append(bit)
        bit *= 2
    return bits, bits[::-1]


def block_order(bits):
    if not bits:
        return [0]
    rest = block_order(bits[1:])
    return [bits[0] ^ r for r in rest] + rest


def exchange_order(me):
    even, odd = (block_order(bits) for bits in link_bits())
    order_even = [1 ^ r for r in odd] + even
    order_odd = [1 ^ r for r in even] + odd
    return me ^ jnp.where((me & 1) == 0, jnp.array(order_even, jnp.int32), jnp.array(order_odd, jnp.int32))


def cross_swap(v, stage):
    even, odd = link_bits()
    n = lax.axis_size("dp")
    return lax.ppermute(v, "dp", [(i, i ^ (odd if i & 1 else even)[stage]) for i in range(n)])


def after(v, *others):
    return lax.optimization_barrier((v,) + others)[0]


class GradientSum:
    def __init__(self, piece):
        self.piece = piece
        self.at = 0
        self.left = D
        self.received = []

    def arrived(self):
        return [(r, self.at - first) for r, first in self.received]

    def send(self):
        self.left //= 2
        give = self.piece(self.at, self.at + self.left, self.arrived())
        stage = len(self.received) - 1
        self.at += self.left
        self.received.append((swap(give, "dp", 1) if stage < 0 else cross_swap(give, stage), self.at))
        return give

    def send_rest(self):
        while self.left > D // lax.axis_size("dp"):
            give = self.send()
        return give

    def last(self):
        return self.at, D, self.arrived()


def two_parts(v):
    high = lax.reduce_precision(v, 8, 7)
    return [high.astype(BF), (v - high).astype(BF)]


def pack_columns(values):
    parts = jnp.stack([part for v in values for part in two_parts(v)], axis=1)
    return jnp.pad(parts, ((0, 0), (0, EXTRA - parts.shape[1])))


def unpack_columns(v, count):
    return [v[:, 2 * i].astype(F32) + v[:, 2 * i + 1].astype(F32) for i in range(count)]


def gather_block_weight(w, dim):
    me = lax.axis_index("dp")
    core = me & 1
    even, odd = (block_order(bits) for bits in link_bits())
    order_even = [1 ^ r for r in odd] + even
    order_odd = [1 ^ r for r in even] + odd
    v = w.astype(BF)
    width = v.shape[dim]
    for stage in reversed(range(len(link_bits()[0]))):
        v = jnp.concatenate([cross_swap(v, stage), v], axis=dim)
    parts = [swap(v, "dp", 1), v]
    shape = list(v.shape)
    shape[dim] *= 2
    whole = jnp.zeros(shape, BF)
    for i, (a, b) in enumerate(zip(order_even, order_odd)):
        part = parts[i * 2 // len(order_even)]
        at = i % (len(order_even) // 2) * width
        block = lax.slice_in_dim(part, at, at + width, axis=dim)
        whole = lax.dynamic_update_slice_in_dim(whole, block, (me ^ jnp.where(core == 0, a, b)) * width, dim)
    return whole


def per_device(
    tokens,
    teacher,
    segments,
    block_counts,
    loss_mask,
    mixer_in,
    mixer_in_moment,
    mixer_in_average,
    mixer_out,
    mixer_out_moment,
    mixer_out_average,
    feed_in,
    feed_in_moment,
    feed_in_average,
    feed_out,
    feed_out_moment,
    feed_out_average,
    norm_gains,
    norm_gains_moment,
    norm_gains_average,
):
    mixer_in_work = gather_weight(mixer_in, 1)
    mixer_out_work = gather_block_weight(mixer_out, 1)
    feed_in_work = gather_weight(feed_in, 1)
    feed_out_work = gather_weight(feed_out, 1)
    gains = gather_gains(norm_gains.astype(BF)).astype(F32)

    row_total = tokens.shape[0]
    seq_here, seq_len = segments.shape
    seq_all = block_counts.shape[0]
    data_rank = lax.axis_index("dp")
    model_rank = lax.axis_index("mp")
    model_size = lax.axis_size("mp")
    local_counts = lax.dynamic_slice_in_dim(block_counts, data_rank * seq_here, seq_here, 0)
    order = exchange_order(data_rank.astype(jnp.int32))
    scalars = jnp.concatenate([local_counts, model_rank[None].astype(jnp.int32)])
    column = jnp.arange(seq_len, dtype=jnp.int32)
    live_all = (column[None, :] < BLOCK * block_counts[:, None]).astype(F32)
    total_count = jnp.sum(loss_mask.reshape(seq_all, seq_len).astype(F32) * live_all)
    first_row = (data_rank * model_size + model_rank) * row_total
    valid = lax.dynamic_slice_in_dim(loss_mask.astype(F32) * live_all.reshape(-1), first_row, row_total, 0)

    inputs = tokens.astype(F32)
    inputs_scale = lax.rsqrt(mean_square(inputs) + EPS)
    tokens_full = gather_near(tokens, "mp").astype(F32)
    first_full = (tokens_full * lax.rsqrt(mean_square(tokens_full) + EPS) * gains[0]).astype(BF)
    z = jnp.einsum("td,jde->jte", first_full, mixer_in_work, preferred_element_type=F32)
    gate_z = z[3]
    local_width = z.shape[2]
    gain_out = lax.dynamic_slice_in_dim(gains[2], model_rank * local_width, local_width, 0)[None]
    recurrent, square, states, pairs = mixer_forward(z, segments, scalars, model_size)
    gate_z_sig = jax.nn.sigmoid(gate_z)
    gate_z_act = gate_z * gate_z_sig
    act_raw = (recurrent * gain_out * gate_z_act).astype(BF)
    mixed_parts = dot(act_raw, mixer_out_work).astype(BF)
    arrived = []
    for k in range(1, model_size):
        rows = slice(k * row_total, (k + 1) * row_total)
        payload = jnp.concatenate([mixed_parts[rows], pack_columns([square[rows, 0]])], axis=1)
        arrived.append(turn(payload, "mp", -k))
    first_blocks = take_blocks(first_full, order)
    *arrived, first_blocks = lax.optimization_barrier((*arrived, first_blocks))
    resid, out_scale_here, norm_second = after_mixer(mixed_parts, square, tokens, gains[1:2], arrived)

    second_full = gather_near(norm_second, "mp")
    gate_up = jnp.einsum("td,jdf->jtf", second_full, feed_in_work, preferred_element_type=F32)
    gate_sig = jax.nn.sigmoid(gate_up[0])
    gate_act = gate_up[0] * gate_sig
    hidden_low = (gate_act * gate_up[1]).astype(BF)
    final = resid + scatter_near(dot(hidden_low, feed_out_work).astype(BF), "mp")
    output = final.astype(BF)

    error = (final - teacher.astype(F32)) * valid[:, None]
    square_sum = jnp.sum(error * error)
    token_slots = row_total * lax.axis_size("dp") * model_size
    grad_final = token_slots / total_count * error

    grad_full = gather_near(grad_final.astype(BF), "mp")
    grad_hidden = dot_nt(grad_full, feed_out_work)
    grad_gate = (grad_hidden * gate_up[1] * gate_sig * (1.0 + gate_up[0] * (1.0 - gate_sig))).astype(BF)
    grad_up = (grad_hidden * gate_act).astype(BF)
    grad_second_parts = (dot_nt(grad_gate, feed_in_work[0]) + dot_nt(grad_up, feed_in_work[1])).astype(BF)
    parts = [grad_second_parts[k * row_total : (k + 1) * row_total] for k in range(1, model_size)]
    *parts, grad_late = lax.optimization_barrier((*parts, grad_full))
    arrived = [turn(part, "mp", -k) for k, part in enumerate(parts, 1)]
    grad_blocks = take_blocks(grad_late, order)
    feed_out_sum = GradientSum(
        lambda a, b, arrived: wide_gradient(hidden_low, grad_blocks, (a, b), arrived, 512)
    )
    sent = feed_out_sum.send()
    feed_in_grad = pair_gradient(second_full, (0, D), grad_gate, after(grad_up, sent), [], 256)
    gain_two_grad = column_sums(grad_second_parts, after(second_full, feed_in_grad)) / gains[1]
    sent = feed_out_sum.send()
    *arrived, feed_in_grad, gain_two_grad, _ = lax.optimization_barrier((*arrived, feed_in_grad, gain_two_grad, sent))
    grad_resid, payload = after_feed(
        grad_second_parts, resid, tokens, grad_final, gains[1:2], out_scale_here, arrived
    )

    pieces = [payload] + [turn(payload, "mp", k) for k in range(1, model_size)]
    *pieces, _ = lax.optimization_barrier((*pieces, feed_out_sum.send_rest()))
    payload = jnp.concatenate(pieces, axis=0)
    resid_full = payload[:, :D]
    out_scale, coef = (v[:, None] for v in unpack_columns(payload[:, D:], 2))
    grad_act = dot_nt(resid_full, mixer_out_work)
    act_low = (act_raw.astype(F32) * out_scale).astype(BF)
    normed = recurrent * out_scale
    gate_dz = (grad_act * normed * gain_out * gate_z_sig * (1.0 + gate_z * (1.0 - gate_z_sig))).astype(BF)
    grad_normed = grad_act * gate_z_act
    gain_out_grad = jnp.sum(grad_normed * normed, axis=0)
    grad_recurrent = out_scale * (grad_normed * gain_out) - recurrent * coef

    gain_out_full = lax.dynamic_update_slice_in_dim(
        jnp.zeros((D,), F32), gain_out_grad, model_rank * local_width, 0
    )
    zero = jnp.zeros((D,), F32)
    small = jnp.stack([gain_two_grad, gain_out_full, jnp.full((D,), square_sum)] + [zero] * (SMALL - 3))
    small = take_blocks(small, order)
    dz = mixer_backward(z, grad_recurrent, gate_dz, segments, scalars, states, pairs, model_size)

    in_sum = GradientSum(None)

    def in_piece(dz_then):
        return lambda a, b, arrived: mixer_gradient(first_blocks, (a, b), dz_then, small, arrived, 256)

    in_sum.piece = in_piece(dz)
    sent = in_sum.send()
    grad_first_parts = project_back(after(dz, sent), mixer_in_work, 512)
    in_sum.piece = in_piece(after(dz, grad_first_parts))
    sent = in_sum.send()
    ranked = jnp.concatenate(
        [
            lax.dynamic_slice_in_dim(grad_first_parts, (model_rank - r) % model_size * row_total, row_total, 0)
            for r in range(model_size)
        ]
    )
    ranked, dz_then, grad_blocks, _ = lax.optimization_barrier((ranked, dz, grad_blocks, sent))
    grad_first = lax.all_to_all(ranked, "mp", 0, 0, tiled=True).reshape(model_size, row_total, D)

    sent = mixer_out_grad = dot_tn(after(act_low, ranked), resid_full).astype(BF)
    at, _, feed_arrived = feed_out_sum.last()
    feed_out_share = wide_gradient(hidden_low, grad_blocks, (at, D), feed_arrived, 512)
    fourth = apply_update(feed_out, feed_out_moment, feed_out_average, feed_out_share.astype(F32))

    in_sum.piece = in_piece(after(dz_then, fourth[3], sent))
    sent = in_sum.send_rest()
    feed_in_share = lax.psum_scatter(feed_in_grad, "dp", scatter_dimension=1, tiled=True)
    feed_in_share = after(feed_in_share, sent)
    third = apply_update(feed_in, feed_in_moment, feed_in_average, feed_in_share.astype(F32))
    *first, gain_one, small = mixer_in_update(
        first_blocks, after(dz, third[3]), small, in_sum.last()[2], mixer_in, mixer_in_moment, mixer_in_average
    )
    sums = jnp.concatenate([gain_one[:1], small[:3]])
    mixer_out_share = lax.psum_scatter(mixer_out_grad, "dp", scatter_dimension=1, tiled=True)
    mixer_out_share = after(mixer_out_share, sums)
    second = apply_update(mixer_out, mixer_out_moment, mixer_out_average, mixer_out_share.astype(F32))
    grad_first = jnp.sum(after(grad_first, sums).astype(F32), axis=0)
    tokens_grad = (grad_resid + norm_back(inputs, inputs_scale, grad_first * gains[0])).astype(BF)
    sums = sums + sum(turn(sums, "mp", k) for k in range(1, model_size))
    sums = after(sums, second[3])
    gains_share = jnp.concatenate([sums[:1] / norm_gains[:1].astype(BF).astype(F32), sums[1:3]])
    loss_value = sums[3, 0] / (total_count * D)
    fifth = apply_update(norm_gains, norm_gains_moment, norm_gains_average, gains_share)
    return (output, tokens_grad, loss_value) + tuple(first) + second + third + fourth + fifth


def solution(mesh):
    tokens = P(("dp", "mp"), None)
    stacked = P(None, "dp", "mp")
    flat = P("mp", "dp")
    gains = P(None, "dp")
    return jax.shard_map(
        per_device,
        mesh=mesh,
        in_specs=(tokens, tokens, P("dp", None), P(), P())
        + (stacked,) * 3 + (flat,) * 3 + (stacked,) * 3 + (flat,) * 3 + (gains,) * 3,
        out_specs=(tokens, tokens, P()) + (stacked,) * 4 + (flat,) * 4 + (stacked,) * 4 + (flat,) * 4 + (gains,) * 4,
        check_vma=False,
    )
```

```python
import functools
import math

import jax
import jax.numpy as jnp
import numpy as np
from jax import lax
from jax.experimental import pallas as pl
from jax.experimental.pallas import tpu as pltpu
from jax.sharding import PartitionSpec as P

D = 2048
HEAD_DIM = 128
BLOCK = 32
CHUNK = 128
LEVELS = 7
TOGETHER = 1
VMEM_LIMIT = 16 * 1024 * 1024

EPS = 1e-06
MOMENT_RATE = 0.5
AVERAGE_RATE = 0.5
LEARN_RATE = 4e-05

BF = jnp.bfloat16
F32 = jnp.float32


def decay_sums():
    t = np.arange(CHUNK)[:, None]
    r = np.arange(CHUNK)[None, :]
    mats = []
    for level in range(LEVELS):
        half = 1 << level
        mid = (t // (2 * half)) * (2 * half) + half
        right = t >= mid
        mats.append(np.where(right, (r >= mid) & (r <= t), (r > t) & (r < mid)))
    mats.append(r <= t)
    mats.append(r > t)
    return np.stack(mats).astype(np.float32)


def dot(a, b):
    return lax.dot_general(a, b, (((1,), (0,)), ((), ())), preferred_element_type=F32)


def dot_nt(a, b):
    return lax.dot_general(a, b, (((1,), (1,)), ((), ())), preferred_element_type=F32)


def dot_tn(a, b):
    return lax.dot_general(a, b, (((0,), (0,)), ((), ())), preferred_element_type=F32)


def sigmoid(v):
    return 1.0 / (1.0 + jnp.exp(-v))


def mean_square(v):
    return jnp.mean(v * v, axis=-1, keepdims=True)


def norm_back(v, scale, weighted):
    return scale * weighted - v * (scale * scale * scale * jnp.mean(weighted * v, axis=-1, keepdims=True))


def forget_parts(z):
    small = jnp.exp(-jnp.abs(z))
    logf = jnp.minimum(z, 0.0) - jnp.log1p(small)
    key = jnp.where(z >= 0.0, small, 1.0) / (1.0 + small)
    return logf, key


def all_decays(sums_ref, pair):
    count = sums_ref.shape[0]
    both = dot(sums_ref[...].reshape(count * CHUNK, CHUNK), pair)
    decays = jnp.exp(both[:, :HEAD_DIM] + both[:, HEAD_DIM:])
    return [decays[i * CHUNK : (i + 1) * CHUNK] for i in range(count)]


def chunk_masks():
    row = lax.broadcasted_iota(jnp.int32, (CHUNK, CHUNK), 0)
    col = lax.broadcasted_iota(jnp.int32, (CHUNK, CHUNK), 1)
    return row, col, row ^ col


class RingRows:
    def __init__(self, rank, ranks, rows):
        self.rank = rank
        self.ranks = ranks
        self.size = rows // ranks
        self.step = math.gcd(CHUNK, self.size)

    def pieces(self, first):
        for at in range(first, first + CHUNK, self.step):
            place = lax.rem(self.rank - at // self.size + self.ranks, self.ranks)
            yield pl.ds(pl.multiple_of(place * self.size + at % self.size, self.step), self.step)

    def load(self, ref, first, lanes, *index):
        return jnp.concatenate([ref[(*index, piece, lanes)] for piece in self.pieces(first)], axis=0)

    def store(self, ref, first, value, lanes, *index):
        for i, piece in enumerate(self.pieces(first)):
            ref[(*index, piece, lanes)] = value[i * self.step : (i + 1) * self.step]


def mixer_forward_kernel(
    ranks, scalar_ref, z_ref, gain_ref, seg_row_ref, seg_col_ref, sums_ref, o_ref, act_ref, square_ref, state_ref, pair_ref
):
    step = pl.program_id(0)
    seqs, _, seq_len = seg_row_ref.shape
    chunks = seq_len // CHUNK
    ring = RingRows(scalar_ref[seqs], ranks, z_ref.shape[1])
    row, col, differ = chunk_masks()
    together = z_ref.shape[2] // HEAD_DIM
    carry = [None] * together
    for seq, c, h in ((s, c, h) for s in range(seqs) for c in range(chunks) for h in range(together)):
        first = seq * seq_len + c * CHUNK
        lanes = pl.ds(h * HEAD_DIM, HEAD_DIM)
        state = carry[h]
        if c == 0:
            state = jnp.zeros((HEAD_DIM, HEAD_DIM), F32)
        z0, z1, value = (ring.load(z_ref, first, lanes, j) for j in range(3))
        query = z0 * sigmoid(z0)
        logf, key = forget_parts(z1)
        high = logf.astype(BF)
        pair = jnp.concatenate([high, (logf - high.astype(F32)).astype(BF)], axis=1)
        decays = all_decays(sums_ref, pair)
        seg_col = seg_col_ref[seq, c * CHUNK : (c + 1) * CHUNK, :]
        seg_row = seg_row_ref[seq, :, c * CHUNK : (c + 1) * CHUNK]
        seg_last = seg_row[:, CHUNK - 1 :]
        value_low = value.astype(BF)
        scores = None
        for level in reversed(range(LEVELS)):
            decay = decays[level]
            right = ((row >> level) & 1) == 1
            mixed = (decay * jnp.where(right, query, key)).astype(BF)
            product = dot_nt(mixed, mixed)
            scores = product if scores is None else jnp.where(differ < (2 << level), product, scores)
        diagonal = jnp.sum(query * key, axis=1, keepdims=True)
        scores = jnp.where(differ == 0, diagonal, scores)
        scores = jnp.where(seg_col == seg_row, scores, 0.0).astype(BF)
        pair_ref[seq, h, c] = scores
        out = dot(jnp.where(row >= col, scores, jnp.zeros_like(scores)), value_low)
        from_start = decays[LEVELS]
        if c > 0:
            carried = seg_col == seg_before
            reach = jnp.where(carried, query * from_start, 0.0).astype(BF)
            out = out + dot_nt(reach, state.astype(BF))
        state_ref[seq, h, c] = state
        position = c * CHUNK + lax.broadcasted_iota(jnp.int32, (CHUNK, 1), 0)
        out = jnp.where(position < scalar_ref[seq] * BLOCK, out, 0.0)
        ring.store(o_ref, first, out, lanes)
        gate = ring.load(z_ref, first, lanes, 3)
        ring.store(act_ref, first, (out * gain_ref[:, lanes] * (gate * sigmoid(gate))).astype(BF), lanes)
        square = jnp.sum(out * out, axis=1, keepdims=True)
        if h == 0:
            square = jnp.where(step == 0, square, ring.load(square_ref, first, slice(None)) + square)
        else:
            square = ring.load(square_ref, first, slice(None)) + square
        ring.store(square_ref, first, square, slice(None))
        if c < chunks - 1:
            to_end = decays[LEVELS + 1]
            tail = jnp.where(seg_col == seg_last, key * to_end, 0.0).astype(BF)
            fresh = dot_tn(value_low, tail)
            if c > 0:
                kept = jnp.where(seg_last == seg_before, from_start[CHUNK - 1 :], 0.0)
                fresh = fresh + state * kept
            carry[h] = fresh
            if h == together - 1:
                seg_before = seg_last


def mixer_backward_kernel(
    ranks, scalar_ref, z_ref, dout_ref, gate_ref, seg_row_ref, seg_col_ref, sums_ref, sums_t_ref, state_ref, pair_ref, dz_ref
):
    seqs, _, seq_len = seg_row_ref.shape
    chunks = seq_len // CHUNK
    ring = RingRows(scalar_ref[seqs], ranks, z_ref.shape[1])
    row, col, differ = chunk_masks()
    dz_ref[3] = gate_ref[...]
    together = z_ref.shape[2] // HEAD_DIM
    carry = [None] * together
    for seq, c, h in ((s, c, h) for s in range(seqs) for c in reversed(range(chunks)) for h in range(together)):
        first = seq * seq_len + c * CHUNK
        lanes = pl.ds(h * HEAD_DIM, HEAD_DIM)
        dstate = carry[h]
        z0, z1, value = (ring.load(z_ref, first, lanes, j) for j in range(3))
        gate0 = sigmoid(z0)
        query = z0 * gate0
        logf, key = forget_parts(z1)
        high = logf.astype(BF)
        pair = jnp.concatenate([high, (logf - high.astype(F32)).astype(BF)], axis=1)
        decays = all_decays(sums_ref, pair)
        seg_col = seg_col_ref[seq, c * CHUNK : (c + 1) * CHUNK, :]
        seg_row = seg_row_ref[seq, :, c * CHUNK : (c + 1) * CHUNK]
        seg_last = seg_row[:, CHUNK - 1 :]
        value_low = value.astype(BF)
        position = c * CHUNK + lax.broadcasted_iota(jnp.int32, (CHUNK, 1), 0)
        dout = jnp.where(position < scalar_ref[seq] * BLOCK, ring.load(dout_ref, first, lanes), 0.0)
        dout_low = dout.astype(BF)

        dscore = jnp.where(row > col, dot_nt(dout_low, value_low), dot_nt(value_low, dout_low))
        dscore = jnp.where(seg_col == seg_row, dscore, 0.0).astype(BF)
        scores = pair_ref[seq, h, c]
        zero = jnp.zeros_like(scores)
        dvalue = dot(jnp.where(col >= row, scores, zero), dout_low)
        diagonal = jnp.sum(dout * value, axis=1, keepdims=True)
        dquery = diagonal * key
        dkey = diagonal * query
        dsums = []
        for level in range(LEVELS):
            decay = decays[level]
            right = ((row >> level) & 1) == 1
            mixed = decay * jnp.where(right, query, key)
            dmixed = dot(jnp.where((differ >> level) == 1, dscore, zero), mixed.astype(BF))
            through = dmixed * decay
            dquery = dquery + jnp.where(right, through, 0.0)
            dkey = dkey + jnp.where(right, 0.0, through)
            dsums.append((dmixed * mixed).astype(BF))
        from_start = decays[LEVELS]
        total = from_start[CHUNK - 1 :]
        if c > 0:
            seg_before = seg_row_ref[seq, :, c * CHUNK - 1 : c * CHUNK]
            carried = seg_col == seg_before
            state = state_ref[seq, h, c]
            reach = jnp.where(carried, query * from_start, 0.0)
            dreach = jnp.where(carried, dot(dout_low, state.astype(BF)), 0.0)
            dquery = dquery + dreach * from_start
            dsums.append((dreach * reach).astype(BF))
            dstate_new = dot_tn(dout_low, reach.astype(BF))
        if c < chunks - 1:
            to_end = decays[LEVELS + 1]
            in_tail = seg_col == seg_last
            tail = jnp.where(in_tail, key * to_end, 0.0)
            dstate_low = dstate.astype(BF)
            dtail = jnp.where(in_tail, dot(value_low, dstate_low), 0.0)
            dkey = dkey + dtail * to_end
            dsums.append((dtail * tail).astype(BF))
            dvalue = dvalue + dot_nt(tail.astype(BF), dstate_low)
            if c > 0:
                kept = jnp.where(seg_last == seg_before, total, 0.0)
                dkept = jnp.sum(state * dstate, axis=0, keepdims=True) * kept
                dstate_new = dstate_new + dstate * kept
        if c > 0:
            carry[h] = dstate_new
        used = LEVELS + int(c > 0)
        sums_t = sums_t_ref[:, : used * CHUNK]
        if c < chunks - 1:
            sums_t = jnp.concatenate([sums_t, sums_t_ref[:, (LEVELS + 1) * CHUNK :]], axis=1)
        dlogf = dot(sums_t, jnp.concatenate(dsums, axis=0))
        if 0 < c < chunks - 1:
            dlogf = dlogf + dkept
        ring.store(dz_ref, first, (dquery * gate0 * (1.0 + z0 * (1.0 - gate0))).astype(BF), lanes, 0)
        ring.store(dz_ref, first, ((dlogf - dkey * (1.0 - key)) * key).astype(BF), lanes, 1)
        ring.store(dz_ref, first, dvalue.astype(BF), lanes, 2)


def mixer_call(kernel, name, operands, kinds, outputs, segments, z, ranks):
    seqs, seq_len = segments.shape
    rows, width = z.shape[1:]
    heads = width // HEAD_DIM
    together = math.gcd(heads, TOGETHER)
    lanes = together * HEAD_DIM
    chunks = seq_len // CHUNK
    matrices = (seqs, heads, chunks, HEAD_DIM, HEAD_DIM)
    shapes = {
        "z": (None, pl.BlockSpec((3, rows, lanes), lambda h: (0, 0, h))),
        "z_all": (None, pl.BlockSpec((4, rows, lanes), lambda h: (0, 0, h))),
        "gain": (None, pl.BlockSpec((1, lanes), lambda h: (0, h))),
        "dz": ((4, rows, width), pl.BlockSpec((4, rows, lanes), lambda h: (0, 0, h))),
        "token": ((rows, width), pl.BlockSpec((rows, lanes), lambda h: (0, h))),
        "column": ((rows, 1), pl.BlockSpec((rows, 1), lambda h: (0, 0))),
        "matrix": (matrices, pl.BlockSpec((seqs, together) + matrices[2:], lambda h: (0, h, 0, 0, 0))),
        "segment_row": (None, pl.BlockSpec((seqs, 1, seq_len), lambda h: (0, 0, 0))),
        "segment_column": (None, pl.BlockSpec((seqs, seq_len, 1), lambda h: (0, 0, 0))),
        "sums": (None, pl.BlockSpec((LEVELS + 2, CHUNK, CHUNK), lambda h: (0, 0, 0))),
        "sums_t": (None, pl.BlockSpec((CHUNK, (LEVELS + 2) * CHUNK), lambda h: (0, 0))),
        "scalar": (None, pl.BlockSpec(memory_space=pltpu.SMEM)),
    }
    return pl.pallas_call(
        functools.partial(kernel, ranks),
        grid=(heads // together,),
        in_specs=[shapes[kind][1] for kind in kinds],
        out_specs=[shapes[kind][1] for kind, _ in outputs],
        out_shape=[jax.ShapeDtypeStruct(shapes[kind][0], dtype) for kind, dtype in outputs],
        compiler_params=pltpu.CompilerParams(vmem_limit_bytes=VMEM_LIMIT),
        name=name,
    )(*operands)


def mixer_forward(z, gain, segments, scalars, ranks):
    sums = jnp.asarray(decay_sums(), BF)
    return mixer_call(
        mixer_forward_kernel,
        "mixer_forward",
        (scalars, z, gain, segments[:, None, :], segments[:, :, None], sums),
        ("scalar", "z_all", "gain", "segment_row", "segment_column", "sums"),
        (("token", F32), ("token", BF), ("column", F32), ("matrix", F32), ("matrix", BF)),
        segments,
        z,
        ranks,
    )


def mixer_backward(z, dout, gate_dz, segments, scalars, states, pairs, ranks):
    sums = decay_sums()
    sums_t = jnp.asarray(sums.reshape(-1, CHUNK).T, BF)
    return mixer_call(
        mixer_backward_kernel,
        "mixer_backward",
        (scalars,)
        + tuple(
            in_hbm(
                z, dout, gate_dz, segments[:, None, :], segments[:, :, None], jnp.asarray(sums, BF), sums_t, states, pairs
            )
        ),
        ("scalar", "z", "token", "token", "segment_row", "segment_column", "sums", "sums_t", "matrix", "matrix"),
        (("dz", BF),),
        segments,
        z,
        ranks,
    )[0]


def in_hbm(*arrays):
    return [pltpu.with_memory_space_constraint(a, pltpu.HBM) for a in arrays]


FREE = pl.CostEstimate(flops=0, bytes_accessed=0, transcendentals=0)


EXTRA = 128
SMALL = 8


def to_columns(small):
    high = small.astype(BF).astype(F32)
    zeros = jnp.zeros((EXTRA - 2 * SMALL, small.shape[1]), F32)
    return jnp.concatenate([high, small - high, zeros], axis=0).T.astype(BF)


def from_columns(columns):
    rows = columns.astype(F32).T
    return rows[:SMALL] + rows[SMALL : 2 * SMALL]


def mixer_gradient_kernel(rows_ref, grads_ref, small_ref, *refs):
    *arrived, out_ref = refs
    rows = rows_ref[...]
    width = grads_ref.shape[2]
    for j in range(grads_ref.shape[0]):
        columns = slice(j * width, (j + 1) * width)
        total = dot_tn(rows, grads_ref[j])
        for ref in arrived:
            total = total + ref[:, columns].astype(F32)
        out_ref[:, columns] = total.astype(BF)
    last = slice(grads_ref.shape[0] * width, out_ref.shape[1])
    small = small_ref[...]
    for ref in arrived:
        small = small + from_columns(ref[:, last])
    out_ref[:, last] = to_columns(small)


def mixer_gradient(rows, span, grads, small, arrived, tile):
    tokens = rows.shape[0]
    count, _, width = grads.shape
    first, last = span
    tile = min(tile, last - first)
    whole = count * width + EXTRA
    return pl.pallas_call(
        mixer_gradient_kernel,
        grid=((last - first) // tile,),
        in_specs=[
            pl.BlockSpec((tokens, tile), lambda i: (0, first // tile + i)),
            pl.BlockSpec((count, tokens, width), lambda i: (0, 0, 0)),
            pl.BlockSpec((SMALL, tile), lambda i: (0, first // tile + i)),
        ]
        + [pl.BlockSpec((tile, whole), lambda i, at=at: (at // tile + i, 0)) for _, at in arrived],
        out_specs=pl.BlockSpec((tile, whole), lambda i: (i, 0)),
        out_shape=jax.ShapeDtypeStruct((last - first, whole), BF),
        compiler_params=pltpu.CompilerParams(vmem_limit_bytes=2 * VMEM_LIMIT),
        cost_estimate=FREE,
        name="mixer_gradient",
    )(rows, grads, small, *[a for a, _ in arrived])


def mixer_in_update_kernel(count, rows_ref, grads_ref, small_ref, *refs):
    arrived, columns = refs[:count], refs[count : 2 * count]
    (master_ref, moment_ref, average_ref, grad_out, master_out, moment_out, average_out, gain_out, small_out) = refs[
        2 * count :
    ]
    total = dot_tn(rows_ref[...], grads_ref[0])
    for ref in arrived:
        total = total + ref[...].astype(F32)
    moment = MOMENT_RATE * moment_ref[0] + total
    master = master_ref[0] - LEARN_RATE * (total + MOMENT_RATE * moment)
    grad_out[0] = total
    moment_out[0] = moment
    master_out[0] = master
    average_out[0] = AVERAGE_RATE * average_ref[0] + (1.0 - AVERAGE_RATE) * master
    product = (master_ref[0].astype(BF).astype(F32) * total).astype(BF)
    gain = dot_nt(jnp.ones((SMALL, product.shape[1]), BF), product)
    gain_out[...] = jnp.where(pl.program_id(0) == 0, gain, gain_out[...] + gain)
    small = small_ref[...]
    for ref in columns:
        small = small + from_columns(ref[...])
    small_out[...] = small


def mixer_in_update(rows, grads, small, arrived, master, moment, average):
    n = master.shape[1]
    count, tokens, width = grads.shape
    last = rows.shape[1] // n - 1
    weight = pl.BlockSpec((1, n, width), lambda k: (k, 0, 0))
    thin = pl.BlockSpec((SMALL, n), lambda k: (0, 0))
    behind = count * width // EXTRA
    return pl.pallas_call(
        functools.partial(mixer_in_update_kernel, len(arrived)),
        grid=(count,),
        in_specs=[
            pl.BlockSpec((tokens, n), lambda k: (0, last)),
            pl.BlockSpec((1, tokens, width), lambda k: (k, 0, 0)),
            pl.BlockSpec((SMALL, n), lambda k: (0, last)),
        ]
        + [pl.BlockSpec((n, width), lambda k, at=at: (at // n, k)) for _, at in arrived]
        + [pl.BlockSpec((n, EXTRA), lambda k, at=at: (at // n, behind)) for _, at in arrived]
        + [weight] * 3,
        out_specs=[weight] * 4 + [thin] * 2,
        out_shape=[jax.ShapeDtypeStruct(master.shape, F32)] * 4 + [jax.ShapeDtypeStruct((SMALL, n), F32)] * 2,
        compiler_params=pltpu.CompilerParams(vmem_limit_bytes=2 * VMEM_LIMIT),
        name="mixer_in_update",
    )(
        rows,
        grads,
        small,
        *[a for a, _ in arrived],
        *[a for a, _ in arrived],
        *in_hbm(master, moment, average),
    )


def pair_gradient_kernel(rows_ref, first_ref, second_ref, *refs):
    *arrived, out_ref = refs
    rows = rows_ref[...]
    for j, side in enumerate((first_ref, second_ref)):
        total = dot_tn(rows, side[...])
        for ref in arrived:
            total = total + ref[j].astype(F32)
        out_ref[j] = total.astype(BF)


def pair_gradient(rows, span, first_side, second_side, arrived, tile):
    tokens = rows.shape[0]
    width = first_side.shape[1]
    first, last = span
    tile = min(tile, last - first)
    side = pl.BlockSpec((tokens, width), lambda i: (0, 0))
    return pl.pallas_call(
        pair_gradient_kernel,
        grid=((last - first) // tile,),
        in_specs=[pl.BlockSpec((tokens, tile), lambda i: (0, first // tile + i)), side, side]
        + [pl.BlockSpec((2, tile, width), lambda i, at=at: (0, at // tile + i, 0)) for _, at in arrived],
        out_specs=pl.BlockSpec((2, tile, width), lambda i: (0, i, 0)),
        out_shape=jax.ShapeDtypeStruct((2, last - first, width), BF),
        compiler_params=pltpu.CompilerParams(vmem_limit_bytes=2 * VMEM_LIMIT),
        cost_estimate=FREE,
        name="pair_gradient",
    )(rows, first_side, second_side, *[a for a, _ in arrived])


def wide_gradient_kernel(left_ref, right_ref, *refs):
    *arrived, out_ref = refs
    total = dot_tn(left_ref[...], right_ref[...])
    for ref in arrived:
        total = total + ref[...].astype(F32)
    out_ref[...] = total.astype(BF)


def wide_gradient(left, right, span, arrived, tile):
    tokens, n = left.shape
    first, last = span
    tile = min(tile, last - first)
    return pl.pallas_call(
        wide_gradient_kernel,
        grid=((last - first) // tile,),
        in_specs=[
            pl.BlockSpec((tokens, n), lambda i: (0, 0)),
            pl.BlockSpec((tokens, tile), lambda i: (0, first // tile + i)),
        ]
        + [pl.BlockSpec((n, tile), lambda i, at=at: (0, at // tile + i)) for _, at in arrived],
        out_specs=pl.BlockSpec((n, tile), lambda i: (0, i)),
        out_shape=jax.ShapeDtypeStruct((n, last - first), BF),
        compiler_params=pltpu.CompilerParams(vmem_limit_bytes=VMEM_LIMIT),
        cost_estimate=FREE,
        name="wide_gradient",
    )(*in_hbm(left, right, *[a for a, _ in arrived]))


def split_column(v):
    high = v.astype(BF)
    return high, (v - high.astype(F32)).astype(BF)


def after_mixer_kernel(count, own_ref, square_ref, tokens_ref, gain_ref, *refs):
    arrived = refs[:count]
    resid_ref, scale_ref, norm_ref = refs[count:]
    mixed = own_ref[...].astype(F32)
    square = square_ref[...]
    for ref in arrived:
        mixed = mixed + ref[:, :D].astype(F32)
        square = square + ref[:, D : D + 1].astype(F32) + ref[:, D + 1 : D + 2].astype(F32)
    scale = lax.rsqrt(square / D + EPS)
    resid = tokens_ref[...].astype(F32) + mixed * scale
    resid_ref[...] = resid
    scale_ref[...] = scale
    norm_ref[...] = (resid * lax.rsqrt(mean_square(resid) + EPS) * gain_ref[...]).astype(BF)


def after_mixer(parts, square, tokens, gain, arrived):
    rows = tokens.shape[0]
    whole = pl.BlockSpec((rows, D), lambda i: (0, 0))
    column = pl.BlockSpec((rows, 1), lambda i: (0, 0))
    return pl.pallas_call(
        functools.partial(after_mixer_kernel, len(arrived)),
        grid=(1,),
        in_specs=[whole, column, whole, pl.BlockSpec((1, D), lambda i: (0, 0))]
        + [pl.BlockSpec((rows, D + EXTRA), lambda i: (0, 0))] * len(arrived),
        out_specs=[whole, column, whole],
        out_shape=[
            jax.ShapeDtypeStruct((rows, D), F32),
            jax.ShapeDtypeStruct((rows, 1), F32),
            jax.ShapeDtypeStruct((rows, D), BF),
        ],
        compiler_params=pltpu.CompilerParams(vmem_limit_bytes=VMEM_LIMIT),
        name="after_mixer",
    )(parts, square, *in_hbm(tokens), gain, *arrived)


def after_feed_kernel(count, own_ref, resid_ref, tokens_ref, final_ref, gain_ref, scale_ref, *refs):
    arrived = refs[:count]
    grad_ref, payload_ref = refs[count:]
    grad = own_ref[...].astype(F32)
    for ref in arrived:
        grad = grad + ref[...].astype(F32)
    resid = resid_ref[...]
    grad = final_ref[...] + norm_back(resid, lax.rsqrt(mean_square(resid) + EPS), grad * gain_ref[...])
    grad_ref[...] = grad
    low = grad.astype(BF)
    payload_ref[:, :D] = low
    scale = scale_ref[...]
    mixed = resid - tokens_ref[...].astype(F32)
    coef = scale * scale * jnp.mean(low.astype(F32) * mixed, axis=-1, keepdims=True)
    columns = [part for v in (scale, coef) for part in split_column(v)]
    lane = lax.broadcasted_iota(jnp.int32, (low.shape[0], EXTRA), 1)
    extra = jnp.zeros((low.shape[0], EXTRA), F32)
    for i, part in enumerate(columns):
        extra = jnp.where(lane == i, part.astype(F32), extra)
    payload_ref[:, D:] = extra.astype(BF)


def after_feed(parts, resid, tokens, final, gain, scale, arrived):
    rows = tokens.shape[0]
    whole = pl.BlockSpec((rows, D), lambda i: (0, 0))
    column = pl.BlockSpec((rows, 1), lambda i: (0, 0))
    return pl.pallas_call(
        functools.partial(after_feed_kernel, len(arrived)),
        grid=(1,),
        in_specs=[whole] * 4 + [pl.BlockSpec((1, D), lambda i: (0, 0)), column] + [whole] * len(arrived),
        out_specs=[whole, pl.BlockSpec((rows, D + EXTRA), lambda i: (0, 0))],
        out_shape=[jax.ShapeDtypeStruct((rows, D), F32), jax.ShapeDtypeStruct((rows, D + EXTRA), BF)],
        compiler_params=pltpu.CompilerParams(vmem_limit_bytes=VMEM_LIMIT),
        name="after_feed",
    )(parts, *in_hbm(resid, tokens, final), gain, scale, *arrived)


def column_sums_kernel(left_ref, right_ref, out_ref):
    product = left_ref[...].astype(F32) * right_ref[...].astype(F32)
    out_ref[...] = jnp.sum(product, axis=0, keepdims=True)


def column_sums(left, right):
    rows, width = left.shape
    tile = width // 4
    block = pl.BlockSpec((rows, tile), lambda i: (0, i))
    return pl.pallas_call(
        column_sums_kernel,
        grid=(4,),
        in_specs=[block, block],
        out_specs=pl.BlockSpec((1, tile), lambda i: (0, i)),
        out_shape=jax.ShapeDtypeStruct((1, width), F32),
        compiler_params=pltpu.CompilerParams(vmem_limit_bytes=VMEM_LIMIT),
        cost_estimate=FREE,
        name="column_sums",
    )(left, right)[0]


def project_back_kernel(grads_ref, weight_ref, out_ref):
    total = dot_nt(grads_ref[0], weight_ref[0])
    for j in range(1, grads_ref.shape[0]):
        total = total + dot_nt(grads_ref[j], weight_ref[j])
    out_ref[...] = total.astype(BF)


def project_back(grads, weight, tile):
    count, rows, width = grads.shape
    n = weight.shape[1]
    return pl.pallas_call(
        project_back_kernel,
        grid=(n // tile,),
        in_specs=[
            pl.BlockSpec((count, rows, width), lambda i: (0, 0, 0)),
            pl.BlockSpec((count, tile, width), lambda i: (0, i, 0)),
        ],
        out_specs=pl.BlockSpec((rows, tile), lambda i: (0, i)),
        out_shape=jax.ShapeDtypeStruct((rows, n), BF),
        compiler_params=pltpu.CompilerParams(vmem_limit_bytes=VMEM_LIMIT),
        cost_estimate=pl.CostEstimate(flops=0, bytes_accessed=100_000_000, transcendentals=0),
        name="project_back",
    )(grads, *in_hbm(weight))


def take_blocks_kernel(order_ref, in_ref, out_ref):
    out_ref[...] = in_ref[...]


def take_blocks(v, order):
    rows, width = v.shape[0], D
    count = order.shape[0]
    block = (rows, width // count)
    return pl.pallas_call(
        take_blocks_kernel,
        grid_spec=pltpu.PrefetchScalarGridSpec(
            num_scalar_prefetch=1,
            grid=(count,),
            in_specs=[pl.BlockSpec(block, lambda i, order: (0, order[i]))],
            out_specs=pl.BlockSpec(block, lambda i, order: (0, i)),
        ),
        out_shape=jax.ShapeDtypeStruct((rows, width), v.dtype),
        compiler_params=pltpu.CompilerParams(vmem_limit_bytes=VMEM_LIMIT),
        cost_estimate=FREE,
        name="take_blocks",
    )(order, v)


def mixer_out_update_kernel(count, act_ref, rows_ref, *refs):
    arrived = refs[:count]
    master_ref, moment_ref, average_ref, grad_out, master_out, moment_out, average_out = refs[count:]
    total = arrived[0][...].astype(F32)
    for ref in arrived[1:]:
        total = total + ref[...].astype(F32)
    total = dot_tn(act_ref[...], rows_ref[...]) + total.T
    moment = MOMENT_RATE * moment_ref[...] + total
    master = master_ref[...] - LEARN_RATE * (total + MOMENT_RATE * moment)
    grad_out[...] = total
    moment_out[...] = moment
    master_out[...] = master
    average_out[...] = AVERAGE_RATE * average_ref[...] + (1.0 - AVERAGE_RATE) * master


def mixer_out_update(act, rows, arrived, master, moment, average):
    n = master.shape[1]
    tokens, width = act.shape
    last = rows.shape[1] // n - 1
    whole = pl.BlockSpec((width, n), lambda i: (0, 0))
    return pl.pallas_call(
        functools.partial(mixer_out_update_kernel, len(arrived)),
        grid=(1,),
        in_specs=[pl.BlockSpec((tokens, width), lambda i: (0, 0)), pl.BlockSpec((tokens, n), lambda i: (0, last))]
        + [pl.BlockSpec((n, width), lambda i, at=at: (at // n, 0)) for _, at in arrived]
        + [whole] * 3,
        out_specs=[whole] * 4,
        out_shape=[jax.ShapeDtypeStruct(master.shape, F32)] * 4,
        compiler_params=pltpu.CompilerParams(vmem_limit_bytes=VMEM_LIMIT),
        name="mixer_out_update",
    )(act, rows, *[a for a, _ in arrived], *in_hbm(master, moment, average))


def turn(v, axis, step):
    n = lax.axis_size(axis)
    return lax.ppermute(v, axis, [(i, (i + step) % n) for i in range(n)])


def swap(v, axis, bit):
    n = lax.axis_size(axis)
    return lax.ppermute(v, axis, [(i, i ^ bit) for i in range(n)])


def gather_near(v, axis):
    n = lax.axis_size(axis)
    return jnp.concatenate([v] + [turn(v, axis, k) for k in range(1, n)], axis=0)


def scatter_near(v, axis):
    n = lax.axis_size(axis)
    rows = v.shape[0] // n
    total = v[:rows].astype(F32)
    for k in range(1, n):
        total = total + turn(v[k * rows : (k + 1) * rows], axis, -k).astype(F32)
    return total


def gather_gains(v):
    bit = 1
    me = lax.axis_index("dp")
    while bit < lax.axis_size("dp"):
        other = swap(v, "dp", bit)
        upper = (me & bit) > 0
        v = jnp.concatenate([jnp.where(upper, other, v), jnp.where(upper, v, other)], axis=1)
        bit *= 2
    return v


def apply_update(master, moment, average, gradient):
    moment_new = MOMENT_RATE * moment + gradient
    master_new = master - LEARN_RATE * (gradient + MOMENT_RATE * moment_new)
    average_new = AVERAGE_RATE * average + (1.0 - AVERAGE_RATE) * master_new
    return (gradient, master_new, moment_new, average_new)


def gather_weight(w, dim):
    return lax.all_gather(w.astype(BF), "dp", axis=dim, tiled=True)


def link_bits():
    bits = []
    bit = 2
    while bit < lax.axis_size("dp"):
        bits.append(bit)
        bit *= 2
    return bits, bits[::-1]


def block_order(bits):
    if not bits:
        return [0]
    rest = block_order(bits[1:])
    return [bits[0] ^ r for r in rest] + rest


def exchange_order(me):
    even, odd = (block_order(bits) for bits in link_bits())
    order_even = [1 ^ r for r in odd] + even
    order_odd = [1 ^ r for r in even] + odd
    return me ^ jnp.where((me & 1) == 0, jnp.array(order_even, jnp.int32), jnp.array(order_odd, jnp.int32))


def cross_swap(v, stage):
    even, odd = link_bits()
    n = lax.axis_size("dp")
    return lax.ppermute(v, "dp", [(i, i ^ (odd if i & 1 else even)[stage]) for i in range(n)])


def after(v, *others):
    return lax.optimization_barrier((v,) + others)[0]


class GradientSum:
    def __init__(self, piece):
        self.piece = piece
        self.at = 0
        self.left = D
        self.received = []

    def arrived(self):
        return [(r, self.at - first) for r, first in self.received]

    def send(self):
        self.left //= 2
        give = self.piece(self.at, self.at + self.left, self.arrived())
        stage = len(self.received) - 1
        self.at += self.left
        self.received.append((swap(give, "dp", 1) if stage < 0 else cross_swap(give, stage), self.at))
        return give

    def send_rest(self):
        while self.left > D // lax.axis_size("dp"):
            give = self.send()
        return give

    def last(self):
        return self.at, D, self.arrived()


def two_parts(v):
    high = lax.reduce_precision(v, 8, 7)
    return [high.astype(BF), (v - high).astype(BF)]


def pack_columns(values):
    parts = jnp.stack([part for v in values for part in two_parts(v)], axis=1)
    return jnp.pad(parts, ((0, 0), (0, EXTRA - parts.shape[1])))


def unpack_columns(v, count):
    return [v[:, 2 * i].astype(F32) + v[:, 2 * i + 1].astype(F32) for i in range(count)]


def gather_block_weight(w, dim):
    me = lax.axis_index("dp")
    core = me & 1
    even, odd = (block_order(bits) for bits in link_bits())
    order_even = [1 ^ r for r in odd] + even
    order_odd = [1 ^ r for r in even] + odd
    v = w.astype(BF)
    width = v.shape[dim]
    for stage in reversed(range(len(link_bits()[0]))):
        v = jnp.concatenate([cross_swap(v, stage), v], axis=dim)
    parts = [swap(v, "dp", 1), v]
    shape = list(v.shape)
    shape[dim] *= 2
    whole = jnp.zeros(shape, BF)
    for i, (a, b) in enumerate(zip(order_even, order_odd)):
        part = parts[i * 2 // len(order_even)]
        at = i % (len(order_even) // 2) * width
        block = lax.slice_in_dim(part, at, at + width, axis=dim)
        whole = lax.dynamic_update_slice_in_dim(whole, block, (me ^ jnp.where(core == 0, a, b)) * width, dim)
    return whole


def per_device(
    tokens,
    teacher,
    segments,
    block_counts,
    loss_mask,
    mixer_in,
    mixer_in_moment,
    mixer_in_average,
    mixer_out,
    mixer_out_moment,
    mixer_out_average,
    feed_in,
    feed_in_moment,
    feed_in_average,
    feed_out,
    feed_out_moment,
    feed_out_average,
    norm_gains,
    norm_gains_moment,
    norm_gains_average,
):
    mixer_in_work = gather_weight(mixer_in, 1)
    mixer_out_work = gather_block_weight(mixer_out, 1)
    feed_in_work = gather_weight(feed_in, 1)
    feed_out_work = gather_weight(feed_out, 1)
    gains = gather_gains(norm_gains.astype(BF)).astype(F32)

    row_total = tokens.shape[0]
    seq_here, seq_len = segments.shape
    seq_all = block_counts.shape[0]
    data_rank = lax.axis_index("dp")
    model_rank = lax.axis_index("mp")
    model_size = lax.axis_size("mp")
    local_counts = lax.dynamic_slice_in_dim(block_counts, data_rank * seq_here, seq_here, 0)
    order = exchange_order(data_rank.astype(jnp.int32))
    scalars = jnp.concatenate([local_counts, model_rank[None].astype(jnp.int32)])
    column = jnp.arange(seq_len, dtype=jnp.int32)
    live_all = (column[None, :] < BLOCK * block_counts[:, None]).astype(F32)
    total_count = jnp.sum(loss_mask.reshape(seq_all, seq_len).astype(F32) * live_all)
    first_row = (data_rank * model_size + model_rank) * row_total
    valid = lax.dynamic_slice_in_dim(loss_mask.astype(F32) * live_all.reshape(-1), first_row, row_total, 0)

    inputs = tokens.astype(F32)
    inputs_scale = lax.rsqrt(mean_square(inputs) + EPS)
    tokens_full = gather_near(tokens, "mp").astype(F32)
    first_full = (tokens_full * lax.rsqrt(mean_square(tokens_full) + EPS) * gains[0]).astype(BF)
    z = jnp.einsum("td,jde->jte", first_full, mixer_in_work, preferred_element_type=F32)
    gate_z = z[3]
    local_width = z.shape[2]
    gain_out = lax.dynamic_slice_in_dim(gains[2], model_rank * local_width, local_width, 0)[None]
    recurrent, act_raw, square, states, pairs = mixer_forward(z, gain_out, segments, scalars, model_size)
    gate_z_sig = jax.nn.sigmoid(gate_z)
    gate_z_act = gate_z * gate_z_sig
    mixed_parts = dot(act_raw, mixer_out_work).astype(BF)
    arrived = []
    for k in range(1, model_size):
        rows = slice(k * row_total, (k + 1) * row_total)
        payload = jnp.concatenate([mixed_parts[rows], pack_columns([square[rows, 0]])], axis=1)
        arrived.append(turn(payload, "mp", -k))
    first_blocks = take_blocks(first_full, order)
    *arrived, first_blocks = lax.optimization_barrier((*arrived, first_blocks))
    resid, out_scale_here, norm_second = after_mixer(mixed_parts, square, tokens, gains[1:2], arrived)

    second_full = gather_near(norm_second, "mp")
    gate_up = jnp.einsum("td,jdf->jtf", second_full, feed_in_work, preferred_element_type=F32)
    gate_sig = jax.nn.sigmoid(gate_up[0])
    gate_act = gate_up[0] * gate_sig
    hidden_low = (gate_act * gate_up[1]).astype(BF)
    final = resid + scatter_near(dot(hidden_low, feed_out_work).astype(BF), "mp")
    output = final.astype(BF)

    error = (final - teacher.astype(F32)) * valid[:, None]
    square_sum = jnp.sum(error * error)
    token_slots = row_total * lax.axis_size("dp") * model_size
    grad_final = token_slots / total_count * error

    grad_full = gather_near(grad_final.astype(BF), "mp")
    grad_hidden = dot_nt(grad_full, feed_out_work)
    grad_gate = (grad_hidden * gate_up[1] * gate_sig * (1.0 + gate_up[0] * (1.0 - gate_sig))).astype(BF)
    grad_up = (grad_hidden * gate_act).astype(BF)
    grad_second_parts = (dot_nt(grad_gate, feed_in_work[0]) + dot_nt(grad_up, feed_in_work[1])).astype(BF)
    parts = [grad_second_parts[k * row_total : (k + 1) * row_total] for k in range(1, model_size)]
    *parts, grad_late = lax.optimization_barrier((*parts, grad_full))
    arrived = [turn(part, "mp", -k) for k, part in enumerate(parts, 1)]
    grad_blocks = take_blocks(grad_late, order)
    feed_out_sum = GradientSum(
        lambda a, b, arrived: wide_gradient(hidden_low, grad_blocks, (a, b), arrived, 512)
    )
    sent = feed_out_sum.send()
    feed_in_grad = pair_gradient(second_full, (0, D), grad_gate, after(grad_up, sent), [], 256)
    gain_two_grad = column_sums(grad_second_parts, after(second_full, feed_in_grad)) / gains[1]
    sent = feed_out_sum.send()
    *arrived, feed_in_grad, gain_two_grad, _ = lax.optimization_barrier((*arrived, feed_in_grad, gain_two_grad, sent))
    grad_resid, payload = after_feed(
        grad_second_parts, resid, tokens, grad_final, gains[1:2], out_scale_here, arrived
    )

    pieces = [payload] + [turn(payload, "mp", k) for k in range(1, model_size)]
    *pieces, _ = lax.optimization_barrier((*pieces, feed_out_sum.send_rest()))
    payload = jnp.concatenate(pieces, axis=0)
    resid_full = payload[:, :D]
    out_scale, coef = (v[:, None] for v in unpack_columns(payload[:, D:], 2))
    grad_act = dot_nt(resid_full, mixer_out_work)
    act_low = (act_raw.astype(F32) * out_scale).astype(BF)
    normed = recurrent * out_scale
    gate_dz = (grad_act * normed * gain_out * gate_z_sig * (1.0 + gate_z * (1.0 - gate_z_sig))).astype(BF)
    grad_normed = grad_act * gate_z_act
    gain_out_grad = jnp.sum(grad_normed * normed, axis=0)
    grad_recurrent = out_scale * (grad_normed * gain_out) - recurrent * coef

    gain_out_full = lax.dynamic_update_slice_in_dim(
        jnp.zeros((D,), F32), gain_out_grad, model_rank * local_width, 0
    )
    zero = jnp.zeros((D,), F32)
    small = jnp.stack([gain_two_grad, gain_out_full, jnp.full((D,), square_sum)] + [zero] * (SMALL - 3))
    small = take_blocks(small, order)
    dz = mixer_backward(z, grad_recurrent, gate_dz, segments, scalars, states, pairs, model_size)

    in_sum = GradientSum(None)

    def in_piece(dz_then):
        return lambda a, b, arrived: mixer_gradient(first_blocks, (a, b), dz_then, small, arrived, 256)

    in_sum.piece = in_piece(dz)
    sent = in_sum.send()
    grad_first_parts = project_back(after(dz, sent), mixer_in_work, 512)
    in_sum.piece = in_piece(after(dz, grad_first_parts))
    sent = in_sum.send()
    ranked = jnp.concatenate(
        [
            lax.dynamic_slice_in_dim(grad_first_parts, (model_rank - r) % model_size * row_total, row_total, 0)
            for r in range(model_size)
        ]
    )
    ranked, dz_then, grad_blocks, _ = lax.optimization_barrier((ranked, dz, grad_blocks, sent))
    grad_first = lax.all_to_all(ranked, "mp", 0, 0, tiled=True).reshape(model_size, row_total, D)

    sent = mixer_out_grad = dot_tn(after(act_low, ranked), resid_full).astype(BF)
    at, _, feed_arrived = feed_out_sum.last()
    feed_out_share = wide_gradient(hidden_low, grad_blocks, (at, D), feed_arrived, 512)
    fourth = apply_update(feed_out, feed_out_moment, feed_out_average, feed_out_share.astype(F32))

    in_sum.piece = in_piece(after(dz_then, fourth[3], sent))
    sent = in_sum.send_rest()
    feed_in_share = lax.psum_scatter(feed_in_grad, "dp", scatter_dimension=1, tiled=True)
    feed_in_share = after(feed_in_share, sent)
    third = apply_update(feed_in, feed_in_moment, feed_in_average, feed_in_share.astype(F32))
    *first, gain_one, small = mixer_in_update(
        first_blocks, after(dz, third[3]), small, in_sum.last()[2], mixer_in, mixer_in_moment, mixer_in_average
    )
    sums = jnp.concatenate([gain_one[:1], small[:3]])
    mixer_out_share = lax.psum_scatter(mixer_out_grad, "dp", scatter_dimension=1, tiled=True)
    mixer_out_share = after(mixer_out_share, sums)
    second = apply_update(mixer_out, mixer_out_moment, mixer_out_average, mixer_out_share.astype(F32))
    grad_first = jnp.sum(after(grad_first, sums).astype(F32), axis=0)
    tokens_grad = (grad_resid + norm_back(inputs, inputs_scale, grad_first * gains[0])).astype(BF)
    sums = sums + sum(turn(sums, "mp", k) for k in range(1, model_size))
    sums = after(sums, second[3])
    gains_share = jnp.concatenate([sums[:1] / norm_gains[:1].astype(BF).astype(F32), sums[1:3]])
    loss_value = sums[3, 0] / (total_count * D)
    fifth = apply_update(norm_gains, norm_gains_moment, norm_gains_average, gains_share)
    return (output, tokens_grad, loss_value) + tuple(first) + second + third + fourth + fifth


def solution(mesh):
    tokens = P(("dp", "mp"), None)
    stacked = P(None, "dp", "mp")
    flat = P("mp", "dp")
    gains = P(None, "dp")
    return jax.shard_map(
        per_device,
        mesh=mesh,
        in_specs=(tokens, tokens, P("dp", None), P(), P())
        + (stacked,) * 3 + (flat,) * 3 + (stacked,) * 3 + (flat,) * 3 + (gains,) * 3,
        out_specs=(tokens, tokens, P()) + (stacked,) * 4 + (flat,) * 4 + (stacked,) * 4 + (flat,) * 4 + (gains,) * 4,
        check_vma=False,
    )
```

```python
import functools
import math

import jax
import jax.numpy as jnp
import numpy as np
from jax import lax
from jax.experimental import pallas as pl
from jax.experimental.pallas import tpu as pltpu
from jax.sharding import PartitionSpec as P

D = 2048
HEAD_DIM = 128
BLOCK = 32
CHUNK = 128
LEVELS = 7
TOGETHER = 2
VMEM_LIMIT = 16 * 1024 * 1024

EPS = 1e-06
MOMENT_RATE = 0.5
AVERAGE_RATE = 0.5
LEARN_RATE = 4e-05

BF = jnp.bfloat16
F32 = jnp.float32


def decay_sums():
    t = np.arange(CHUNK)[:, None]
    r = np.arange(CHUNK)[None, :]
    mats = []
    for level in range(LEVELS):
        half = 1 << level
        mid = (t // (2 * half)) * (2 * half) + half
        right = t >= mid
        mats.append(np.where(right, (r >= mid) & (r <= t), (r > t) & (r < mid)))
    mats.append(r <= t)
    mats.append(r > t)
    return np.stack(mats).astype(np.float32)


def dot(a, b):
    return lax.dot_general(a, b, (((1,), (0,)), ((), ())), preferred_element_type=F32)


def dot_nt(a, b):
    return lax.dot_general(a, b, (((1,), (1,)), ((), ())), preferred_element_type=F32)


def dot_tn(a, b):
    return lax.dot_general(a, b, (((0,), (0,)), ((), ())), preferred_element_type=F32)


def sigmoid(v):
    return 1.0 / (1.0 + jnp.exp(-v))


def mean_square(v):
    return jnp.mean(v * v, axis=-1, keepdims=True)


def norm_back(v, scale, weighted):
    return scale * weighted - v * (scale * scale * scale * jnp.mean(weighted * v, axis=-1, keepdims=True))


def forget_parts(z):
    small = jnp.exp(-jnp.abs(z))
    logf = jnp.minimum(z, 0.0) - jnp.log1p(small)
    key = jnp.where(z >= 0.0, small, 1.0) / (1.0 + small)
    return logf, key


def all_decays(sums_ref, pair):
    count = sums_ref.shape[0]
    both = dot(sums_ref[...].reshape(count * CHUNK, CHUNK), pair)
    decays = jnp.exp(both[:, :HEAD_DIM] + both[:, HEAD_DIM:])
    return [decays[i * CHUNK : (i + 1) * CHUNK] for i in range(count)]


def chunk_masks():
    row = lax.broadcasted_iota(jnp.int32, (CHUNK, CHUNK), 0)
    col = lax.broadcasted_iota(jnp.int32, (CHUNK, CHUNK), 1)
    return row, col, row ^ col


class RingRows:
    def __init__(self, rank, ranks, rows):
        self.rank = rank
        self.ranks = ranks
        self.size = rows // ranks
        self.step = math.gcd(CHUNK, self.size)

    def pieces(self, first):
        for at in range(first, first + CHUNK, self.step):
            place = lax.rem(self.rank - at // self.size + self.ranks, self.ranks)
            yield pl.ds(pl.multiple_of(place * self.size + at % self.size, self.step), self.step)

    def load(self, ref, first, lanes, *index):
        return jnp.concatenate([ref[(*index, piece, lanes)] for piece in self.pieces(first)], axis=0)

    def store(self, ref, first, value, lanes, *index):
        for i, piece in enumerate(self.pieces(first)):
            ref[(*index, piece, lanes)] = value[i * self.step : (i + 1) * self.step]


def mixer_forward_kernel(
    ranks, scalar_ref, z_ref, gain_ref, seg_row_ref, seg_col_ref, sums_ref, o_ref, act_ref, square_ref, state_ref, pair_ref
):
    step = pl.program_id(0)
    seqs, _, seq_len = seg_row_ref.shape
    chunks = seq_len // CHUNK
    ring = RingRows(scalar_ref[seqs], ranks, z_ref.shape[1])
    row, col, differ = chunk_masks()
    together = z_ref.shape[2] // HEAD_DIM
    carry = [None] * together
    for seq, c, h in ((s, c, h) for s in range(seqs) for c in range(chunks) for h in range(together)):
        first = seq * seq_len + c * CHUNK
        lanes = pl.ds(h * HEAD_DIM, HEAD_DIM)
        state = carry[h]
        if c == 0:
            state = jnp.zeros((HEAD_DIM, HEAD_DIM), F32)
        z0, z1, value = (ring.load(z_ref, first, lanes, j) for j in range(3))
        query = z0 * sigmoid(z0)
        logf, key = forget_parts(z1)
        high = logf.astype(BF)
        pair = jnp.concatenate([high, (logf - high.astype(F32)).astype(BF)], axis=1)
        decays = all_decays(sums_ref, pair)
        seg_col = seg_col_ref[seq, c * CHUNK : (c + 1) * CHUNK, :]
        seg_row = seg_row_ref[seq, :, c * CHUNK : (c + 1) * CHUNK]
        seg_last = seg_row[:, CHUNK - 1 :]
        value_low = value.astype(BF)
        scores = None
        for level in reversed(range(LEVELS)):
            decay = decays[level]
            right = ((row >> level) & 1) == 1
            mixed = (decay * jnp.where(right, query, key)).astype(BF)
            product = dot_nt(mixed, mixed)
            scores = product if scores is None else jnp.where(differ < (2 << level), product, scores)
        diagonal = jnp.sum(query * key, axis=1, keepdims=True)
        scores = jnp.where(differ == 0, diagonal, scores)
        scores = jnp.where(seg_col == seg_row, scores, 0.0).astype(BF)
        pair_ref[seq, h, c] = scores
        out = dot(jnp.where(row >= col, scores, jnp.zeros_like(scores)), value_low)
        from_start = decays[LEVELS]
        if c > 0:
            carried = seg_col == seg_before
            reach = jnp.where(carried, query * from_start, 0.0).astype(BF)
            out = out + dot_nt(reach, state.astype(BF))
        state_ref[seq, h, c] = state
        position = c * CHUNK + lax.broadcasted_iota(jnp.int32, (CHUNK, 1), 0)
        out = jnp.where(position < scalar_ref[seq] * BLOCK, out, 0.0)
        ring.store(o_ref, first, out, lanes)
        gate = ring.load(z_ref, first, lanes, 3)
        ring.store(act_ref, first, (out * gain_ref[:, lanes] * (gate * sigmoid(gate))).astype(BF), lanes)
        square = jnp.sum(out * out, axis=1, keepdims=True)
        if h == 0:
            square = jnp.where(step == 0, square, ring.load(square_ref, first, slice(None)) + square)
        else:
            square = ring.load(square_ref, first, slice(None)) + square
        ring.store(square_ref, first, square, slice(None))
        if c < chunks - 1:
            to_end = decays[LEVELS + 1]
            tail = jnp.where(seg_col == seg_last, key * to_end, 0.0).astype(BF)
            fresh = dot_tn(value_low, tail)
            if c > 0:
                kept = jnp.where(seg_last == seg_before, from_start[CHUNK - 1 :], 0.0)
                fresh = fresh + state * kept
            carry[h] = fresh
            if h == together - 1:
                seg_before = seg_last


def mixer_backward_kernel(
    ranks, scalar_ref, z_ref, dout_ref, gate_ref, seg_row_ref, seg_col_ref, sums_ref, sums_t_ref, state_ref, pair_ref, dz_ref
):
    seqs, _, seq_len = seg_row_ref.shape
    chunks = seq_len // CHUNK
    ring = RingRows(scalar_ref[seqs], ranks, z_ref.shape[1])
    row, col, differ = chunk_masks()
    dz_ref[3] = gate_ref[...]
    together = z_ref.shape[2] // HEAD_DIM
    carry = [None] * together
    for seq, c, h in ((s, c, h) for s in range(seqs) for c in reversed(range(chunks)) for h in range(together)):
        first = seq * seq_len + c * CHUNK
        lanes = pl.ds(h * HEAD_DIM, HEAD_DIM)
        dstate = carry[h]
        z0, z1, value = (ring.load(z_ref, first, lanes, j) for j in range(3))
        gate0 = sigmoid(z0)
        query = z0 * gate0
        logf, key = forget_parts(z1)
        high = logf.astype(BF)
        pair = jnp.concatenate([high, (logf - high.astype(F32)).astype(BF)], axis=1)
        decays = all_decays(sums_ref, pair)
        seg_col = seg_col_ref[seq, c * CHUNK : (c + 1) * CHUNK, :]
        seg_row = seg_row_ref[seq, :, c * CHUNK : (c + 1) * CHUNK]
        seg_last = seg_row[:, CHUNK - 1 :]
        value_low = value.astype(BF)
        position = c * CHUNK + lax.broadcasted_iota(jnp.int32, (CHUNK, 1), 0)
        dout = jnp.where(position < scalar_ref[seq] * BLOCK, ring.load(dout_ref, first, lanes), 0.0)
        dout_low = dout.astype(BF)

        dscore = jnp.where(row > col, dot_nt(dout_low, value_low), dot_nt(value_low, dout_low))
        dscore = jnp.where(seg_col == seg_row, dscore, 0.0).astype(BF)
        scores = pair_ref[seq, h, c]
        zero = jnp.zeros_like(scores)
        dvalue = dot(jnp.where(col >= row, scores, zero), dout_low)
        diagonal = jnp.sum(dout * value, axis=1, keepdims=True)
        dquery = diagonal * key
        dkey = diagonal * query
        dsums = []
        for level in range(LEVELS):
            decay = decays[level]
            right = ((row >> level) & 1) == 1
            mixed = decay * jnp.where(right, query, key)
            dmixed = dot(jnp.where((differ >> level) == 1, dscore, zero), mixed.astype(BF))
            through = dmixed * decay
            dquery = dquery + jnp.where(right, through, 0.0)
            dkey = dkey + jnp.where(right, 0.0, through)
            dsums.append((dmixed * mixed).astype(BF))
        from_start = decays[LEVELS]
        total = from_start[CHUNK - 1 :]
        if c > 0:
            seg_before = seg_row_ref[seq, :, c * CHUNK - 1 : c * CHUNK]
            carried = seg_col == seg_before
            state = state_ref[seq, h, c]
            reach = jnp.where(carried, query * from_start, 0.0)
            dreach = jnp.where(carried, dot(dout_low, state.astype(BF)), 0.0)
            dquery = dquery + dreach * from_start
            dsums.append((dreach * reach).astype(BF))
            dstate_new = dot_tn(dout_low, reach.astype(BF))
        if c < chunks - 1:
            to_end = decays[LEVELS + 1]
            in_tail = seg_col == seg_last
            tail = jnp.where(in_tail, key * to_end, 0.0)
            dstate_low = dstate.astype(BF)
            dtail = jnp.where(in_tail, dot(value_low, dstate_low), 0.0)
            dkey = dkey + dtail * to_end
            dsums.append((dtail * tail).astype(BF))
            dvalue = dvalue + dot_nt(tail.astype(BF), dstate_low)
            if c > 0:
                kept = jnp.where(seg_last == seg_before, total, 0.0)
                dkept = jnp.sum(state * dstate, axis=0, keepdims=True) * kept
                dstate_new = dstate_new + dstate * kept
        if c > 0:
            carry[h] = dstate_new
        used = LEVELS + int(c > 0)
        sums_t = sums_t_ref[:, : used * CHUNK]
        if c < chunks - 1:
            sums_t = jnp.concatenate([sums_t, sums_t_ref[:, (LEVELS + 1) * CHUNK :]], axis=1)
        dlogf = dot(sums_t, jnp.concatenate(dsums, axis=0))
        if 0 < c < chunks - 1:
            dlogf = dlogf + dkept
        ring.store(dz_ref, first, (dquery * gate0 * (1.0 + z0 * (1.0 - gate0))).astype(BF), lanes, 0)
        ring.store(dz_ref, first, ((dlogf - dkey * (1.0 - key)) * key).astype(BF), lanes, 1)
        ring.store(dz_ref, first, dvalue.astype(BF), lanes, 2)


def mixer_call(kernel, name, operands, kinds, outputs, segments, z, ranks):
    seqs, seq_len = segments.shape
    rows, width = z.shape[1:]
    heads = width // HEAD_DIM
    together = math.gcd(heads, TOGETHER)
    lanes = together * HEAD_DIM
    chunks = seq_len // CHUNK
    matrices = (seqs, heads, chunks, HEAD_DIM, HEAD_DIM)
    shapes = {
        "z": (None, pl.BlockSpec((3, rows, lanes), lambda h: (0, 0, h))),
        "z_all": (None, pl.BlockSpec((4, rows, lanes), lambda h: (0, 0, h))),
        "gain": (None, pl.BlockSpec((1, lanes), lambda h: (0, h))),
        "dz": ((4, rows, width), pl.BlockSpec((4, rows, lanes), lambda h: (0, 0, h))),
        "token": ((rows, width), pl.BlockSpec((rows, lanes), lambda h: (0, h))),
        "column": ((rows, 1), pl.BlockSpec((rows, 1), lambda h: (0, 0))),
        "matrix": (matrices, pl.BlockSpec((seqs, together) + matrices[2:], lambda h: (0, h, 0, 0, 0))),
        "segment_row": (None, pl.BlockSpec((seqs, 1, seq_len), lambda h: (0, 0, 0))),
        "segment_column": (None, pl.BlockSpec((seqs, seq_len, 1), lambda h: (0, 0, 0))),
        "sums": (None, pl.BlockSpec((LEVELS + 2, CHUNK, CHUNK), lambda h: (0, 0, 0))),
        "sums_t": (None, pl.BlockSpec((CHUNK, (LEVELS + 2) * CHUNK), lambda h: (0, 0))),
        "scalar": (None, pl.BlockSpec(memory_space=pltpu.SMEM)),
    }
    return pl.pallas_call(
        functools.partial(kernel, ranks),
        grid=(heads // together,),
        in_specs=[shapes[kind][1] for kind in kinds],
        out_specs=[shapes[kind][1] for kind, _ in outputs],
        out_shape=[jax.ShapeDtypeStruct(shapes[kind][0], dtype) for kind, dtype in outputs],
        compiler_params=pltpu.CompilerParams(vmem_limit_bytes=VMEM_LIMIT),
        name=name,
    )(*operands)


def mixer_forward(z, gain, segments, scalars, ranks):
    sums = jnp.asarray(decay_sums(), BF)
    return mixer_call(
        mixer_forward_kernel,
        "mixer_forward",
        (scalars, z, gain, segments[:, None, :], segments[:, :, None], sums),
        ("scalar", "z_all", "gain", "segment_row", "segment_column", "sums"),
        (("token", F32), ("token", BF), ("column", F32), ("matrix", F32), ("matrix", BF)),
        segments,
        z,
        ranks,
    )


def mixer_backward(z, dout, gate_dz, segments, scalars, states, pairs, ranks):
    sums = decay_sums()
    sums_t = jnp.asarray(sums.reshape(-1, CHUNK).T, BF)
    return mixer_call(
        mixer_backward_kernel,
        "mixer_backward",
        (scalars,)
        + tuple(
            in_hbm(
                z, dout, gate_dz, segments[:, None, :], segments[:, :, None], jnp.asarray(sums, BF), sums_t, states, pairs
            )
        ),
        ("scalar", "z", "token", "token", "segment_row", "segment_column", "sums", "sums_t", "matrix", "matrix"),
        (("dz", BF),),
        segments,
        z,
        ranks,
    )[0]


def in_hbm(*arrays):
    return [pltpu.with_memory_space_constraint(a, pltpu.HBM) for a in arrays]


FREE = pl.CostEstimate(flops=0, bytes_accessed=0, transcendentals=0)


EXTRA = 128
SMALL = 8


def to_columns(small):
    high = small.astype(BF).astype(F32)
    zeros = jnp.zeros((EXTRA - 2 * SMALL, small.shape[1]), F32)
    return jnp.concatenate([high, small - high, zeros], axis=0).T.astype(BF)


def from_columns(columns):
    rows = columns.astype(F32).T
    return rows[:SMALL] + rows[SMALL : 2 * SMALL]


def mixer_gradient_kernel(rows_ref, grads_ref, small_ref, *refs):
    *arrived, out_ref = refs
    rows = rows_ref[...]
    width = grads_ref.shape[2]
    for j in range(grads_ref.shape[0]):
        columns = slice(j * width, (j + 1) * width)
        total = dot_tn(rows, grads_ref[j])
        for ref in arrived:
            total = total + ref[:, columns].astype(F32)
        out_ref[:, columns] = total.astype(BF)
    last = slice(grads_ref.shape[0] * width, out_ref.shape[1])
    small = small_ref[...]
    for ref in arrived:
        small = small + from_columns(ref[:, last])
    out_ref[:, last] = to_columns(small)


def mixer_gradient(rows, span, grads, small, arrived, tile):
    tokens = rows.shape[0]
    count, _, width = grads.shape
    first, last = span
    tile = min(tile, last - first)
    whole = count * width + EXTRA
    return pl.pallas_call(
        mixer_gradient_kernel,
        grid=((last - first) // tile,),
        in_specs=[
            pl.BlockSpec((tokens, tile), lambda i: (0, first // tile + i)),
            pl.BlockSpec((count, tokens, width), lambda i: (0, 0, 0)),
            pl.BlockSpec((SMALL, tile), lambda i: (0, first // tile + i)),
        ]
        + [pl.BlockSpec((tile, whole), lambda i, at=at: (at // tile + i, 0)) for _, at in arrived],
        out_specs=pl.BlockSpec((tile, whole), lambda i: (i, 0)),
        out_shape=jax.ShapeDtypeStruct((last - first, whole), BF),
        compiler_params=pltpu.CompilerParams(vmem_limit_bytes=2 * VMEM_LIMIT),
        cost_estimate=FREE,
        name="mixer_gradient",
    )(rows, grads, small, *[a for a, _ in arrived])


def mixer_in_update_kernel(count, rows_ref, grads_ref, small_ref, *refs):
    arrived, columns = refs[:count], refs[count : 2 * count]
    (master_ref, moment_ref, average_ref, grad_out, master_out, moment_out, average_out, gain_out, small_out) = refs[
        2 * count :
    ]
    total = dot_tn(rows_ref[...], grads_ref[0])
    for ref in arrived:
        total = total + ref[...].astype(F32)
    moment = MOMENT_RATE * moment_ref[0] + total
    master = master_ref[0] - LEARN_RATE * (total + MOMENT_RATE * moment)
    grad_out[0] = total
    moment_out[0] = moment
    master_out[0] = master
    average_out[0] = AVERAGE_RATE * average_ref[0] + (1.0 - AVERAGE_RATE) * master
    product = (master_ref[0].astype(BF).astype(F32) * total).astype(BF)
    gain = dot_nt(jnp.ones((SMALL, product.shape[1]), BF), product)
    gain_out[...] = jnp.where(pl.program_id(0) == 0, gain, gain_out[...] + gain)
    small = small_ref[...]
    for ref in columns:
        small = small + from_columns(ref[...])
    small_out[...] = small


def mixer_in_update(rows, grads, small, arrived, master, moment, average):
    n = master.shape[1]
    count, tokens, width = grads.shape
    last = rows.shape[1] // n - 1
    weight = pl.BlockSpec((1, n, width), lambda k: (k, 0, 0))
    thin = pl.BlockSpec((SMALL, n), lambda k: (0, 0))
    behind = count * width // EXTRA
    return pl.pallas_call(
        functools.partial(mixer_in_update_kernel, len(arrived)),
        grid=(count,),
        in_specs=[
            pl.BlockSpec((tokens, n), lambda k: (0, last)),
            pl.BlockSpec((1, tokens, width), lambda k: (k, 0, 0)),
            pl.BlockSpec((SMALL, n), lambda k: (0, last)),
        ]
        + [pl.BlockSpec((n, width), lambda k, at=at: (at // n, k)) for _, at in arrived]
        + [pl.BlockSpec((n, EXTRA), lambda k, at=at: (at // n, behind)) for _, at in arrived]
        + [weight] * 3,
        out_specs=[weight] * 4 + [thin] * 2,
        out_shape=[jax.ShapeDtypeStruct(master.shape, F32)] * 4 + [jax.ShapeDtypeStruct((SMALL, n), F32)] * 2,
        compiler_params=pltpu.CompilerParams(vmem_limit_bytes=2 * VMEM_LIMIT),
        name="mixer_in_update",
    )(
        rows,
        grads,
        small,
        *[a for a, _ in arrived],
        *[a for a, _ in arrived],
        *in_hbm(master, moment, average),
    )


def pair_gradient_kernel(rows_ref, first_ref, second_ref, *refs):
    *arrived, out_ref = refs
    rows = rows_ref[...]
    for j, side in enumerate((first_ref, second_ref)):
        total = dot_tn(rows, side[...])
        for ref in arrived:
            total = total + ref[j].astype(F32)
        out_ref[j] = total.astype(BF)


def pair_gradient(rows, span, first_side, second_side, arrived, tile):
    tokens = rows.shape[0]
    width = first_side.shape[1]
    first, last = span
    tile = min(tile, last - first)
    side = pl.BlockSpec((tokens, width), lambda i: (0, 0))
    return pl.pallas_call(
        pair_gradient_kernel,
        grid=((last - first) // tile,),
        in_specs=[pl.BlockSpec((tokens, tile), lambda i: (0, first // tile + i)), side, side]
        + [pl.BlockSpec((2, tile, width), lambda i, at=at: (0, at // tile + i, 0)) for _, at in arrived],
        out_specs=pl.BlockSpec((2, tile, width), lambda i: (0, i, 0)),
        out_shape=jax.ShapeDtypeStruct((2, last - first, width), BF),
        compiler_params=pltpu.CompilerParams(vmem_limit_bytes=2 * VMEM_LIMIT),
        cost_estimate=FREE,
        name="pair_gradient",
    )(rows, first_side, second_side, *[a for a, _ in arrived])


def wide_gradient_kernel(left_ref, right_ref, *refs):
    *arrived, out_ref = refs
    total = dot_tn(left_ref[...], right_ref[...])
    for ref in arrived:
        total = total + ref[...].astype(F32)
    out_ref[...] = total.astype(BF)


def wide_gradient(left, right, span, arrived, tile):
    tokens, n = left.shape
    first, last = span
    tile = min(tile, last - first)
    return pl.pallas_call(
        wide_gradient_kernel,
        grid=((last - first) // tile,),
        in_specs=[
            pl.BlockSpec((tokens, n), lambda i: (0, 0)),
            pl.BlockSpec((tokens, tile), lambda i: (0, first // tile + i)),
        ]
        + [pl.BlockSpec((n, tile), lambda i, at=at: (0, at // tile + i)) for _, at in arrived],
        out_specs=pl.BlockSpec((n, tile), lambda i: (0, i)),
        out_shape=jax.ShapeDtypeStruct((n, last - first), BF),
        compiler_params=pltpu.CompilerParams(vmem_limit_bytes=VMEM_LIMIT),
        cost_estimate=FREE,
        name="wide_gradient",
    )(*in_hbm(left, right, *[a for a, _ in arrived]))


def split_column(v):
    high = v.astype(BF)
    return high, (v - high.astype(F32)).astype(BF)


def after_mixer_kernel(count, own_ref, square_ref, tokens_ref, gain_ref, *refs):
    arrived = refs[:count]
    resid_ref, scale_ref, norm_ref = refs[count:]
    mixed = own_ref[...].astype(F32)
    square = square_ref[...]
    for ref in arrived:
        mixed = mixed + ref[:, :D].astype(F32)
        square = square + ref[:, D : D + 1].astype(F32) + ref[:, D + 1 : D + 2].astype(F32)
    scale = lax.rsqrt(square / D + EPS)
    resid = tokens_ref[...].astype(F32) + mixed * scale
    resid_ref[...] = resid
    scale_ref[...] = scale
    norm_ref[...] = (resid * lax.rsqrt(mean_square(resid) + EPS) * gain_ref[...]).astype(BF)


def after_mixer(parts, square, tokens, gain, arrived):
    rows = tokens.shape[0]
    whole = pl.BlockSpec((rows, D), lambda i: (0, 0))
    column = pl.BlockSpec((rows, 1), lambda i: (0, 0))
    return pl.pallas_call(
        functools.partial(after_mixer_kernel, len(arrived)),
        grid=(1,),
        in_specs=[whole, column, whole, pl.BlockSpec((1, D), lambda i: (0, 0))]
        + [pl.BlockSpec((rows, D + EXTRA), lambda i: (0, 0))] * len(arrived),
        out_specs=[whole, column, whole],
        out_shape=[
            jax.ShapeDtypeStruct((rows, D), F32),
            jax.ShapeDtypeStruct((rows, 1), F32),
            jax.ShapeDtypeStruct((rows, D), BF),
        ],
        compiler_params=pltpu.CompilerParams(vmem_limit_bytes=VMEM_LIMIT),
        name="after_mixer",
    )(parts, square, *in_hbm(tokens), gain, *arrived)


def after_feed_kernel(count, own_ref, resid_ref, tokens_ref, final_ref, gain_ref, scale_ref, *refs):
    arrived = refs[:count]
    grad_ref, payload_ref = refs[count:]
    grad = own_ref[...].astype(F32)
    for ref in arrived:
        grad = grad + ref[...].astype(F32)
    resid = resid_ref[...]
    grad = final_ref[...] + norm_back(resid, lax.rsqrt(mean_square(resid) + EPS), grad * gain_ref[...])
    grad_ref[...] = grad
    low = grad.astype(BF)
    payload_ref[:, :D] = low
    scale = scale_ref[...]
    mixed = resid - tokens_ref[...].astype(F32)
    coef = scale * scale * jnp.mean(low.astype(F32) * mixed, axis=-1, keepdims=True)
    columns = [part for v in (scale, coef) for part in split_column(v)]
    lane = lax.broadcasted_iota(jnp.int32, (low.shape[0], EXTRA), 1)
    extra = jnp.zeros((low.shape[0], EXTRA), F32)
    for i, part in enumerate(columns):
        extra = jnp.where(lane == i, part.astype(F32), extra)
    payload_ref[:, D:] = extra.astype(BF)


def after_feed(parts, resid, tokens, final, gain, scale, arrived):
    rows = tokens.shape[0]
    whole = pl.BlockSpec((rows, D), lambda i: (0, 0))
    column = pl.BlockSpec((rows, 1), lambda i: (0, 0))
    return pl.pallas_call(
        functools.partial(after_feed_kernel, len(arrived)),
        grid=(1,),
        in_specs=[whole] * 4 + [pl.BlockSpec((1, D), lambda i: (0, 0)), column] + [whole] * len(arrived),
        out_specs=[whole, pl.BlockSpec((rows, D + EXTRA), lambda i: (0, 0))],
        out_shape=[jax.ShapeDtypeStruct((rows, D), F32), jax.ShapeDtypeStruct((rows, D + EXTRA), BF)],
        compiler_params=pltpu.CompilerParams(vmem_limit_bytes=VMEM_LIMIT),
        name="after_feed",
    )(parts, *in_hbm(resid, tokens, final), gain, scale, *arrived)


def column_sums_kernel(left_ref, right_ref, out_ref):
    product = left_ref[...].astype(F32) * right_ref[...].astype(F32)
    out_ref[...] = jnp.sum(product, axis=0, keepdims=True)


def column_sums(left, right):
    rows, width = left.shape
    tile = width // 4
    block = pl.BlockSpec((rows, tile), lambda i: (0, i))
    return pl.pallas_call(
        column_sums_kernel,
        grid=(4,),
        in_specs=[block, block],
        out_specs=pl.BlockSpec((1, tile), lambda i: (0, i)),
        out_shape=jax.ShapeDtypeStruct((1, width), F32),
        compiler_params=pltpu.CompilerParams(vmem_limit_bytes=VMEM_LIMIT),
        cost_estimate=FREE,
        name="column_sums",
    )(left, right)[0]


def project_back_kernel(grads_ref, weight_ref, out_ref):
    total = dot_nt(grads_ref[0], weight_ref[0])
    for j in range(1, grads_ref.shape[0]):
        total = total + dot_nt(grads_ref[j], weight_ref[j])
    out_ref[...] = total.astype(BF)


def project_back(grads, weight, tile):
    count, rows, width = grads.shape
    n = weight.shape[1]
    return pl.pallas_call(
        project_back_kernel,
        grid=(n // tile,),
        in_specs=[
            pl.BlockSpec((count, rows, width), lambda i: (0, 0, 0)),
            pl.BlockSpec((count, tile, width), lambda i: (0, i, 0)),
        ],
        out_specs=pl.BlockSpec((rows, tile), lambda i: (0, i)),
        out_shape=jax.ShapeDtypeStruct((rows, n), BF),
        compiler_params=pltpu.CompilerParams(vmem_limit_bytes=VMEM_LIMIT),
        cost_estimate=pl.CostEstimate(flops=0, bytes_accessed=100_000_000, transcendentals=0),
        name="project_back",
    )(grads, *in_hbm(weight))


def take_blocks_kernel(order_ref, in_ref, out_ref):
    out_ref[...] = in_ref[...]


def take_blocks(v, order):
    rows, width = v.shape[0], D
    count = order.shape[0]
    block = (rows, width // count)
    return pl.pallas_call(
        take_blocks_kernel,
        grid_spec=pltpu.PrefetchScalarGridSpec(
            num_scalar_prefetch=1,
            grid=(count,),
            in_specs=[pl.BlockSpec(block, lambda i, order: (0, order[i]))],
            out_specs=pl.BlockSpec(block, lambda i, order: (0, i)),
        ),
        out_shape=jax.ShapeDtypeStruct((rows, width), v.dtype),
        compiler_params=pltpu.CompilerParams(vmem_limit_bytes=VMEM_LIMIT),
        cost_estimate=FREE,
        name="take_blocks",
    )(order, v)


def mixer_out_update_kernel(count, act_ref, rows_ref, *refs):
    arrived = refs[:count]
    master_ref, moment_ref, average_ref, grad_out, master_out, moment_out, average_out = refs[count:]
    total = arrived[0][...].astype(F32)
    for ref in arrived[1:]:
        total = total + ref[...].astype(F32)
    total = dot_tn(act_ref[...], rows_ref[...]) + total.T
    moment = MOMENT_RATE * moment_ref[...] + total
    master = master_ref[...] - LEARN_RATE * (total + MOMENT_RATE * moment)
    grad_out[...] = total
    moment_out[...] = moment
    master_out[...] = master
    average_out[...] = AVERAGE_RATE * average_ref[...] + (1.0 - AVERAGE_RATE) * master


def mixer_out_update(act, rows, arrived, master, moment, average):
    n = master.shape[1]
    tokens, width = act.shape
    last = rows.shape[1] // n - 1
    whole = pl.BlockSpec((width, n), lambda i: (0, 0))
    return pl.pallas_call(
        functools.partial(mixer_out_update_kernel, len(arrived)),
        grid=(1,),
        in_specs=[pl.BlockSpec((tokens, width), lambda i: (0, 0)), pl.BlockSpec((tokens, n), lambda i: (0, last))]
        + [pl.BlockSpec((n, width), lambda i, at=at: (at // n, 0)) for _, at in arrived]
        + [whole] * 3,
        out_specs=[whole] * 4,
        out_shape=[jax.ShapeDtypeStruct(master.shape, F32)] * 4,
        compiler_params=pltpu.CompilerParams(vmem_limit_bytes=VMEM_LIMIT),
        name="mixer_out_update",
    )(act, rows, *[a for a, _ in arrived], *in_hbm(master, moment, average))


def turn(v, axis, step):
    n = lax.axis_size(axis)
    return lax.ppermute(v, axis, [(i, (i + step) % n) for i in range(n)])


def swap(v, axis, bit):
    n = lax.axis_size(axis)
    return lax.ppermute(v, axis, [(i, i ^ bit) for i in range(n)])


def gather_near(v, axis):
    n = lax.axis_size(axis)
    return jnp.concatenate([v] + [turn(v, axis, k) for k in range(1, n)], axis=0)


def scatter_near(v, axis):
    n = lax.axis_size(axis)
    rows = v.shape[0] // n
    total = v[:rows].astype(F32)
    for k in range(1, n):
        total = total + turn(v[k * rows : (k + 1) * rows], axis, -k).astype(F32)
    return total


def gather_gains(v):
    bit = 1
    me = lax.axis_index("dp")
    while bit < lax.axis_size("dp"):
        other = swap(v, "dp", bit)
        upper = (me & bit) > 0
        v = jnp.concatenate([jnp.where(upper, other, v), jnp.where(upper, v, other)], axis=1)
        bit *= 2
    return v


def apply_update(master, moment, average, gradient):
    moment_new = MOMENT_RATE * moment + gradient
    master_new = master - LEARN_RATE * (gradient + MOMENT_RATE * moment_new)
    average_new = AVERAGE_RATE * average + (1.0 - AVERAGE_RATE) * master_new
    return (gradient, master_new, moment_new, average_new)


def gather_weight(w, dim):
    return lax.all_gather(w.astype(BF), "dp", axis=dim, tiled=True)


def link_bits():
    bits = []
    bit = 2
    while bit < lax.axis_size("dp"):
        bits.append(bit)
        bit *= 2
    return bits, bits[::-1]


def block_order(bits):
    if not bits:
        return [0]
    rest = block_order(bits[1:])
    return [bits[0] ^ r for r in rest] + rest


def exchange_order(me):
    even, odd = (block_order(bits) for bits in link_bits())
    order_even = [1 ^ r for r in odd] + even
    order_odd = [1 ^ r for r in even] + odd
    return me ^ jnp.where((me & 1) == 0, jnp.array(order_even, jnp.int32), jnp.array(order_odd, jnp.int32))


def cross_swap(v, stage):
    even, odd = link_bits()
    n = lax.axis_size("dp")
    return lax.ppermute(v, "dp", [(i, i ^ (odd if i & 1 else even)[stage]) for i in range(n)])


def after(v, *others):
    return lax.optimization_barrier((v,) + others)[0]


class GradientSum:
    def __init__(self, piece):
        self.piece = piece
        self.at = 0
        self.left = D
        self.received = []

    def arrived(self):
        return [(r, self.at - first) for r, first in self.received]

    def send(self):
        self.left //= 2
        give = self.piece(self.at, self.at + self.left, self.arrived())
        stage = len(self.received) - 1
        self.at += self.left
        self.received.append((swap(give, "dp", 1) if stage < 0 else cross_swap(give, stage), self.at))
        return give

    def send_rest(self):
        while self.left > D // lax.axis_size("dp"):
            give = self.send()
        return give

    def last(self):
        return self.at, D, self.arrived()


def two_parts(v):
    high = lax.reduce_precision(v, 8, 7)
    return [high.astype(BF), (v - high).astype(BF)]


def pack_columns(values):
    parts = jnp.stack([part for v in values for part in two_parts(v)], axis=1)
    return jnp.pad(parts, ((0, 0), (0, EXTRA - parts.shape[1])))


def unpack_columns(v, count):
    return [v[:, 2 * i].astype(F32) + v[:, 2 * i + 1].astype(F32) for i in range(count)]


def gather_block_weight(w, dim):
    me = lax.axis_index("dp")
    core = me & 1
    even, odd = (block_order(bits) for bits in link_bits())
    order_even = [1 ^ r for r in odd] + even
    order_odd = [1 ^ r for r in even] + odd
    v = w.astype(BF)
    width = v.shape[dim]
    for stage in reversed(range(len(link_bits()[0]))):
        v = jnp.concatenate([cross_swap(v, stage), v], axis=dim)
    parts = [swap(v, "dp", 1), v]
    shape = list(v.shape)
    shape[dim] *= 2
    whole = jnp.zeros(shape, BF)
    for i, (a, b) in enumerate(zip(order_even, order_odd)):
        part = parts[i * 2 // len(order_even)]
        at = i % (len(order_even) // 2) * width
        block = lax.slice_in_dim(part, at, at + width, axis=dim)
        whole = lax.dynamic_update_slice_in_dim(whole, block, (me ^ jnp.where(core == 0, a, b)) * width, dim)
    return whole


def per_device(
    tokens,
    teacher,
    segments,
    block_counts,
    loss_mask,
    mixer_in,
    mixer_in_moment,
    mixer_in_average,
    mixer_out,
    mixer_out_moment,
    mixer_out_average,
    feed_in,
    feed_in_moment,
    feed_in_average,
    feed_out,
    feed_out_moment,
    feed_out_average,
    norm_gains,
    norm_gains_moment,
    norm_gains_average,
):
    mixer_in_work = gather_weight(mixer_in, 1)
    mixer_out_work = gather_block_weight(mixer_out, 1)
    feed_in_work = gather_weight(feed_in, 1)
    feed_out_work = gather_weight(feed_out, 1)
    gains = gather_gains(norm_gains.astype(BF)).astype(F32)

    row_total = tokens.shape[0]
    seq_here, seq_len = segments.shape
    seq_all = block_counts.shape[0]
    data_rank = lax.axis_index("dp")
    model_rank = lax.axis_index("mp")
    model_size = lax.axis_size("mp")
    local_counts = lax.dynamic_slice_in_dim(block_counts, data_rank * seq_here, seq_here, 0)
    order = exchange_order(data_rank.astype(jnp.int32))
    scalars = jnp.concatenate([local_counts, model_rank[None].astype(jnp.int32)])
    column = jnp.arange(seq_len, dtype=jnp.int32)
    live_all = (column[None, :] < BLOCK * block_counts[:, None]).astype(F32)
    total_count = jnp.sum(loss_mask.reshape(seq_all, seq_len).astype(F32) * live_all)
    first_row = (data_rank * model_size + model_rank) * row_total
    valid = lax.dynamic_slice_in_dim(loss_mask.astype(F32) * live_all.reshape(-1), first_row, row_total, 0)

    inputs = tokens.astype(F32)
    inputs_scale = lax.rsqrt(mean_square(inputs) + EPS)
    tokens_full = gather_near(tokens, "mp").astype(F32)
    first_full = (tokens_full * lax.rsqrt(mean_square(tokens_full) + EPS) * gains[0]).astype(BF)
    z = jnp.einsum("td,jde->jte", first_full, mixer_in_work, preferred_element_type=F32)
    gate_z = z[3]
    local_width = z.shape[2]
    gain_out = lax.dynamic_slice_in_dim(gains[2], model_rank * local_width, local_width, 0)[None]
    recurrent, act_raw, square, states, pairs = mixer_forward(z, gain_out, segments, scalars, model_size)
    gate_z_sig = jax.nn.sigmoid(gate_z)
    gate_z_act = gate_z * gate_z_sig
    mixed_parts = dot(act_raw, mixer_out_work).astype(BF)
    arrived = []
    for k in range(1, model_size):
        rows = slice(k * row_total, (k + 1) * row_total)
        payload = jnp.concatenate([mixed_parts[rows], pack_columns([square[rows, 0]])], axis=1)
        arrived.append(turn(payload, "mp", -k))
    first_blocks = take_blocks(first_full, order)
    *arrived, first_blocks = lax.optimization_barrier((*arrived, first_blocks))
    resid, out_scale_here, norm_second = after_mixer(mixed_parts, square, tokens, gains[1:2], arrived)

    second_full = gather_near(norm_second, "mp")
    gate_up = jnp.einsum("td,jdf->jtf", second_full, feed_in_work, preferred_element_type=F32)
    gate_sig = jax.nn.sigmoid(gate_up[0])
    gate_act = gate_up[0] * gate_sig
    hidden_low = (gate_act * gate_up[1]).astype(BF)
    final = resid + scatter_near(dot(hidden_low, feed_out_work).astype(BF), "mp")
    output = final.astype(BF)

    error = (final - teacher.astype(F32)) * valid[:, None]
    square_sum = jnp.sum(error * error)
    token_slots = row_total * lax.axis_size("dp") * model_size
    grad_final = token_slots / total_count * error

    grad_full = gather_near(grad_final.astype(BF), "mp")
    grad_hidden = dot_nt(grad_full, feed_out_work)
    grad_gate = (grad_hidden * gate_up[1] * gate_sig * (1.0 + gate_up[0] * (1.0 - gate_sig))).astype(BF)
    grad_up = (grad_hidden * gate_act).astype(BF)
    grad_second_parts = (dot_nt(grad_gate, feed_in_work[0]) + dot_nt(grad_up, feed_in_work[1])).astype(BF)
    parts = [grad_second_parts[k * row_total : (k + 1) * row_total] for k in range(1, model_size)]
    *parts, grad_late = lax.optimization_barrier((*parts, grad_full))
    arrived = [turn(part, "mp", -k) for k, part in enumerate(parts, 1)]
    grad_blocks = take_blocks(grad_late, order)
    feed_out_sum = GradientSum(
        lambda a, b, arrived: wide_gradient(hidden_low, grad_blocks, (a, b), arrived, 512)
    )
    sent = feed_out_sum.send()
    feed_in_grad = pair_gradient(second_full, (0, D), grad_gate, after(grad_up, sent), [], 256)
    gain_two_grad = column_sums(grad_second_parts, after(second_full, feed_in_grad)) / gains[1]
    sent = feed_out_sum.send()
    *arrived, feed_in_grad, gain_two_grad, _ = lax.optimization_barrier((*arrived, feed_in_grad, gain_two_grad, sent))
    grad_resid, payload = after_feed(
        grad_second_parts, resid, tokens, grad_final, gains[1:2], out_scale_here, arrived
    )

    pieces = [payload] + [turn(payload, "mp", k) for k in range(1, model_size)]
    *pieces, _ = lax.optimization_barrier((*pieces, feed_out_sum.send_rest()))
    payload = jnp.concatenate(pieces, axis=0)
    resid_full = payload[:, :D]
    out_scale, coef = (v[:, None] for v in unpack_columns(payload[:, D:], 2))
    grad_act = dot_nt(resid_full, mixer_out_work)
    act_low = (act_raw.astype(F32) * out_scale).astype(BF)
    normed = recurrent * out_scale
    gate_dz = (grad_act * normed * gain_out * gate_z_sig * (1.0 + gate_z * (1.0 - gate_z_sig))).astype(BF)
    grad_normed = grad_act * gate_z_act
    gain_out_grad = jnp.sum(grad_normed * normed, axis=0)
    grad_recurrent = out_scale * (grad_normed * gain_out) - recurrent * coef

    gain_out_full = lax.dynamic_update_slice_in_dim(
        jnp.zeros((D,), F32), gain_out_grad, model_rank * local_width, 0
    )
    zero = jnp.zeros((D,), F32)
    small = jnp.stack([gain_two_grad, gain_out_full, jnp.full((D,), square_sum)] + [zero] * (SMALL - 3))
    small = take_blocks(small, order)
    dz = mixer_backward(z, grad_recurrent, gate_dz, segments, scalars, states, pairs, model_size)

    in_sum = GradientSum(None)

    def in_piece(dz_then):
        return lambda a, b, arrived: mixer_gradient(first_blocks, (a, b), dz_then, small, arrived, 256)

    in_sum.piece = in_piece(dz)
    sent = in_sum.send()
    grad_first_parts = project_back(after(dz, sent), mixer_in_work, 512)
    in_sum.piece = in_piece(after(dz, grad_first_parts))
    sent = in_sum.send()
    ranked = jnp.concatenate(
        [
            lax.dynamic_slice_in_dim(grad_first_parts, (model_rank - r) % model_size * row_total, row_total, 0)
            for r in range(model_size)
        ]
    )
    ranked, dz_then, grad_blocks, _ = lax.optimization_barrier((ranked, dz, grad_blocks, sent))
    grad_first = lax.all_to_all(ranked, "mp", 0, 0, tiled=True).reshape(model_size, row_total, D)

    sent = mixer_out_grad = dot_tn(after(act_low, ranked), resid_full).astype(BF)
    at, _, feed_arrived = feed_out_sum.last()
    feed_out_share = wide_gradient(hidden_low, grad_blocks, (at, D), feed_arrived, 512)
    fourth = apply_update(feed_out, feed_out_moment, feed_out_average, feed_out_share.astype(F32))

    in_sum.piece = in_piece(after(dz_then, fourth[3], sent))
    sent = in_sum.send_rest()
    feed_in_share = lax.psum_scatter(feed_in_grad, "dp", scatter_dimension=1, tiled=True)
    feed_in_share = after(feed_in_share, sent)
    third = apply_update(feed_in, feed_in_moment, feed_in_average, feed_in_share.astype(F32))
    *first, gain_one, small = mixer_in_update(
        first_blocks, after(dz, third[3]), small, in_sum.last()[2], mixer_in, mixer_in_moment, mixer_in_average
    )
    sums = jnp.concatenate([gain_one[:1], small[:3]])
    mixer_out_share = lax.psum_scatter(mixer_out_grad, "dp", scatter_dimension=1, tiled=True)
    mixer_out_share = after(mixer_out_share, sums)
    second = apply_update(mixer_out, mixer_out_moment, mixer_out_average, mixer_out_share.astype(F32))
    grad_first = jnp.sum(after(grad_first, sums).astype(F32), axis=0)
    tokens_grad = (grad_resid + norm_back(inputs, inputs_scale, grad_first * gains[0])).astype(BF)
    sums = sums + sum(turn(sums, "mp", k) for k in range(1, model_size))
    sums = after(sums, second[3])
    gains_share = jnp.concatenate([sums[:1] / norm_gains[:1].astype(BF).astype(F32), sums[1:3]])
    loss_value = sums[3, 0] / (total_count * D)
    fifth = apply_update(norm_gains, norm_gains_moment, norm_gains_average, gains_share)
    return (output, tokens_grad, loss_value) + tuple(first) + second + third + fourth + fifth


def solution(mesh):
    tokens = P(("dp", "mp"), None)
    stacked = P(None, "dp", "mp")
    flat = P("mp", "dp")
    gains = P(None, "dp")
    return jax.shard_map(
        per_device,
        mesh=mesh,
        in_specs=(tokens, tokens, P("dp", None), P(), P())
        + (stacked,) * 3 + (flat,) * 3 + (stacked,) * 3 + (flat,) * 3 + (gains,) * 3,
        out_specs=(tokens, tokens, P()) + (stacked,) * 4 + (flat,) * 4 + (stacked,) * 4 + (flat,) * 4 + (gains,) * 4,
        check_vma=False,
    )
```
